512 devices in a mesh: wide: 64 (over x, y, core), narrow: 8 (over z).
Axes of the slice: x: 4, y: 8, z: 8, core: 2. Of those that a mesh axis runs over, the one named last changes fastest.
Arguments:
- source: float32 [512, 32, 1024], P('wide', None, 'narrow'), may hold values from -60 to 60
- permeability: float32 [512, 32, 1024], P('wide', None, 'narrow'), may hold values from 0.1 to 10
- leakage: float32 [512, 32, 1024], P('wide', None, 'narrow'), may hold values from 0.02 to 0.5
Outputs:
- pressure: float32 [512, 32, 1024], P('wide', None, 'narrow')
The draws below stay inside these ranges and needn't reach their ends.
All inputs are finite; a program needn't handle non-finite values.
Results may differ from the reference program's by a relative error of at most 0.000068.
Values sent between devices are 32-bit elements; how exact they have to be, the bound alone decides.
A program may use at most 64 MiB of HBM per device.

```python
import math
import jax
import jax.numpy as jnp

CY = 32
LEVELS = 4
NX = 512
NZ = 1024


def levels(rng, extent, split, least, high):
    factor_of, own = 1.0, jax.random.fold_in(rng, 6)
    for dim, blocks in split:
        draws = jnp.exp(jax.random.uniform(jax.random.fold_in(own, dim), (blocks,), jnp.float32, least / len(split), high / len(split)))
        factor_of = factor_of * jnp.repeat(draws, extent[dim] // blocks).reshape([-1 if axis == dim else 1 for axis in range(len(extent))])
    return factor_of


def gaussian(own_key, extent, deviation, limit, split=(), kind=jnp.bfloat16):
    level = levels(own_key, extent, split, -0.22, 0.18) if split else 1.0
    array = jax.random.normal(own_key, extent, jnp.float32) * deviation * level
    return jnp.minimum(jnp.maximum(array, -limit), limit).astype(kind)


def setup_inputs(seed: int = 0) -> dict:
    splits = jax.random.split(jax.random.key(seed), 4)
    source = gaussian(splits[0], (NX, CY, NZ), 10.0, 60.0, ((0, 64), (2, 8)), jnp.float32)
    permeability = jnp.clip(jnp.exp(math.log(10.0) - 4.6051702 * jax.random.uniform(splits[1], (NX, CY, NZ), jnp.float32) ** levels(splits[1], (NX, CY, NZ), ((0, 64), (2, 8)), -0.2, 0.2)), 0.1, 10.0)
    leakage = jnp.clip(jnp.exp(math.log(0.5) - 3.218876 * jax.random.uniform(splits[2], (NX, CY, NZ), jnp.float32) ** levels(splits[2], (NX, CY, NZ), ((0, 64), (2, 8)), -0.2, 0.2)), 0.02, 0.5)
    return {"source": source, "permeability": permeability, "leakage": leakage}


OMEGA = 0.8


def offsets():
    table = []
    for a in (-1, 0, 1):
        for b in (-1, 0, 1):
            for c in (-1, 0, 1):
                count = abs(a) + abs(b) + abs(c)
                if count == 0:
                    continue
                base = (abs(a) * 1.0 + abs(b) * 0.7 + abs(c) * 0.4) / count
                factor = {1: 1.0, 2: 0.25, 3: 0.1}[count]
                table.append((a, b, c, base * factor))
    return table


def window(padded, a, b, c, shape):
    return padded[1 + a:1 + a + shape[0], 1 + b:1 + b + shape[1], 1 + c:1 + c + shape[2]]


def diagonal(perm_pad, leak, scale):
    shape = leak.shape
    center = window(perm_pad, 0, 0, 0, shape)
    total = leak
    for a, b, c, weight in offsets():
        total = total + (weight * scale * 0.5) * (center + window(perm_pad, a, b, c, shape))
    return total


def apply_op(field_pad, perm_pad, leak, scale):
    shape = leak.shape
    center = window(perm_pad, 0, 0, 0, shape)
    field = window(field_pad, 0, 0, 0, shape)
    total = leak * field
    for a, b, c, weight in offsets():
        couple = (weight * scale * 0.5) * (center + window(perm_pad, a, b, c, shape))
        total = total + couple * (field - window(field_pad, a, b, c, shape))
    return total


def mean_eight(v):
    nx, ny, nz = v.shape
    return v.reshape(nx // 2, 2, ny // 2, 2, nz // 2, 2).sum(axis=(1, 3, 5)) * 0.125


def expand(v):
    return jnp.repeat(jnp.repeat(jnp.repeat(v, 2, axis=0), 2, axis=1), 2, axis=2)


def cycle(rhs, perm, leak, level):
    scale = 0.25 ** level
    perm_pad = jnp.pad(perm, 1)
    diag = diagonal(perm_pad, leak, scale)
    value = OMEGA * rhs / diag
    value = value + OMEGA * (rhs - apply_op(jnp.pad(value, 1), perm_pad, leak, scale)) / diag
    if level < LEVELS - 1:
        resid = rhs - apply_op(jnp.pad(value, 1), perm_pad, leak, scale)
        coarse = cycle(mean_eight(resid), mean_eight(perm), mean_eight(leak), level + 1)
        value = value + expand(coarse)
        for sweep in range(2):
            value = value + OMEGA * (rhs - apply_op(jnp.pad(value, 1), perm_pad, leak, scale)) / diag
    return value


def reference(source, permeability, leakage):
    return cycle(source, permeability, leakage, 0)
```

```python
import jax
import jax.numpy as jnp
from jax import lax
from jax.experimental import pallas as pl
from jax.experimental.pallas import tpu as pltpu
from jax.sharding import PartitionSpec as P

MESH = pl.DeviceIdType.MESH
OMEGA = 0.8
F32 = jnp.float32


def weight(a, b, c):
    n = a + b + c
    return (a * 1.0 + b * 0.7 + c * 0.4) / n * {1: 1.0, 2: 0.25, 3: 0.1}[n]


CX, CY, CZ = weight(1, 0, 0), weight(0, 1, 0), weight(0, 0, 1)
CXY, CXZ, CYZ, CXYZ = weight(1, 1, 0), weight(1, 0, 1), weight(0, 1, 1), weight(1, 1, 1)
CALL = 2 * (CX + CY + CZ) + 4 * (CXY + CXZ + CYZ) + 8 * CXYZ

SIDES = [(a, b) for b in (-1, 1) for a in (-1, 0, 1)]
FAR = [(a, b) for a in range(-4, 5) for b in (-1, 0, 1) if (a, b) != (0, 0)]


def iota(shape, dim):
    return lax.broadcasted_iota(jnp.int32, shape, dim)


def lanes():
    return iota((8, 128), 1)


def rot(x, shift, axis):
    shift %= x.shape[axis]
    return x if shift == 0 else pltpu.roll(x, shift, axis)


def ysum(t):
    axis = t.ndim - 2
    n = t.shape[axis]
    row = iota(t.shape, axis)
    up = jnp.where(row == 0, 0.0, rot(t, 1, axis))
    down = jnp.where(row == n - 1, 0.0, rot(t, n - 1, axis))
    return up + down


def planes_of(u, pz):
    g = CX * u + CXZ * pz + ysum(CXY * u + CXYZ * pz)
    h = CZ * pz + ysum(CY * u + CYZ * pz)
    return g, h


def zsum_pair(m, s):
    lane = iota(m.shape, 1)
    first, last = lane == 0, lane == 127
    rm, rs, lm, ls = rot(m, 1, 1), rot(s, 1, 1), rot(m, 127, 1), rot(s, 127, 1)
    pm = jnp.where(first, rs, rm) + jnp.where(last, ls, lm)
    ps = jnp.where(first, rm, rs) + jnp.where(last, lm, ls)
    return pm, ps


def zsum_main(m, s):
    lane = iota(m.shape, 1)
    return jnp.where(lane == 0, rot(s, 1, 1), rot(m, 1, 1)) + jnp.where(lane == 127, rot(s, 127, 1), rot(m, 127, 1))


def ring_sum(u):
    pz = rot(u, 1, 2) + rot(u, 127, 2)
    g, h = planes_of(u, pz)
    return g[:-2] + g[2:] + h[1:-1]


def ring_apply(v, k, diag, half):
    return diag * v[1:-1] - half * (k[1:-1] * ring_sum(v) + ring_sum(k * v))


def dot(a, b):
    return lax.dot_general(a, b, (((1,), (0,)), ((), ())), precision=lax.Precision.HIGHEST, preferred_element_type=F32)


def ring_map(fine_of, coarse_cut, transpose=False):
    f_dim = 1 if transpose else 0
    i, j = iota((128, 128), f_dim), iota((128, 128), 1 - f_dim)
    return ((fine_of(i) >> 1) == jnp.where(j < coarse_cut, j, j - 128)).astype(F32)


def cut(c):
    return lambda i: jnp.where(i < c, i, i - 128)


def main_z(i):
    return i


def side_z(i):
    return jnp.where(i < 64, 128 + i, i - 128)


def halve_rows(ref, n):
    return ref[pl.ds(0, n, stride=2), :] + ref[pl.ds(1, n, stride=2), :]


def double_rows(ref, x):
    n = x.shape[0]
    ref[pl.ds(0, n, stride=2), :] = x
    ref[pl.ds(1, n, stride=2), :] = x


def kernel(
    nw, nz, f_hbm, k_hbm, l_hbm, out_ref,
    km, ks, fm, fs, lm, ls, dgm, dgs, dm, ds_, v1m, v1s, v2m, v2s,
    g1m, g1s, h1m, h1s, g2m, g2s, h2m, h2s, tm, ts,
    pack0, rs0, packv, rsv, kd1, kd1x, gg1, gg1x, pack1, rs1, pv1, rsv1, vv1, vv1x,
    k1l, k1, dg1, f1, va1, t1, p2c, p2s, r2c, r2s, k2, dg2, f2, l2, t2, t3, loc_sem, send_sem, recv_sem,
):
    w, z = lax.axis_index("wide"), lax.axis_index("narrow")

    def device(a, b):
        return (lax.rem(w + (a + nw), nw), lax.rem(z + (b + nz), nz))

    has_left, has_right = (z > 0).astype(jnp.int32), (z < nz - 1).astype(jnp.int32)

    def inside(step):
        return jnp.logical_and(w + step >= 0, w + step < nw).astype(jnp.int32)

    started = []
    count = [0]

    def send(src, dst, a, b):
        n = count[0]
        count[0] += 1
        copy = pltpu.make_async_remote_copy(
            src_ref=src, dst_ref=dst, send_sem=send_sem.at[n], recv_sem=recv_sem.at[n],
            device_id=device(a, b), device_id_type=MESH,
        )
        copy.start()
        started.append(copy)
        return copy

    barrier = pltpu.get_barrier_semaphore()
    for a, b in FAR:
        pl.semaphore_signal(barrier, inc=1, device_id=device(a, b), device_id_type=MESH)
    loads = []
    for n, (src, dst) in enumerate(((k_hbm, km.at[4:12]), (f_hbm, fm.at[2:10]), (l_hbm, lm.at[2:10]))):
        loads.append(pltpu.make_async_copy(src, dst, loc_sem.at[n]))
        loads[-1].start()

    lane = lanes()

    def pack_sides(ref, off):
        left, right = jnp.zeros((8, 128), F32), jnp.zeros((8, 128), F32)
        for x in range(8):
            for t in range(4):
                j = 4 * x + t
                r = rot(ref[x + off, 8 * t : 8 * t + 8, :], 4 * j, 1)
                left = jnp.where((lane >> 2) == j, r, left)
                right = jnp.where((lane >> 2) == (j - 1) % 32, r, right)
        return left, right

    def unpack_sides(rs, n, ref, depth, masked):
        for p in range(8 + 2 * depth):
            x = p - depth
            step = (x + 8) // 8
            for t in range(4):
                j = 4 * (x % 8) + t
                from_right = rot(rs[step, 0, n], -4 * j, 1)
                from_left = rot(rs[step, 1, n], -4 * j, 1)
                tile = jnp.where(lane < 64, from_right, from_left)
                if masked:
                    there = inside(step - 1)
                    keep = jnp.logical_or(lane < 4 * has_right * there, lane >= 128 - 4 * has_left * there)
                    tile = jnp.where(keep, tile, 0.0)
                ref[p, 8 * t : 8 * t + 8, :] = tile

    for n, (ref, off) in enumerate(((km, 4), (fm, 2), (lm, 2))):
        loads[n].wait()
        pack0[0, n], pack0[1, n] = pack_sides(ref, off)

    pl.semaphore_wait(barrier, len(FAR))

    def send_planes(src_lo, dst_hi, src_hi, dst_lo):
        return [send(src_hi, dst_lo, 1, 0), send(src_lo, dst_hi, -1, 0)]

    def send_sides(pack, rs):
        return [send(pack.at[0 if b < 0 else 1], rs.at[1 - a, 0 if b < 0 else 1], a, b) for a, b in SIDES]

    e0k = send_planes(km.at[4:8], km.at[12:16], km.at[8:12], km.at[0:4])
    e0s = send_sides(pack0, rs0)
    e0f = send_planes(fm.at[2:4], fm.at[10:12], fm.at[8:10], fm.at[0:2])
    e0l = send_planes(lm.at[2:4], lm.at[10:12], lm.at[8:10], lm.at[0:2])

    rm01, rs01 = ring_map(main_z, 96), ring_map(side_z, 96)
    r12, r23 = ring_map(cut(96), 64), ring_map(cut(64), 64)

    for c in e0k + e0s:
        c.wait_recv()
    low, high = inside(-1).astype(F32), inside(1).astype(F32)
    km[0:4] = km[0:4] * low
    km[12:16] = km[12:16] * high
    unpack_sides(rs0, 0, ks, 4, True)

    def k_parts(p, c):
        m, s = km[p], ks[p]
        pm, ps = zsum_pair(m, s)
        g1m[p], h1m[p] = planes_of(m, pm)
        g1s[p], h1s[p] = planes_of(s, ps)
        return c

    lax.fori_loop(1, 15, k_parts, 0)

    def k_pairs(i, c):
        tm[pl.ds(pl.multiple_of(32 * i, 32), 32), :] = km[2 * i] + km[2 * i + 1]
        ts[pl.ds(pl.multiple_of(32 * i, 32), 32), :] = ks[2 * i] + ks[2 * i + 1]
        return c

    lax.fori_loop(0, 8, k_pairs, 0)
    coarse = dot(halve_rows(tm, 128), rm01) + dot(halve_rows(ts, 128), rs01)
    k1l[...] = (0.125 * coarse).reshape(8, 16, 128)

    def l_pairs(i, c):
        tm[pl.ds(pl.multiple_of(32 * i, 32), 32), :] = lm[2 * i + 2] + lm[2 * i + 3]
        return c

    lax.fori_loop(0, 4, l_pairs, 0)
    l1 = (0.125 * dot(halve_rows(tm, 64), rm01)).reshape(4, 16, 128)
    own1 = k1l[2:6]
    half1 = 0.5 * 0.25
    diag1 = l1 + half1 * (CALL * own1 + ring_sum(k1l[1:7]))
    lane16 = iota((4, 16, 128), 2)
    kd1[...] = jnp.where(lane16 < 64, own1, rot(diag1, 64, 2))
    ekd = send_planes(kd1.at[0:3], kd1x.at[1], kd1.at[1:4], kd1x.at[0])

    kk = k1l[...]
    for i in range(4):
        t1[16 * i : 16 * i + 16, :] = kk[2 * i] + kk[2 * i + 1]
    k2l = (0.125 * dot(halve_rows(t1, 32), r12)).reshape(4, 8, 128)
    for i in range(2):
        t1[16 * i : 16 * i + 16, :] = l1[2 * i] + l1[2 * i + 1]
    l2own = (0.125 * dot(halve_rows(t1, 16), r12)).reshape(2, 8, 128)
    half2 = 0.5 * 0.0625
    diag2 = l2own + half2 * (CALL * k2l[1:3] + ring_sum(k2l))
    lane8 = iota((2, 8, 128), 2)
    p2c[...] = jnp.where(
        lane8 < 64, rot(l2own, 32, 2), jnp.where(lane8 < 96, rot(k2l[1:3], 64, 2), rot(diag2, 96, 2))
    )

    for c in e0f + e0l:
        c.wait_recv()
    unpack_sides(rs0, 1, fs, 2, False)
    unpack_sides(rs0, 2, ls, 2, False)

    def there0(q):
        return jnp.where(q < 2, inside(-1), jnp.where(q >= 10, inside(1), 1))

    lane32 = iota((32, 128), 1)

    def first(q, c):
        there = there0(q)
        total = g1m[q + 1] + g1m[q + 3] + h1m[q + 2]
        diag = lm[q] + 0.5 * (CALL * km[q + 2] + total)
        inv = jnp.where(lane32 < 128 * there, OMEGA / diag, 0.0)
        dgm[q], dm[q] = diag, inv
        v1m[q] = inv * fm[q]
        total = g1s[q + 1] + g1s[q + 3] + h1s[q + 2]
        diag = ls[q] + 0.5 * (CALL * ks[q + 2] + total)
        keep = jnp.logical_or(lane32 < 4 * has_right * there, lane32 >= 128 - 4 * has_left * there)
        inv = jnp.where(keep, OMEGA / diag, 0.0)
        dgs[q], ds_[q] = diag, inv
        v1s[q] = inv * fs[q]
        return c

    lax.fori_loop(0, 12, first, 0)

    def parts(vm, vs):
        def body(q, c):
            m, s = vm[q], vs[q]
            pm, ps = zsum_pair(m, s)
            g1m[q], h1m[q] = planes_of(m, pm)
            g1s[q], h1s[q] = planes_of(s, ps)
            m, s = m * km[q + 2], s * ks[q + 2]
            pm, ps = zsum_pair(m, s)
            g2m[q], h2m[q] = planes_of(m, pm)
            g2s[q], h2s[q] = planes_of(s, ps)
            return c

        return body

    def parts_main(vm, vs):
        def body(q, c):
            m, s = vm[q], vs[q]
            g1m[q], h1m[q] = planes_of(m, zsum_main(m, s))
            m, s = m * km[q + 2], s * ks[q + 2]
            g2m[q], h2m[q] = planes_of(m, zsum_main(m, s))
            return c

        return body

    def resid(q, vm, f, dg, k, g1, h1, g2, h2):
        s1 = g1[q - 1] + g1[q + 1] + h1[q]
        s2 = g2[q - 1] + g2[q + 1] + h2[q]
        return f[q] - dg[q] * vm[q] + 0.5 * (k[q + 2] * s1 + s2)

    def sweep(vm, vs, om, os):
        def body(q, c):
            om[q] = vm[q] + dm[q] * resid(q, vm, fm, dgm, km, g1m, h1m, g2m, h2m)
            os[q] = vs[q] + ds_[q] * resid(q, vs, fs, dgs, ks, g1s, h1s, g2s, h2s)
            return c

        return body

    lax.fori_loop(0, 12, parts(v1m, v1s), 0)
    lax.fori_loop(1, 11, sweep(v1m, v1s, v2m, v2s), 0)
    lax.fori_loop(1, 11, parts_main(v2m, v2s), 0)

    def resid_pairs(i, c):
        r = [resid(2 * i + 2 + n, v2m, fm, dgm, km, g1m, h1m, g2m, h2m) for n in (0, 1)]
        tm[pl.ds(pl.multiple_of(32 * i, 32), 32), :] = r[0] + r[1]
        return c

    lax.fori_loop(0, 4, resid_pairs, 0)
    gg1[...] = (0.125 * dot(halve_rows(tm, 64), rm01)).reshape(4, 16, 128)

    def pack_sides1(arrays):
        left, right = jnp.zeros((8, 128), F32), jnp.zeros((8, 128), F32)
        for n, arr in enumerate(arrays):
            for x in range(4):
                for t in range(2):
                    slot = 8 * n + 2 * x + t
                    tile = arr[x, 8 * t : 8 * t + 8, :]
                    hit = (lane >> 2) == slot
                    left = jnp.where(hit, rot(tile, 4 * slot, 1), left)
                    right = jnp.where(hit, rot(tile, 4 * slot - 60, 1), right)
        return left, right

    e1x = send_planes(gg1.at[0:2], gg1x.at[1], gg1.at[2:4], gg1x.at[0])
    pack1[0], pack1[1] = pack_sides1([own1, diag1, gg1[...]])
    e1s = send_sides(pack1, rs1)

    packv[0, 0], packv[1, 0] = pack_sides(v2m, 2)
    evx = [send(v2m.at[8], v2m.at[0], 1, 0), send(v2m.at[3], v2m.at[11], -1, 0)]
    evs = send_sides(packv, rsv)

    for c in ekd + e1x + e1s:
        c.wait_recv()

    def keep1(step):
        there = inside(step)
        return jnp.logical_or(lane < (64 + 4 * has_right) * there, lane >= 128 - 4 * has_left * there)

    def fill1(ref, depth, center, rs, n, masked):
        for p in range(4 + 2 * depth):
            x = p - depth
            step = (x + 4) // 4
            for t in range(2):
                slot = 8 * n + 2 * (x % 4) + t
                tile = jnp.where(
                    lane < 64,
                    center(x, slice(8 * t, 8 * t + 8)),
                    jnp.where(lane < 96, rot(rs[step, 0], 64 - 4 * slot, 1), rot(rs[step, 1], 124 - 4 * slot, 1)),
                )
                if masked:
                    tile = jnp.where(keep1(step - 1), tile, 0.0)
                ref[p, 8 * t : 8 * t + 8, :] = tile

    def pick(own, x_ref, depth, x, rows, shift=0):
        if x < 0:
            return rot(x_ref[0, x + depth, rows, :], shift, 1)
        if x > 3:
            return rot(x_ref[1, x - 4, rows, :], shift, 1)
        return rot(own[x, rows, :], shift, 1)

    fill1(k1, 3, lambda x, r: pick(kd1, kd1x, 3, x, r), rs1, 0, True)
    fill1(dg1, 2, lambda x, r: pick(kd1, kd1x, 3, x, r, 64), rs1, 1, False)
    fill1(f1, 2, lambda x, r: pick(gg1, gg1x, 2, x, r), rs1, 2, False)

    lane1 = iota((2, 16, 128), 2)

    def inverse1(lo, hi, step):
        there = inside(step)
        keep = jnp.logical_or(lane1 < (64 + 4 * has_right) * there, lane1 >= 128 - 4 * has_left * there)
        return jnp.where(keep, OMEGA / dg1[lo:hi], 0.0)

    def level1_inverse():
        return jnp.concatenate([inverse1(0, 2, -1), inverse1(2, 4, 0), inverse1(4, 6, 0), inverse1(6, 8, 1)], axis=0)

    def sweep1(v, depth, inv):
        kk = k1[3 - depth : 7 + depth]
        lo, hi = 3 - depth, 5 + depth
        rest = f1[lo:hi] - ring_apply(v, kk, dg1[lo:hi], half1)
        return v[1:-1] + inv[lo:hi] * rest

    inv1 = level1_inverse()
    v = sweep1(inv1 * f1[...], 2, inv1)
    r = f1[2:6] - ring_apply(v, k1[2:8], dg1[2:6], half1)
    for i in range(2):
        t1[16 * i : 16 * i + 16, :] = r[2 * i] + r[2 * i + 1]
    rhs2 = (0.125 * dot(halve_rows(t1, 16), r12)).reshape(2, 8, 128)

    whole = jnp.where(lane8 < 32, rhs2, p2c[...])
    p2c[...] = whole
    left, right = jnp.zeros((8, 128), F32), jnp.zeros((8, 128), F32)
    for n in range(4):
        for x in range(2):
            slot = 2 * n + x
            hit = (lane >> 3) == slot
            left = jnp.where(hit, rot(whole[x], 8 * slot - 32 * n, 1), left)
            right = jnp.where(hit, rot(whole[x], 8 * slot - 32 * n - 24, 1), right)
    p2s[0], p2s[1] = left, right
    e2 = []
    for a, b in FAR:
        if b == 0:
            e2.append(send(p2c, r2c.at[4 - a], a, b))
        else:
            side = 0 if b < 0 else 1
            e2.append(send(p2s.at[side], r2s.at[4 - a, side], a, b))

    vv1[...] = v[1:5]
    pv1[0], pv1[1] = pack_sides1([v[1:5]])
    ev1x = send_planes(vv1.at[0:3], vv1x.at[1], vv1.at[1:4], vv1x.at[0])
    ev1s = send_sides(pv1, rsv1)
    r2c[4] = whole

    for c in e2:
        c.wait_recv()

    for step in range(9):
        there = inside(step - 4)
        keep = jnp.logical_or(lane < (32 + 8 * has_right) * there, lane >= 128 - 8 * has_left * there)
        for x in range(2):
            mid = r2c[step, x]
            for n, ref in enumerate((f2, l2, k2, dg2)):
                slot = 2 * n + x
                tile = jnp.where(
                    lane < 32,
                    rot(mid, -32 * n, 1),
                    jnp.where(
                        lane < 64, rot(r2s[step, 0], 32 - 8 * slot, 1), rot(r2s[step, 1], 120 - 8 * slot, 1)
                    ),
                )
                if ref is k2:
                    tile = jnp.where(keep, tile, 0.0)
                elif ref is dg2:
                    t2[2 * step + x] = jnp.where(keep, OMEGA / tile, 0.0)
                ref[2 * step + x] = tile

    def sweep2(v, depth):
        lo, hi = 9 - depth, 9 + depth
        rest = f2[lo:hi] - ring_apply(v, k2[lo - 1 : hi + 1], dg2[lo:hi], half2)
        return v[1:-1] + t2[lo:hi] * rest

    vb = sweep2(t2[...] * f2[...], 8)
    r = f2[2:16] - ring_apply(vb, k2[1:17], dg2[2:16], half2)

    def to_level3(x, planes):
        for i in range(planes):
            t1[8 * i : 8 * i + 8, :] = x[2 * i] + x[2 * i + 1]
        y = 0.125 * dot(halve_rows(t1, 4 * planes), r23)
        for i in range(planes):
            t3[i, 0:4, :] = y[4 * i : 4 * i + 4, :]
        return t3[0:planes]

    t3[...] = jnp.zeros_like(t3)
    half3 = 0.5 * 0.015625
    k3 = to_level3(k2[...], 9)
    l3 = to_level3(l2[2:16], 7)
    f3 = to_level3(r, 7)
    diag3 = l3 + half3 * (CALL * k3[1:-1] + ring_sum(k3))
    row = iota((8, 128), 0)
    inv3 = []
    for i in range(7):
        there = inside(i - 3)
        keep = jnp.logical_or(lane < (16 + 4 * has_right) * there, lane >= 128 - 4 * has_left * there)
        inv3.append(jnp.where(jnp.logical_and(keep, row < 4), OMEGA / diag3[i], 0.0)[None])
    inv3 = jnp.concatenate(inv3, axis=0)
    v3 = inv3 * f3
    rest = f3[1:-1] - ring_apply(v3, k3[1:-1], diag3[1:-1], half3)
    v3 = v3[1:-1] + inv3[1:-1] * rest

    p32 = ring_map(cut(64), 64, True)
    wide3 = dot(v3.reshape(40, 128), p32)
    for i in range(5):
        double_rows(t1.at[8 * i : 8 * i + 8, :], wide3[8 * i : 8 * i + 4, :])
    e3 = t1[0:40, :].reshape(5, 8, 128)
    e3 = jnp.concatenate([e3[i // 2][None] for i in range(10)], axis=0)
    vb = vb[3:13] + e3
    vb = sweep2(vb, 4)
    vb = sweep2(vb, 3)

    for c in ev1x + ev1s:
        c.wait_recv()
    fill1(va1, 3, lambda x, r: pick(vv1, vv1x, 3, x, r), rsv1, 0, True)
    p21 = ring_map(cut(96), 64, True)
    double_rows(tm.at[0:96, :], dot(vb.reshape(48, 128), p21))
    e2v = tm[0:96, :].reshape(6, 16, 128)
    v = jnp.concatenate([va1[p : p + 1] + e2v[((p - 3) // 2 + 2) : ((p - 3) // 2 + 3)] for p in range(10)], axis=0)
    keep_planes = jnp.concatenate(
        [jnp.where(keep1((p + 1) // 4 - 1), 1.0, 0.0)[None] for p in range(10)], axis=0
    )
    v = v * jnp.concatenate([keep_planes, keep_planes], axis=1)
    v = sweep1(v, 3, inv1)
    v = sweep1(v, 2, inv1)

    e1 = v.reshape(96, 128)
    double_rows(tm.at[0:192, :], dot(e1, ring_map(main_z, 96, True)))
    double_rows(ts.at[0:192, :], dot(e1, ring_map(side_z, 96, True)))
    for c in evx + evs:
        c.wait()
    unpack_sides(rsv, 0, v2s, 2, True)

    def correct(q, c):
        there = there0(q)
        rows = pl.ds(pl.multiple_of(32 * (q // 2), 32), 32)
        v1m[q] = jnp.where(lane32 < 128 * there, v2m[q] + tm[rows, :], 0.0)
        keep = jnp.logical_or(lane32 < 4 * has_right * there, lane32 >= 128 - 4 * has_left * there)
        v1s[q] = jnp.where(keep, v2s[q] + ts[rows, :], 0.0)
        return c

    lax.fori_loop(0, 12, correct, 0)
    lax.fori_loop(0, 12, parts(v1m, v1s), 0)
    lax.fori_loop(1, 11, sweep(v1m, v1s, v2m, v2s), 0)
    lax.fori_loop(1, 11, parts_main(v2m, v2s), 0)

    def last(q, c):
        out_ref[q - 2] = v2m[q] + dm[q] * resid(q, v2m, fm, dgm, km, g1m, h1m, g2m, h2m)
        return c

    lax.fori_loop(2, 10, last, 0)
    for c in started:
        if not any(c is done for done in evx + evs):
            c.wait_send()


def solution(mesh):
    nw, nz = mesh.shape["wide"], mesh.shape["narrow"]

    def on_device(source, permeability, leakage):
        def vm(*shape):
            return pltpu.VMEM(shape, F32)

        p16, p12 = vm(16, 32, 128), vm(12, 32, 128)
        scratch = [p16, p16, p12, p12, p12, p12, p12, p12, p12, p12, p12, p12, p12, p12]
        scratch += [p16, p16, p16, p16, p12, p12, p12, p12, vm(256, 128), vm(256, 128)]
        scratch += [vm(2, 3, 8, 128), vm(3, 2, 3, 8, 128), vm(2, 1, 8, 128), vm(3, 2, 1, 8, 128)]
        scratch += [vm(4, 16, 128), vm(2, 3, 16, 128), vm(4, 16, 128), vm(2, 2, 16, 128)]
        scratch += [vm(2, 8, 128), vm(3, 2, 8, 128), vm(2, 8, 128), vm(3, 2, 8, 128)]
        scratch += [vm(4, 16, 128), vm(2, 3, 16, 128)]
        scratch += [vm(8, 16, 128), vm(10, 16, 128), vm(8, 16, 128), vm(8, 16, 128), vm(10, 16, 128), vm(128, 128)]
        scratch += [vm(2, 8, 128), vm(2, 8, 128), vm(9, 2, 8, 128), vm(9, 2, 8, 128)]
        scratch += [vm(18, 8, 128), vm(18, 8, 128), vm(18, 8, 128), vm(18, 8, 128), vm(18, 8, 128), vm(9, 8, 128)]
        n = 12 + 2 + 8 + 8 + 26 + 8
        scratch += [pltpu.SemaphoreType.DMA((3,)), pltpu.SemaphoreType.DMA((n,)), pltpu.SemaphoreType.DMA((n,))]

        def body(*refs):
            kernel(nw, nz, *refs)

        return pl.pallas_call(
            body,
            out_shape=jax.ShapeDtypeStruct(source.shape, F32),
            in_specs=[pl.BlockSpec(memory_space=pl.ANY)] * 3,
            out_specs=pl.BlockSpec(memory_space=pltpu.VMEM),
            scratch_shapes=scratch,
            compiler_params=pltpu.CompilerParams(
                collective_id=0, has_side_effects=True, vmem_limit_bytes=48 * 2**20
            ),
            name="vcycle",
        )(source, permeability, leakage)

    spec = P("wide", None, "narrow")
    return jax.shard_map(on_device, mesh=mesh, in_specs=(spec, spec, spec), out_specs=spec, check_vma=False)
```

```python
import jax
import jax.numpy as jnp
from jax import lax
from jax.experimental import pallas as pl
from jax.experimental.pallas import tpu as pltpu
from jax.sharding import PartitionSpec as P

MESH = pl.DeviceIdType.MESH
OMEGA = 0.8
F32 = jnp.float32


def weight(a, b, c):
    n = a + b + c
    return (a * 1.0 + b * 0.7 + c * 0.4) / n * {1: 1.0, 2: 0.25, 3: 0.1}[n]


CX, CY, CZ = weight(1, 0, 0), weight(0, 1, 0), weight(0, 0, 1)
CXY, CXZ, CYZ, CXYZ = weight(1, 1, 0), weight(1, 0, 1), weight(0, 1, 1), weight(1, 1, 1)
CALL = 2 * (CX + CY + CZ) + 4 * (CXY + CXZ + CYZ) + 8 * CXYZ

SIDES = [(a, b) for b in (-1, 1) for a in (-1, 0, 1)]
FAR = [(a, b) for a in range(-4, 5) for b in (-1, 0, 1) if (a, b) != (0, 0)]


def iota(shape, dim):
    return lax.broadcasted_iota(jnp.int32, shape, dim)


def lanes():
    return iota((8, 128), 1)


def rot(x, shift, axis):
    shift %= x.shape[axis]
    return x if shift == 0 else pltpu.roll(x, shift, axis)


def rows_beside(t):
    axis = t.ndim - 2
    n = t.shape[axis]
    row = iota(t.shape, axis)
    up = jnp.where(row == 0, 0.0, rot(t, 1, axis))
    down = jnp.where(row == n - 1, 0.0, rot(t, n - 1, axis))
    return up + down


def planes_of(u, pz):
    g = CX * u + CXZ * pz + rows_beside(CXY * u + CXYZ * pz)
    h = CZ * pz + rows_beside(CY * u + CYZ * pz)
    return g, h


def neighbours(u, p, y):
    x, xp = u[0] + u[2], p[0] + p[2]
    inner = CXY * x + CXYZ * xp + CY * u[1] + CYZ * p[1]
    return CX * x + CXZ * xp + CZ * p[1] + y(inner)


def lanes_main(m, s):
    lane = iota(m.shape, 1)
    below = jnp.concatenate([rot(s, 105 - 32 * t, 1) for t in range(4)], axis=0)
    above = jnp.concatenate([rot(s, 119 - 32 * t, 1) for t in range(4)], axis=0)
    return jnp.where(lane == 0, below, rot(m, 1, 1)) + jnp.where(lane == 127, above, rot(m, 127, 1))


def lanes_strip(s):
    return rot(s, 1, 1) + rot(s, 127, 1)


def rows_strip(c):
    row, lane = iota((8, 128), 0), iota((8, 128), 1)
    up, down = rot(c, 1, 0), rot(c, 7, 0)
    up = jnp.where(row == 0, jnp.where(lane < 32, 0.0, rot(up, 32, 1)), up)
    down = jnp.where(row == 7, jnp.where(lane >= 96, 0.0, rot(down, 96, 1)), down)
    return up + down


def ring_sum(u):
    pz = rot(u, 1, 2) + rot(u, 127, 2)
    g, h = planes_of(u, pz)
    return g[:-2] + g[2:] + h[1:-1]


def ring_apply(v, k, diag, half):
    return diag * v[1:-1] - half * (k[1:-1] * ring_sum(v) + ring_sum(k * v))


def dot(a, b):
    return lax.dot_general(a, b, (((1,), (0,)), ((), ())), precision=lax.Precision.HIGHEST, preferred_element_type=F32)


def ring_map(fine_of, coarse_cut, transpose=False):
    f_dim = 1 if transpose else 0
    i, j = iota((128, 128), f_dim), iota((128, 128), 1 - f_dim)
    return ((fine_of(i) >> 1) == jnp.where(j < coarse_cut, j, j - 128)).astype(F32)


def cut(c):
    return lambda i: jnp.where(i < c, i, i - 128)


def main_z(i):
    return i


def strip_z(i):
    r = i & 31
    return jnp.where(r < 16, r + 120, r - 24)


def strip_halo_z(i):
    r = i & 31
    return jnp.where(jnp.logical_or(r < 8, r >= 24), 4096, strip_z(i))


def halve_rows(ref, n):
    return ref[pl.ds(0, n, stride=2), :] + ref[pl.ds(1, n, stride=2), :]


def double_rows(ref, x):
    n = x.shape[0]
    ref[pl.ds(0, n, stride=2), :] = x
    ref[pl.ds(1, n, stride=2), :] = x


def kernel(
    nw, nz, f_hbm, k_hbm, l_hbm, out_ref,
    km, ks, pkm, pks, fm, fs, lm, ls, dgm, dgs, dm, ds_,
    avm, avs, apm, aps, aqm, aqs, arm, ars, bvm, bvs, bpm, bps, bqm, bqs, brm, brs, tm, ts,
    pack0, rs0, packv, rsv, kd1, kd1x, gg1, gg1x, pack1, rs1, pv1, rsv1, vv1, vv1x,
    k1l, k1, dg1, f1, va1, t1, kd2, kd2x, gl2, gl2x, k2, dg2, f2, l2, t2, t3, loc_sem, send_sem, recv_sem,
):
    w, z = lax.axis_index("wide"), lax.axis_index("narrow")

    def device(a, b):
        return (lax.rem(w + (a + nw), nw), lax.rem(z + (b + nz), nz))

    def in_grid(a, b):
        ok = jnp.logical_and(w + a >= 0, w + a < nw)
        return ok if b == 0 else jnp.logical_and(ok, jnp.logical_and(z + b >= 0, z + b < nz))

    has_left, has_right = (z > 0).astype(jnp.int32), (z < nz - 1).astype(jnp.int32)

    def inside(step):
        return jnp.logical_and(w + step >= 0, w + step < nw).astype(jnp.int32)

    class Message:
        def __init__(self, n, src, dst, a, b):
            self.to, self.origin = (a, b), (-a, -b)
            self.copy = pltpu.make_async_remote_copy(
                src_ref=src, dst_ref=dst, send_sem=send_sem.at[n], recv_sem=recv_sem.at[n],
                device_id=device(a, b), device_id_type=MESH,
            )
            pl.when(in_grid(*self.to))(self.copy.start)

        def arrived(self):
            pl.when(in_grid(*self.origin))(self.copy.wait_recv)

        def left(self):
            pl.when(in_grid(*self.to))(self.copy.wait_send)

    started = []

    def send(src, dst, a, b):
        started.append(Message(len(started), src, dst, a, b))
        return started[-1]

    lane, row = lanes(), iota((8, 128), 0)
    group, place = lane >> 5, lane & 31

    for ref in (rs0, rsv, rs1, rsv1, kd1x, gg1x, vv1x, kd2x, gl2x):
        ref[...] = jnp.zeros_like(ref)

    def clear(k_planes, planes, v_plane):
        def body():
            km[k_planes] = jnp.zeros((4, 32, 128), F32)
            fm[planes] = jnp.zeros((2, 32, 128), F32)
            lm[planes] = jnp.zeros((2, 32, 128), F32)
            bvm[v_plane] = jnp.zeros((32, 128), F32)

        return body

    pl.when(w == 0)(clear(slice(0, 4), slice(0, 2), 0))
    pl.when(w == nw - 1)(clear(slice(12, 16), slice(10, 12), 11))

    barrier = pltpu.get_barrier_semaphore()

    def greet(a, b):
        def body():
            pl.semaphore_signal(barrier, inc=1, device_id=device(a, b), device_id_type=MESH)

        return body

    for a, b in FAR:
        pl.when(in_grid(a, b))(greet(a, b))
    loads = []
    for n, (src, dst) in enumerate(((k_hbm, km.at[4:12]), (f_hbm, fm.at[2:10]), (l_hbm, lm.at[2:10]))):
        loads.append(pltpu.make_async_copy(src, dst, loc_sem.at[n]))
        loads[-1].start()

    def own_strip(m):
        out = None
        for t in range(4):
            tile = m[8 * t : 8 * t + 8, :]
            part = jnp.where(place < 16, rot(tile, 32 * t + 8, 1), rot(tile, 32 * t + 24, 1))
            out = part if out is None else jnp.where(group == t, part, out)
        return out

    def pack_strips(strips):
        left, right = jnp.zeros((8, 128), F32), jnp.zeros((8, 128), F32)
        for x, s in enumerate(strips):
            hit = (place >> 2) == x
            left = jnp.where(hit, rot(s, 4 * x - 24, 1), left)
            right = jnp.where(hit, rot(s, 4 * x - 4, 1), right)
        return left, right

    def whole_strip(own, rs, n, x):
        step, at = (x + 8) // 8, x % 8
        halo = jnp.where(place < 16, rot(rs[step, 0, n], 8 - 4 * at, 1), rot(rs[step, 1, n], 20 - 4 * at, 1))
        halo = jnp.where(jnp.logical_or(place < 12, place >= 20), halo, 0.0)
        return jnp.where(jnp.logical_or(place < 8, place >= 24), own, halo)

    for n, (ref, strip, off) in enumerate(((km, ks, 4), (fm, fs, 2), (lm, ls, 2))):
        loads[n].wait()
        own = [own_strip(ref[x + off]) for x in range(8)]
        for x in range(8):
            strip[x + off] = own[x]
        pack0[0, n], pack0[1, n] = pack_strips(own)

    def count(pos, reach, size):
        return jnp.minimum(pos, reach) + 1 + jnp.minimum(size - 1 - pos, reach)

    pl.semaphore_wait(barrier, count(w, 4, nw) * count(z, 1, nz) - 1)

    def send_planes(src_lo, dst_hi, src_hi, dst_lo):
        return [send(src_hi, dst_lo, 1, 0), send(src_lo, dst_hi, -1, 0)]

    def send_sides(pack, rs):
        return [send(pack.at[0 if b < 0 else 1], rs.at[1 - a, 0 if b < 0 else 1], a, b) for a, b in SIDES]

    def send_far(src, dst):
        return [send(src, dst.at[4 - a, 1 - b], a, b) for a, b in FAR]

    e0k = send_planes(km.at[4:8], km.at[12:16], km.at[8:12], km.at[0:4])
    e0s = send_sides(pack0, rs0)
    e0f = send_planes(fm.at[2:4], fm.at[10:12], fm.at[8:10], fm.at[0:2])
    e0l = send_planes(lm.at[2:4], lm.at[10:12], lm.at[8:10], lm.at[0:2])

    rm01, rs01 = ring_map(main_z, 96), ring_map(strip_halo_z, 96)
    r12, r23 = ring_map(cut(96), 64), ring_map(cut(64), 64)

    for c in e0k + e0s:
        c.arrived()
    for p in range(16):
        own = ks[p] if 4 <= p < 12 else own_strip(km[p])
        ks[p] = whole_strip(own, rs0, 0, p - 4)

    def k_lanes(i, c):
        for p in (2 * i, 2 * i + 1):
            m, s = km[p], ks[p]
            pkm[p], pks[p] = lanes_main(m, s), lanes_strip(s)
        tm[pl.ds(pl.multiple_of(32 * i, 32), 32), :] = km[2 * i] + km[2 * i + 1]
        pair = ks[2 * i] + ks[2 * i + 1]
        parts = [jnp.where(group == t, pair, 0.0) for t in range(4)]
        ts[pl.ds(pl.multiple_of(32 * i, 32), 32), :] = jnp.concatenate(parts, axis=0)
        return c

    lax.fori_loop(0, 8, k_lanes, 0)

    coarse = dot(halve_rows(tm, 128), rm01) + dot(halve_rows(ts, 128), rs01)
    k1l[...] = (0.125 * coarse).reshape(8, 16, 128)

    def l_pairs(i, c):
        tm[pl.ds(pl.multiple_of(32 * i, 32), 32), :] = lm[2 * i + 2] + lm[2 * i + 3]
        return c

    lax.fori_loop(0, 4, l_pairs, 0)
    l1 = (0.125 * dot(halve_rows(tm, 64), rm01)).reshape(4, 16, 128)
    own1 = k1l[2:6]
    half1 = 0.5 * 0.25
    diag1 = l1 + half1 * (CALL * own1 + ring_sum(k1l[1:7]))
    lane16 = iota((4, 16, 128), 2)
    kd1[...] = jnp.where(lane16 < 64, own1, rot(diag1, 64, 2))
    ekd = send_planes(kd1.at[0:3], kd1x.at[1], kd1.at[1:4], kd1x.at[0])

    for c in e0f + e0l:
        c.arrived()
    for n, (ref, strip) in ((1, (fm, fs)), (2, (lm, ls))):
        for p in range(12):
            own = strip[p] if 2 <= p < 10 else own_strip(ref[p])
            strip[p] = whole_strip(own, rs0, n, p - 2)

    lane32 = iota((32, 128), 1)

    def three(ref, i):
        return ref[i - 1], ref[i], ref[i + 1]

    def ready(v, i, m, s, strips):
        vm, vs, pm, ps, qm, qs, rm, rs = v
        vm[i], vs[i] = m, s
        pm[i] = lanes_main(m, s)
        m, s = m * km[i + 2], s * ks[i + 2]
        qm[i], rm[i] = m, lanes_main(m, s)
        if strips:
            ps[i] = lanes_strip(vs[i])
            qs[i], rs[i] = s, lanes_strip(s)

    field_a = (avm, avs, apm, aps, aqm, aqs, arm, ars)
    field_b = (bvm, bvs, bpm, bps, bqm, bqs, brm, brs)

    def resid_main(v, i):
        vm, vs, pm, ps, qm, qs, rm, rs = v
        s1 = neighbours(three(vm, i), three(pm, i), rows_beside)
        s2 = neighbours(three(qm, i), three(rm, i), rows_beside)
        return fm[i] - dgm[i] * vm[i] + 0.5 * (km[i + 2] * s1 + s2)

    def resid_strip(v, i):
        vm, vs, pm, ps, qm, qs, rm, rs = v
        s1 = neighbours(three(vs, i), three(ps, i), rows_strip)
        s2 = neighbours(three(qs, i), three(rs, i), rows_strip)
        return fs[i] - dgs[i] * vs[i] + 0.5 * (ks[i + 2] * s1 + s2)

    def loop(lo, hi, step, body):
        def go(n, c):
            for i in range(step):
                body(lo + step * n + i)
            return c

        lax.fori_loop(0, (hi - lo) // step, go, 0)

    def first(i):
        there = jnp.where(i < 2, inside(-1), jnp.where(i >= 10, inside(1), 1))
        around = neighbours(three(km, i + 2), three(pkm, i + 2), rows_beside)
        diag = lm[i] + 0.5 * (CALL * km[i + 2] + around)
        inv = jnp.where(lane32 < 128 * there, OMEGA / diag, 0.0)
        dgm[i], dm[i] = diag, inv
        m = inv * fm[i]
        around = neighbours(three(ks, i + 2), three(pks, i + 2), rows_strip)
        diag = ls[i] + 0.5 * (CALL * ks[i + 2] + around)
        keep = jnp.logical_or(place < (8 + 4 * has_right) * there, place >= 32 - (8 + 4 * has_left) * there)
        inv = jnp.where(keep, OMEGA / diag, 0.0)
        dgs[i], ds_[i] = diag, inv
        ready(field_a, i, m, inv * fs[i], True)

    loop(0, 12, 2, first)

    def sweep(i):
        m = avm[i] + dm[i] * resid_main(field_a, i)
        s = avs[i] + ds_[i] * resid_strip(field_a, i)
        ready(field_b, i, m, s, False)

    loop(1, 11, 2, sweep)

    def resid_pairs(i, c):
        pair = resid_main(field_b, 2 * i + 2) + resid_main(field_b, 2 * i + 3)
        tm[pl.ds(pl.multiple_of(32 * i, 32), 32), :] = pair
        return c

    lax.fori_loop(0, 4, resid_pairs, 0)
    gg1[...] = (0.125 * dot(halve_rows(tm, 64), rm01)).reshape(4, 16, 128)

    def pack_sides1(arrays):
        left, right = jnp.zeros((8, 128), F32), jnp.zeros((8, 128), F32)
        for n, arr in enumerate(arrays):
            for x in range(4):
                for t in range(2):
                    slot = 8 * n + 2 * x + t
                    tile = arr[x, 8 * t : 8 * t + 8, :]
                    hit = (lane >> 2) == slot
                    left = jnp.where(hit, rot(tile, 4 * slot, 1), left)
                    right = jnp.where(hit, rot(tile, 4 * slot - 60, 1), right)
        return left, right

    e1x = send_planes(gg1.at[0:2], gg1x.at[1], gg1.at[2:4], gg1x.at[0])
    pack1[0], pack1[1] = pack_sides1([own1, diag1, gg1[...]])
    e1s = send_sides(pack1, rs1)

    kk = k1l[...]
    for i in range(4):
        t1[16 * i : 16 * i + 16, :] = kk[2 * i] + kk[2 * i + 1]
    k2l = (0.125 * dot(halve_rows(t1, 32), r12)).reshape(4, 8, 128)
    for i in range(2):
        t1[16 * i : 16 * i + 16, :] = l1[2 * i] + l1[2 * i + 1]
    l2own = (0.125 * dot(halve_rows(t1, 16), r12)).reshape(2, 8, 128)
    half2 = 0.5 * 0.0625
    diag2 = l2own + half2 * (CALL * k2l[1:3] + ring_sum(k2l))
    both = (k2l[1], k2l[2], diag2[0], diag2[1])
    low = jnp.where(lane < 32, both[0], rot(both[1], 32, 1))
    high = jnp.where(lane < 96, rot(both[2], 64, 1), rot(both[3], 96, 1))
    kd2[...] = jnp.where(lane < 64, low, high)
    l2sum = rot(l2own[0] + l2own[1], 64, 1)
    ekd2 = send_far(kd2, kd2x)

    packv[0, 0], packv[1, 0] = pack_strips([bvs[x + 2] for x in range(8)])
    evx = [send(bvm.at[8], bvm.at[0], 1, 0), send(bvm.at[3], bvm.at[11], -1, 0)]
    evs = send_sides(packv, rsv)

    def fill1(ref, depth, center, rs, n):
        for p in range(4 + 2 * depth):
            x = p - depth
            step = (x + 4) // 4
            for t in range(2):
                slot = 8 * n + 2 * (x % 4) + t
                beside = jnp.where(lane < 96, rot(rs[step, 0], 64 - 4 * slot, 1), rot(rs[step, 1], 124 - 4 * slot, 1))
                beside = jnp.where(jnp.logical_or(lane < 68, lane >= 124), beside, 0.0)
                ref[p, 8 * t : 8 * t + 8, :] = jnp.where(lane < 64, center(x, slice(8 * t, 8 * t + 8)), beside)

    def pick(own, x_ref, depth, x, rows, shift=0):
        if x < 0:
            return rot(x_ref[0, x + depth, rows, :], shift, 1)
        if x > 3:
            return rot(x_ref[1, x - 4, rows, :], shift, 1)
        return rot(own[x, rows, :], shift, 1)

    for c in ekd + e1x + e1s:
        c.arrived()
    fill1(k1, 3, lambda x, r: pick(kd1, kd1x, 3, x, r), rs1, 0)
    fill1(dg1, 2, lambda x, r: pick(kd1, kd1x, 3, x, r, 64), rs1, 1)
    fill1(f1, 2, lambda x, r: pick(gg1, gg1x, 2, x, r), rs1, 2)

    lane1 = iota((2, 16, 128), 2)

    def inverse1(lo, hi, step):
        there = inside(step)
        keep = jnp.logical_or(lane1 < (64 + 4 * has_right) * there, lane1 >= 128 - 4 * has_left * there)
        return jnp.where(keep, OMEGA / dg1[lo:hi], 0.0)

    def sweep1(v, depth, inv):
        kk = k1[3 - depth : 7 + depth]
        lo, hi = 3 - depth, 5 + depth
        rest = f1[lo:hi] - ring_apply(v, kk, dg1[lo:hi], half1)
        return v[1:-1] + inv[lo:hi] * rest

    inv1 = jnp.concatenate([inverse1(0, 2, -1), inverse1(2, 4, 0), inverse1(4, 6, 0), inverse1(6, 8, 1)], axis=0)
    v = sweep1(inv1 * f1[...], 2, inv1)
    r = f1[2:6] - ring_apply(v, k1[2:8], dg1[2:6], half1)
    for i in range(2):
        t1[16 * i : 16 * i + 16, :] = r[2 * i] + r[2 * i + 1]
    rhs2 = (0.125 * dot(halve_rows(t1, 16), r12)).reshape(2, 8, 128)

    gl2[...] = jnp.where(lane < 32, rhs2[0], jnp.where(lane < 64, rot(rhs2[1], 32, 1), l2sum))
    e2 = send_far(gl2, gl2x)
    vv1[...] = v[1:5]
    pv1[0], pv1[1] = pack_sides1([v[1:5]])
    ev1x = send_planes(vv1.at[0:3], vv1x.at[1], vv1.at[1:4], vv1x.at[0])
    ev1s = send_sides(pv1, rsv1)

    def near2(own, ref, step, n):
        mid = own if step == 4 else ref[step, 1]
        beside = jnp.where(lane < 64, rot(ref[step, 2], 32 - 32 * n, 1), rot(ref[step, 0], 96 - 32 * n, 1))
        beside = jnp.where(jnp.logical_or(lane < 40, lane >= 120), beside, 0.0)
        return jnp.where(lane < 32, rot(mid, -32 * n, 1), beside)

    for c in ekd2:
        c.arrived()
    mine = kd2[...]
    for step in range(9):
        there = inside(step - 4)
        keep = jnp.logical_or(lane < (32 + 8 * has_right) * there, lane >= 128 - 8 * has_left * there)
        for x in range(2):
            k2[2 * step + x] = near2(mine, kd2x, step, x)
            diag = near2(mine, kd2x, step, 2 + x)
            dg2[2 * step + x] = diag
            t2[2 * step + x] = jnp.where(keep, OMEGA / diag, 0.0)

    def to_level3(pairs):
        n = len(pairs)
        for i, pair in enumerate(pairs):
            t1[8 * i : 8 * i + 8, :] = pair
        y = 0.125 * dot(halve_rows(t1, 4 * n), r23)
        for i in range(n):
            t3[i, 0:4, :] = y[4 * i : 4 * i + 4, :]
        return t3[0:n]

    t3[...] = jnp.zeros_like(t3)
    half3 = 0.5 * 0.015625
    k3 = to_level3([k2[2 * i] + k2[2 * i + 1] for i in range(9)])
    most3 = half3 * (CALL * k3[1:-1] + ring_sum(k3))

    for c in e2:
        c.arrived()
    mine = gl2[...]
    for step in range(9):
        for x in range(2):
            f2[2 * step + x] = near2(mine, gl2x, step, x)
        l2[step] = near2(mine, gl2x, step, 2)

    def sweep2(v, depth):
        lo, hi = 9 - depth, 9 + depth
        rest = f2[lo:hi] - ring_apply(v, k2[lo - 1 : hi + 1], dg2[lo:hi], half2)
        return v[1:-1] + t2[lo:hi] * rest

    vb = sweep2(t2[...] * f2[...], 8)
    r = f2[2:16] - ring_apply(vb, k2[1:17], dg2[2:16], half2)
    l3 = to_level3([l2[i + 1] for i in range(7)])
    f3 = to_level3([r[2 * i] + r[2 * i + 1] for i in range(7)])
    diag3 = l3 + most3
    inv3 = []
    for i in range(7):
        there = inside(i - 3)
        keep = jnp.logical_or(lane < (16 + 4 * has_right) * there, lane >= 128 - 4 * has_left * there)
        inv3.append(jnp.where(jnp.logical_and(keep, row < 4), OMEGA / diag3[i], 0.0)[None])
    inv3 = jnp.concatenate(inv3, axis=0)
    v3 = inv3 * f3
    rest = f3[1:-1] - ring_apply(v3, k3[1:-1], diag3[1:-1], half3)
    v3 = v3[1:-1] + inv3[1:-1] * rest

    p32 = ring_map(cut(64), 64, True)
    wide3 = dot(v3.reshape(40, 128), p32)
    for i in range(5):
        double_rows(t1.at[8 * i : 8 * i + 8, :], wide3[8 * i : 8 * i + 4, :])
    e3 = t1[0:40, :].reshape(5, 8, 128)
    e3 = jnp.concatenate([e3[i // 2][None] for i in range(10)], axis=0)
    vb = vb[3:13] + e3
    vb = sweep2(vb, 4)
    vb = sweep2(vb, 3)

    for c in ev1x + ev1s:
        c.arrived()
    fill1(va1, 3, lambda x, r: pick(vv1, vv1x, 3, x, r), rsv1, 0)
    p21 = ring_map(cut(96), 64, True)
    double_rows(tm.at[0:96, :], dot(vb.reshape(48, 128), p21))
    e2v = tm[0:96, :].reshape(6, 16, 128)
    inner = jnp.logical_or(lane < 68, lane >= 124)
    inner = jnp.concatenate([inner, inner], axis=0)
    v = [jnp.where(inner, va1[p] + e2v[(p - 3) // 2 + 2], 0.0)[None] for p in range(10)]
    v = sweep1(jnp.concatenate(v, axis=0), 3, inv1)
    v = sweep1(v, 2, inv1)

    e1 = v.reshape(96, 128)
    double_rows(tm.at[0:192, :], dot(e1, ring_map(main_z, 96, True)))
    double_rows(ts.at[0:192, :], dot(e1, ring_map(strip_z, 96, True)))
    for c in evx + evs:
        c.arrived()
        c.left()
    for p in range(12):
        own = bvs[p] if 1 <= p < 11 else own_strip(bvm[p])
        bvs[p] = whole_strip(own, rsv, 0, p - 2)

    def correct(i):
        at = 32 * (i // 2)
        m = bvm[i] + tm[pl.ds(pl.multiple_of(at, 32), 32), :]
        s = ts[pl.ds(pl.multiple_of(at, 8), 8), :]
        for t in range(1, 4):
            s = jnp.where(group == t, ts[pl.ds(pl.multiple_of(at + 8 * t, 8), 8), :], s)
        s = jnp.where(jnp.logical_or(place < 12, place >= 20), bvs[i] + s, 0.0)
        ready(field_a, i, m, s, True)

    loop(0, 12, 2, correct)
    loop(1, 11, 2, sweep)

    def last(i):
        out_ref[i - 2] = bvm[i] + dm[i] * resid_main(field_b, i)

    loop(2, 10, 2, last)
    for c in started:
        if not any(c is done for done in evx + evs):
            c.left()


def solution(mesh):
    nw, nz = mesh.shape["wide"], mesh.shape["narrow"]

    def on_device(source, permeability, leakage):
        def vm(*shape):
            return pltpu.VMEM(shape, F32)

        def pair(n):
            return [vm(n, 32, 128), vm(n, 8, 128)]

        scratch = pair(16) * 2 + pair(12) * 4 + pair(12) * 8 + [vm(256, 128), vm(256, 128)]
        scratch += [vm(2, 3, 8, 128), vm(3, 2, 3, 8, 128), vm(2, 1, 8, 128), vm(3, 2, 1, 8, 128)]
        scratch += [vm(4, 16, 128), vm(2, 3, 16, 128), vm(4, 16, 128), vm(2, 2, 16, 128)]
        scratch += [vm(2, 8, 128), vm(3, 2, 8, 128), vm(2, 8, 128), vm(3, 2, 8, 128)]
        scratch += [vm(4, 16, 128), vm(2, 3, 16, 128)]
        scratch += [vm(8, 16, 128), vm(10, 16, 128), vm(8, 16, 128), vm(8, 16, 128), vm(10, 16, 128), vm(128, 128)]
        scratch += [vm(8, 128), vm(9, 3, 8, 128), vm(8, 128), vm(9, 3, 8, 128)]
        scratch += [vm(18, 8, 128), vm(18, 8, 128), vm(18, 8, 128), vm(9, 8, 128), vm(18, 8, 128), vm(9, 8, 128)]
        n = 12 + 2 + 8 + 26 + 8 + 26 + 8
        scratch += [pltpu.SemaphoreType.DMA((3,)), pltpu.SemaphoreType.DMA((n,)), pltpu.SemaphoreType.DMA((n,))]

        def body(*refs):
            kernel(nw, nz, *refs)

        return pl.pallas_call(
            body,
            out_shape=jax.ShapeDtypeStruct(source.shape, F32),
            in_specs=[pl.BlockSpec(memory_space=pltpu.HBM)] * 3,
            out_specs=pl.BlockSpec(memory_space=pltpu.VMEM),
            scratch_shapes=scratch,
            compiler_params=pltpu.CompilerParams(
                collective_id=0, has_side_effects=True, vmem_limit_bytes=60 * 2**20
            ),
            name="vcycle",
        )(source, permeability, leakage)

    spec = P("wide", None, "narrow")
    return jax.shard_map(on_device, mesh=mesh, in_specs=(spec, spec, spec), out_specs=spec, check_vma=False)
```

```python
import jax
import jax.numpy as jnp
from jax import lax
from jax.experimental import pallas as pl
from jax.experimental.pallas import tpu as pltpu
from jax.sharding import PartitionSpec as P

MESH = pl.DeviceIdType.MESH
OMEGA = 0.8
F32 = jnp.float32


def weight(a, b, c):
    n = a + b + c
    return (a * 1.0 + b * 0.7 + c * 0.4) / n * {1: 1.0, 2: 0.25, 3: 0.1}[n]


CX, CY, CZ = weight(1, 0, 0), weight(0, 1, 0), weight(0, 0, 1)
CXY, CXZ, CYZ, CXYZ = weight(1, 1, 0), weight(1, 0, 1), weight(0, 1, 1), weight(1, 1, 1)
CALL = 2 * (CX + CY + CZ) + 4 * (CXY + CXZ + CYZ) + 8 * CXYZ

SIDES = [(a, b) for b in (-1, 1) for a in (-1, 0, 1)]
FAR = [(a, b) for a in range(-4, 5) for b in (-1, 0, 1) if (a, b) != (0, 0)]


def iota(shape, dim):
    return lax.broadcasted_iota(jnp.int32, shape, dim)


def lanes():
    return iota((8, 128), 1)


def rot(x, shift, axis):
    shift %= x.shape[axis]
    return x if shift == 0 else pltpu.roll(x, shift, axis)


def rows_beside(t):
    axis = t.ndim - 2
    n = t.shape[axis]
    row = iota(t.shape, axis)
    up = jnp.where(row == 0, 0.0, rot(t, 1, axis))
    down = jnp.where(row == n - 1, 0.0, rot(t, n - 1, axis))
    return up + down


def neighbours(u, p, y):
    x, xp = u[0] + u[2], p[0] + p[2]
    inner = CXY * x + CXYZ * xp + CY * u[1] + CYZ * p[1]
    return CX * x + CXZ * xp + CZ * p[1] + y(inner)


def beside_main(m, s):
    lane = iota(m.shape, 1)
    edge = jnp.where((iota(s.shape, 1) & 31) < 7, s, rot(s, -18, 1))
    edge = jnp.concatenate([rot(edge, 121 - 32 * t, 1) for t in range(4)], axis=0)
    return jnp.where(lane == 0, edge, rot(m, 1, 1)), jnp.where(lane == 127, edge, rot(m, 127, 1))


def beside(u, axis=1):
    return rot(u, 1, axis), rot(u, 127, axis)


def rows_strip(c):
    row, lane = iota((8, 128), 0), iota((8, 128), 1)
    up, down = rot(c, 1, 0), rot(c, 7, 0)
    up = jnp.where(row == 0, jnp.where(lane < 32, 0.0, rot(up, 32, 1)), up)
    down = jnp.where(row == 7, jnp.where(lane >= 96, 0.0, rot(down, 96, 1)), down)
    return up + down


def slabs(u):
    return u[:-2], u[1:-1], u[2:]


def ring_sum(u):
    below, above = beside(u, 2)
    return neighbours(slabs(u), slabs(below + above), rows_beside)


def ring_apply(v, k, diag, half):
    k, k_below, k_above = k
    below, above = beside(v, 2)
    s1 = neighbours(slabs(v), slabs(below + above), rows_beside)
    s2 = neighbours(slabs(k * v), slabs(k_below * below + k_above * above), rows_beside)
    return diag * v[1:-1] - half * (k[1:-1] * s1 + s2)


def cut_planes(k, lo, hi):
    return tuple(part[lo:hi] for part in k)


def dot(a, b):
    return lax.dot_general(a, b, (((1,), (0,)), ((), ())), precision=lax.Precision.HIGHEST, preferred_element_type=F32)


def ring_map(fine_of, coarse_cut, transpose=False):
    f_dim = 1 if transpose else 0
    i, j = iota((128, 128), f_dim), iota((128, 128), 1 - f_dim)
    return ((fine_of(i) >> 1) == jnp.where(j < coarse_cut, j, j - 128)).astype(F32)


def cut(c):
    return lambda i: jnp.where(i < c, i, i - 128)


def main_z(i):
    return i


def strip_z(i):
    r = i & 31
    return jnp.where(r < 16, r + 122, r - 26)


def strip_halo_z(i):
    r = i & 31
    return jnp.where(jnp.logical_or(r < 6, r >= 26), 4096, strip_z(i))


def halve_rows(ref, n):
    return ref[pl.ds(0, n, stride=2), :] + ref[pl.ds(1, n, stride=2), :]


def double_rows(ref, x):
    n = x.shape[0]
    ref[pl.ds(0, n, stride=2), :] = x
    ref[pl.ds(1, n, stride=2), :] = x


def kernel(
    nw, nz, f_hbm, k_hbm, l_hbm, out_ref,
    km, ks, pkm, pks, kbm, kbs, kam, kas, fm, fs, lm, ls, dgm, dgs, dm, ds_,
    avm, avs, apm, aps, aqm, aqs, arm, ars, bvm, bvs, bpm, bps, bqm, bqs, brm, brs, tm, ts,
    pack0, rs0, packv, rsv, kd1, kd1x, gg1, gg1x, pack1, rs1, pv1, rsv1, vv1, vv1x,
    k1l, k1, dg1, f1, va1, t1, kd2, kd2x, gl2, gl2x, k2, dg2, f2, l2, t2, t3, loc_sem, send_sem, recv_sem,
):
    w, z = lax.axis_index("wide"), lax.axis_index("narrow")

    def device(a, b):
        return (lax.rem(w + (a + nw), nw), lax.rem(z + (b + nz), nz))

    def in_grid(a, b):
        ok = jnp.logical_and(w + a >= 0, w + a < nw)
        return ok if b == 0 else jnp.logical_and(ok, jnp.logical_and(z + b >= 0, z + b < nz))

    has_left, has_right = (z > 0).astype(jnp.int32), (z < nz - 1).astype(jnp.int32)

    def inside(step):
        return jnp.logical_and(w + step >= 0, w + step < nw).astype(jnp.int32)

    class Message:
        def __init__(self, n, src, dst, a, b):
            self.to, self.origin = (a, b), (-a, -b)
            self.copy = pltpu.make_async_remote_copy(
                src_ref=src, dst_ref=dst, send_sem=send_sem.at[n], recv_sem=recv_sem.at[n],
                device_id=device(a, b), device_id_type=MESH,
            )
            pl.when(in_grid(*self.to))(self.copy.start)

        def arrived(self):
            pl.when(in_grid(*self.origin))(self.copy.wait_recv)

        def left(self):
            pl.when(in_grid(*self.to))(self.copy.wait_send)

    started = []

    def send(src, dst, a, b):
        started.append(Message(len(started), src, dst, a, b))
        return started[-1]

    def loop(lo, hi, body):
        for i in range(lo, hi):
            body(i)

    lane, row = lanes(), iota((8, 128), 0)
    group, place = lane >> 5, lane & 31

    for ref in (rs0, rsv, rs1, rsv1, kd1x, gg1x, vv1x, kd2x, gl2x):
        ref[...] = jnp.zeros_like(ref)

    def clear(k_planes, planes, v_plane):
        def body():
            km[k_planes] = jnp.zeros((4, 32, 128), F32)
            fm[planes] = jnp.zeros((2, 32, 128), F32)
            lm[planes] = jnp.zeros((2, 32, 128), F32)
            bvm[v_plane] = jnp.zeros((32, 128), F32)

        return body

    pl.when(w == 0)(clear(slice(0, 4), slice(0, 2), 0))
    pl.when(w == nw - 1)(clear(slice(12, 16), slice(10, 12), 11))

    barrier = pltpu.get_barrier_semaphore()

    def greet(a, b):
        def body():
            pl.semaphore_signal(barrier, inc=1, device_id=device(a, b), device_id_type=MESH)

        return body

    for a, b in FAR:
        pl.when(in_grid(a, b))(greet(a, b))
    loads = []
    for n, (src, dst) in enumerate(((k_hbm, km.at[4:12]), (f_hbm, fm.at[2:10]), (l_hbm, lm.at[2:10]))):
        loads.append(pltpu.make_async_copy(src, dst, loc_sem.at[n]))
        loads[-1].start()

    def own_strip(m):
        out = rot(m[0:8, :], 6, 1)
        for t in range(1, 4):
            out = jnp.where(group == t, rot(m[8 * t : 8 * t + 8, :], 32 * t + 6, 1), out)
        return jnp.where(place < 16, out, rot(out, 20, 1))

    def pack_strips(strips):
        left, right = jnp.zeros((8, 128), F32), jnp.zeros((8, 128), F32)
        for x, s in enumerate(strips):
            r = rot(s, 4 * x - 26, 1)
            left = jnp.where((place >> 2) == x, r, left)
            right = jnp.where((place >> 2) == (x + 2) % 8, r, right)
        return left, right

    def halves(rs, n):
        out = []
        for step in range(3):
            left, right = rs[step, 0, n], rot(rs[step, 1, n], 40, 1)
            out.append((jnp.where(place < 16, left, right), jnp.where(place < 16, right, left)))
        return out

    own_lanes = jnp.logical_or(place < 6, place >= 26)
    used_lanes = jnp.logical_or(place < 10, place >= 22)

    def whole_strip(own, merged, x):
        step, at = (x + 8) // 8, x % 8
        halo = rot(merged[step][at // 4], 6 - 4 * at, 1)
        return jnp.where(own_lanes, own, jnp.where(used_lanes, halo, 0.0))

    for n, (ref, strip, off) in enumerate(((km, ks, 4), (fm, fs, 2), (lm, ls, 2))):
        loads[n].wait()
        own = [own_strip(ref[x + off]) for x in range(8)]
        for x in range(8):
            strip[x + off] = own[x]
        pack0[0, n], pack0[1, n] = pack_strips(own)

    def count(pos, reach, size):
        return jnp.minimum(pos, reach) + 1 + jnp.minimum(size - 1 - pos, reach)

    pl.semaphore_wait(barrier, count(w, 4, nw) * count(z, 1, nz) - 1)

    def send_planes(src_lo, dst_hi, src_hi, dst_lo):
        return [send(src_hi, dst_lo, 1, 0), send(src_lo, dst_hi, -1, 0)]

    def send_sides(pack, rs):
        return [send(pack.at[0 if b < 0 else 1], rs.at[1 - a, 0 if b < 0 else 1], a, b) for a, b in SIDES]

    def send_far(src, dst):
        return [send(src, dst.at[4 - a, 1 - b], a, b) for a, b in FAR]

    e0k = send_planes(km.at[4:8], km.at[12:16], km.at[8:12], km.at[0:4])
    e0s = send_sides(pack0, rs0)
    e0f = send_planes(fm.at[2:4], fm.at[10:12], fm.at[8:10], fm.at[0:2])
    e0l = send_planes(lm.at[2:4], lm.at[10:12], lm.at[8:10], lm.at[0:2])

    rm01, rs01 = ring_map(main_z, 96), ring_map(strip_halo_z, 96)
    r12, r23 = ring_map(cut(96), 64), ring_map(cut(64), 64)

    for c in e0k + e0s:
        c.arrived()
    merged = halves(rs0, 0)
    for p in range(16):
        own = ks[p] if 4 <= p < 12 else own_strip(km[p])
        ks[p] = whole_strip(own, merged, p - 4)

    def k_lanes(i):
        for p in (2 * i, 2 * i + 1):
            m, s = km[p], ks[p]
            below, above = beside_main(m, s)
            kbm[p], kam[p], pkm[p] = below, above, below + above
            below, above = beside(s)
            kbs[p], kas[p], pks[p] = below, above, below + above
        tm[32 * i : 32 * i + 32, :] = km[2 * i] + km[2 * i + 1]
        pair = ks[2 * i] + ks[2 * i + 1]
        parts = [jnp.where(group == t, pair, 0.0) for t in range(4)]
        ts[32 * i : 32 * i + 32, :] = jnp.concatenate(parts, axis=0)

    loop(0, 8, k_lanes)

    coarse = dot(halve_rows(tm, 128), rm01) + dot(halve_rows(ts, 128), rs01)
    k1l[...] = (0.125 * coarse).reshape(8, 16, 128)

    def l_pairs(i):
        tm[32 * i : 32 * i + 32, :] = lm[2 * i + 2] + lm[2 * i + 3]

    loop(0, 4, l_pairs)
    l1 = (0.125 * dot(halve_rows(tm, 64), rm01)).reshape(4, 16, 128)
    own1 = k1l[2:6]
    half1 = 0.5 * 0.25
    diag1 = l1 + half1 * (CALL * own1 + ring_sum(k1l[1:7]))
    lane16 = iota((4, 16, 128), 2)
    kd1[...] = jnp.where(lane16 < 64, own1, rot(diag1, 64, 2))
    ekd = send_planes(kd1.at[0:3], kd1x.at[1], kd1.at[1:4], kd1x.at[0])

    for c in e0f + e0l:
        c.arrived()
    for n, (ref, strip) in ((1, (fm, fs)), (2, (lm, ls))):
        merged = halves(rs0, n)
        for p in range(12):
            own = strip[p] if 2 <= p < 10 else own_strip(ref[p])
            strip[p] = whole_strip(own, merged, p - 2)

    lane32 = iota((32, 128), 1)

    def three(ref, i):
        return ref[i - 1], ref[i], ref[i + 1]

    def ready(v, i, m, s, strips):
        vm, vs, pm, ps, qm, qs, rm, rs = v
        vm[i], vs[i] = m, s
        below, above = beside_main(m, s)
        pm[i], qm[i] = below + above, m * km[i + 2]
        rm[i] = below * kbm[i + 2] + above * kam[i + 2]
        if strips:
            below, above = beside(s)
            ps[i], qs[i] = below + above, s * ks[i + 2]
            rs[i] = below * kbs[i + 2] + above * kas[i + 2]

    field_a = (avm, avs, apm, aps, aqm, aqs, arm, ars)
    field_b = (bvm, bvs, bpm, bps, bqm, bqs, brm, brs)

    def resid_main(v, i):
        vm, vs, pm, ps, qm, qs, rm, rs = v
        s1 = neighbours(three(vm, i), three(pm, i), rows_beside)
        s2 = neighbours(three(qm, i), three(rm, i), rows_beside)
        return fm[i] - dgm[i] * vm[i] + 0.5 * (km[i + 2] * s1 + s2)

    def resid_strip(v, i):
        vm, vs, pm, ps, qm, qs, rm, rs = v
        s1 = neighbours(three(vs, i), three(ps, i), rows_strip)
        s2 = neighbours(three(qs, i), three(rs, i), rows_strip)
        return fs[i] - dgs[i] * vs[i] + 0.5 * (ks[i + 2] * s1 + s2)

    def first(i):
        there = inside(-1) if i < 2 else inside(1) if i >= 10 else 1
        around = neighbours(three(km, i + 2), three(pkm, i + 2), rows_beside)
        diag = lm[i] + 0.5 * (CALL * km[i + 2] + around)
        inv = jnp.where(lane32 < 128 * there, OMEGA / diag, 0.0)
        dgm[i], dm[i] = diag, inv
        m = inv * fm[i]
        around = neighbours(three(ks, i + 2), three(pks, i + 2), rows_strip)
        diag = ls[i] + 0.5 * (CALL * ks[i + 2] + around)
        keep = jnp.logical_or(place < (6 + 4 * has_right) * there, place >= 32 - (6 + 4 * has_left) * there)
        inv = jnp.where(keep, OMEGA / diag, 0.0)
        dgs[i], ds_[i] = diag, inv
        ready(field_a, i, m, inv * fs[i], True)

    loop(0, 12, first)

    def sweep(i):
        m = avm[i] + dm[i] * resid_main(field_a, i)
        s = avs[i] + ds_[i] * resid_strip(field_a, i)
        ready(field_b, i, m, s, False)

    loop(1, 11, sweep)

    def resid_pairs(i):
        pair = resid_main(field_b, 2 * i + 2) + resid_main(field_b, 2 * i + 3)
        tm[32 * i : 32 * i + 32, :] = pair

    loop(0, 4, resid_pairs)
    gg1[...] = (0.125 * dot(halve_rows(tm, 64), rm01)).reshape(4, 16, 128)

    def pack_sides1(arrays):
        left, right = jnp.zeros((8, 128), F32), jnp.zeros((8, 128), F32)
        for n, arr in enumerate(arrays):
            for x in range(4):
                for t in range(2):
                    slot = 8 * n + 2 * x + t
                    tile = arr[x, 8 * t : 8 * t + 8, :]
                    r = rot(tile, 4 * slot, 1)
                    left = jnp.where((lane >> 2) == slot, r, left)
                    right = jnp.where((lane >> 2) == (slot + 15) % 32, r, right)
        return left, right

    e1x = send_planes(gg1.at[0:2], gg1x.at[1], gg1.at[2:4], gg1x.at[0])
    pack1[0], pack1[1] = pack_sides1([own1, diag1, gg1[...]])
    e1s = send_sides(pack1, rs1)

    kk = k1l[...]
    for i in range(4):
        t1[16 * i : 16 * i + 16, :] = kk[2 * i] + kk[2 * i + 1]
    k2l = (0.125 * dot(halve_rows(t1, 32), r12)).reshape(4, 8, 128)
    for i in range(2):
        t1[16 * i : 16 * i + 16, :] = l1[2 * i] + l1[2 * i + 1]
    l2own = (0.125 * dot(halve_rows(t1, 16), r12)).reshape(2, 8, 128)
    half2 = 0.5 * 0.0625
    diag2 = l2own + half2 * (CALL * k2l[1:3] + ring_sum(k2l))
    both = (k2l[1], k2l[2], diag2[0], diag2[1])
    low = jnp.where(lane < 32, both[0], rot(both[1], 32, 1))
    high = jnp.where(lane < 96, rot(both[2], 64, 1), rot(both[3], 96, 1))
    kd2[...] = jnp.where(lane < 64, low, high)
    l2sum = rot(l2own[0] + l2own[1], 64, 1)
    ekd2 = send_far(kd2, kd2x)

    packv[0, 0], packv[1, 0] = pack_strips([bvs[x + 2] for x in range(8)])
    evx = [send(bvm.at[8], bvm.at[0], 1, 0), send(bvm.at[3], bvm.at[11], -1, 0)]
    evs = send_sides(packv, rsv)

    def fill1(ref, depth, own, x_ref, x_depth, shift, rs, n):
        merged = [jnp.where(group == n, rs[step, 0], rs[step, 1]) for step in range(3)]
        for p in range(4 + 2 * depth):
            x = p - depth
            for t in range(2):
                slot = 8 * n + 2 * (x % 4) + t
                side = rot(merged[(x + 4) // 4], 64 - 4 * slot, 1)
                rows = slice(8 * t, 8 * t + 8)
                if x < 0:
                    center = rot(x_ref[0, x + x_depth, rows, :], shift, 1)
                elif x > 3:
                    center = rot(x_ref[1, x - 4, rows, :], shift, 1)
                else:
                    center = own[x, rows, :]
                side = jnp.where(jnp.logical_or(lane < 68, lane >= 124), side, 0.0)
                ref[p, 8 * t : 8 * t + 8, :] = jnp.where(lane < 64, center, side)

    for c in ekd + e1x + e1s:
        c.arrived()
    fill1(k1, 3, own1, kd1x, 3, 0, rs1, 0)
    fill1(dg1, 2, diag1, kd1x, 3, 64, rs1, 1)
    fill1(f1, 2, gg1, gg1x, 2, 0, rs1, 2)
    k1_all = k1[...]
    k1_all = (k1_all,) + beside(k1_all, 2)

    lane1 = iota((2, 16, 128), 2)

    def inverse1(lo, hi, step):
        there = inside(step)
        keep = jnp.logical_or(lane1 < (64 + 4 * has_right) * there, lane1 >= 128 - 4 * has_left * there)
        return jnp.where(keep, OMEGA / dg1[lo:hi], 0.0)

    def sweep1(v, depth, inv):
        kk = cut_planes(k1_all, 3 - depth, 7 + depth)
        lo, hi = 3 - depth, 5 + depth
        rest = f1[lo:hi] - ring_apply(v, kk, dg1[lo:hi], half1)
        return v[1:-1] + inv[lo:hi] * rest

    inv1 = jnp.concatenate([inverse1(0, 2, -1), inverse1(2, 4, 0), inverse1(4, 6, 0), inverse1(6, 8, 1)], axis=0)
    v = sweep1(inv1 * f1[...], 2, inv1)
    r = f1[2:6] - ring_apply(v, cut_planes(k1_all, 2, 8), dg1[2:6], half1)
    for i in range(2):
        t1[16 * i : 16 * i + 16, :] = r[2 * i] + r[2 * i + 1]
    rhs2 = (0.125 * dot(halve_rows(t1, 16), r12)).reshape(2, 8, 128)

    gl2[...] = jnp.where(lane < 32, rhs2[0], jnp.where(lane < 64, rot(rhs2[1], 32, 1), l2sum))
    e2 = send_far(gl2, gl2x)
    vv1[...] = v[1:5]
    pv1[0], pv1[1] = pack_sides1([v[1:5]])
    ev1x = send_planes(vv1.at[0:3], vv1x.at[1], vv1.at[1:4], vv1x.at[0])
    ev1s = send_sides(pv1, rsv1)

    def around2(mine, ref, step):
        mid = mine if step == 4 else ref[step, 1]
        return mid, rot(ref[step, 2], 32, 1), rot(ref[step, 0], -32, 1)

    def near2(parts, n):
        mid, right, left = parts
        at = (lane - 32 * n) & 127
        side = jnp.where(at < 40, right, jnp.where(at >= 120, left, 0.0))
        return rot(jnp.where(at < 32, mid, side), -32 * n, 1)

    for c in ekd2:
        c.arrived()
    mine = kd2[...]
    for step in range(9):
        there = inside(step - 4)
        keep = jnp.logical_or(lane < (32 + 8 * has_right) * there, lane >= 128 - 8 * has_left * there)
        parts = around2(mine, kd2x, step)
        for x in range(2):
            k2[2 * step + x] = near2(parts, x)
            diag = near2(parts, 2 + x)
            dg2[2 * step + x] = diag
            t2[2 * step + x] = jnp.where(keep, OMEGA / diag, 0.0)

    def to_level3(pairs):
        n = len(pairs)
        for i, pair in enumerate(pairs):
            t1[8 * i : 8 * i + 8, :] = pair
        y = 0.125 * dot(halve_rows(t1, 4 * n), r23)
        for i in range(n):
            t3[i, 0:4, :] = y[4 * i : 4 * i + 4, :]
        return t3[0:n]

    k2_all = k2[...]
    k2_all = (k2_all,) + beside(k2_all, 2)
    t3[...] = jnp.zeros_like(t3)
    half3 = 0.5 * 0.015625
    k3 = to_level3([k2[2 * i] + k2[2 * i + 1] for i in range(9)])
    most3 = half3 * (CALL * k3[1:-1] + ring_sum(k3))

    for c in e2:
        c.arrived()
    mine = gl2[...]
    for step in range(9):
        parts = around2(mine, gl2x, step)
        for x in range(2):
            f2[2 * step + x] = near2(parts, x)
        l2[step] = near2(parts, 2)

    def sweep2(v, depth):
        lo, hi = 9 - depth, 9 + depth
        rest = f2[lo:hi] - ring_apply(v, cut_planes(k2_all, lo - 1, hi + 1), dg2[lo:hi], half2)
        return v[1:-1] + t2[lo:hi] * rest

    vb = sweep2(t2[...] * f2[...], 8)
    r = f2[2:16] - ring_apply(vb, cut_planes(k2_all, 1, 17), dg2[2:16], half2)
    l3 = to_level3([l2[i + 1] for i in range(7)])
    f3 = to_level3([r[2 * i] + r[2 * i + 1] for i in range(7)])
    diag3 = l3 + most3
    inv3 = []
    for i in range(7):
        there = inside(i - 3)
        keep = jnp.logical_or(lane < (16 + 4 * has_right) * there, lane >= 128 - 4 * has_left * there)
        inv3.append(jnp.where(jnp.logical_and(keep, row < 4), OMEGA / diag3[i], 0.0)[None])
    inv3 = jnp.concatenate(inv3, axis=0)
    v3 = inv3 * f3
    rest = f3[1:-1] - ring_apply(v3, cut_planes((k3,) + beside(k3, 2), 1, 8), diag3[1:-1], half3)
    v3 = v3[1:-1] + inv3[1:-1] * rest

    p32 = ring_map(cut(64), 64, True)
    wide3 = dot(v3.reshape(40, 128), p32)
    for i in range(5):
        double_rows(t1.at[8 * i : 8 * i + 8, :], wide3[8 * i : 8 * i + 4, :])
    e3 = t1[0:40, :].reshape(5, 8, 128)
    e3 = jnp.concatenate([e3[i // 2][None] for i in range(10)], axis=0)
    vb = vb[3:13] + e3
    vb = sweep2(vb, 4)
    vb = sweep2(vb, 3)

    for c in ev1x + ev1s:
        c.arrived()
    fill1(va1, 3, vv1, vv1x, 3, 0, rsv1, 0)
    p21 = ring_map(cut(96), 64, True)
    double_rows(tm.at[0:96, :], dot(vb.reshape(48, 128), p21))
    e2v = tm[0:96, :].reshape(6, 16, 128)
    inner = jnp.logical_or(lane < 68, lane >= 124)
    inner = jnp.concatenate([inner, inner], axis=0)
    v = [jnp.where(inner, va1[p] + e2v[(p - 3) // 2 + 2], 0.0)[None] for p in range(10)]
    v = sweep1(jnp.concatenate(v, axis=0), 3, inv1)
    v = sweep1(v, 2, inv1)

    e1 = v.reshape(96, 128)
    double_rows(tm.at[0:192, :], dot(e1, ring_map(main_z, 96, True)))
    double_rows(ts.at[0:192, :], dot(e1, ring_map(strip_z, 96, True)))
    for c in evx + evs:
        c.arrived()
        c.left()
    merged = halves(rsv, 0)
    for p in range(12):
        own = bvs[p] if 1 <= p < 11 else own_strip(bvm[p])
        bvs[p] = whole_strip(own, merged, p - 2)

    def correct(i):
        at = 32 * (i // 2)
        m = bvm[i] + tm[at : at + 32, :]
        s = ts[at : at + 8, :]
        for t in range(1, 4):
            s = jnp.where(group == t, ts[at + 8 * t : at + 8 * t + 8, :], s)
        s = jnp.where(used_lanes, bvs[i] + s, 0.0)
        ready(field_a, i, m, s, True)

    loop(0, 12, correct)
    loop(1, 11, sweep)

    def last(i):
        out_ref[i - 2] = bvm[i] + dm[i] * resid_main(field_b, i)

    loop(2, 10, last)
    for c in started:
        if not any(c is done for done in evx + evs):
            c.left()


def solution(mesh):
    nw, nz = mesh.shape["wide"], mesh.shape["narrow"]

    def on_device(source, permeability, leakage):
        def vm(*shape):
            return pltpu.VMEM(shape, F32)

        def pair(n):
            return [vm(n, 32, 128), vm(n, 8, 128)]

        scratch = pair(16) * 4 + pair(12) * 4 + pair(12) * 8 + [vm(256, 128), vm(256, 128)]
        scratch += [vm(2, 3, 8, 128), vm(3, 2, 3, 8, 128), vm(2, 1, 8, 128), vm(3, 2, 1, 8, 128)]
        scratch += [vm(4, 16, 128), vm(2, 3, 16, 128), vm(4, 16, 128), vm(2, 2, 16, 128)]
        scratch += [vm(2, 8, 128), vm(3, 2, 8, 128), vm(2, 8, 128), vm(3, 2, 8, 128)]
        scratch += [vm(4, 16, 128), vm(2, 3, 16, 128)]
        scratch += [vm(8, 16, 128), vm(10, 16, 128), vm(8, 16, 128), vm(8, 16, 128), vm(10, 16, 128), vm(128, 128)]
        scratch += [vm(8, 128), vm(9, 3, 8, 128), vm(8, 128), vm(9, 3, 8, 128)]
        scratch += [vm(18, 8, 128), vm(18, 8, 128), vm(18, 8, 128), vm(9, 8, 128), vm(18, 8, 128), vm(9, 8, 128)]
        n = 12 + 2 + 8 + 26 + 8 + 26 + 8
        scratch += [pltpu.SemaphoreType.DMA((3,)), pltpu.SemaphoreType.DMA((n,)), pltpu.SemaphoreType.DMA((n,))]

        def body(*refs):
            kernel(nw, nz, *refs)

        return pl.pallas_call(
            body,
            out_shape=jax.ShapeDtypeStruct(source.shape, F32),
            in_specs=[pl.BlockSpec(memory_space=pltpu.HBM)] * 3,
            out_specs=pl.BlockSpec(memory_space=pltpu.VMEM),
            scratch_shapes=scratch,
            compiler_params=pltpu.CompilerParams(
                collective_id=0, has_side_effects=True, vmem_limit_bytes=60 * 2**20
            ),
            name="vcycle",
        )(source, permeability, leakage)

    spec = P("wide", None, "narrow")
    return jax.shard_map(on_device, mesh=mesh, in_specs=(spec, spec, spec), out_specs=spec, check_vma=False)
```

```python
import jax
import jax.numpy as jnp
from jax import lax
from jax.experimental import pallas as pl
from jax.experimental.pallas import tpu as pltpu
from jax.sharding import PartitionSpec as P

MESH = pl.DeviceIdType.MESH
OMEGA = 0.8
F32 = jnp.float32


def weight(a, b, c):
    n = a + b + c
    return (a * 1.0 + b * 0.7 + c * 0.4) / n * {1: 1.0, 2: 0.25, 3: 0.1}[n]


CX, CY, CZ = weight(1, 0, 0), weight(0, 1, 0), weight(0, 0, 1)
CXY, CXZ, CYZ, CXYZ = weight(1, 1, 0), weight(1, 0, 1), weight(0, 1, 1), weight(1, 1, 1)
CALL = 2 * (CX + CY + CZ) + 4 * (CXY + CXZ + CYZ) + 8 * CXYZ

SIDES = [(a, b) for b in (-1, 1) for a in (-1, 0, 1)]
FAR = [(a, b) for a in range(-4, 5) for b in (-1, 0, 1) if (a, b) != (0, 0)]


def iota(shape, dim):
    return lax.broadcasted_iota(jnp.int32, shape, dim)


def lanes():
    return iota((8, 128), 1)


def rot(x, shift, axis):
    shift %= x.shape[axis]
    return x if shift == 0 else pltpu.roll(x, shift, axis)


def rows_beside(t):
    axis = t.ndim - 2
    n = t.shape[axis]
    row = iota(t.shape, axis)
    up = jnp.where(row == 0, 0.0, rot(t, 1, axis))
    down = jnp.where(row == n - 1, 0.0, rot(t, n - 1, axis))
    return up + down


def neighbours(u, p, y):
    x, xp = u[0] + u[2], p[0] + p[2]
    inner = CXY * x + CXYZ * xp + CY * u[1] + CYZ * p[1]
    return CX * x + CXZ * xp + CZ * p[1] + y(inner)


def beside_main(m, s):
    lane = iota(m.shape, 1)
    edge = jnp.where((iota(s.shape, 1) & 31) < 7, s, rot(s, -18, 1))
    edge = jnp.concatenate([rot(edge, 121 - 32 * t, 1) for t in range(4)], axis=0)
    return jnp.where(lane == 0, edge, rot(m, 1, 1)), jnp.where(lane == 127, edge, rot(m, 127, 1))


def beside(u, axis=1):
    return rot(u, 1, axis), rot(u, 127, axis)


def rows_strip(c):
    row, lane = iota((8, 128), 0), iota((8, 128), 1)
    up, down = rot(c, 1, 0), rot(c, 7, 0)
    up = jnp.where(row == 0, jnp.where(lane < 32, 0.0, rot(up, 32, 1)), up)
    down = jnp.where(row == 7, jnp.where(lane >= 96, 0.0, rot(down, 96, 1)), down)
    return up + down


def slabs(u):
    return u[:-2], u[1:-1], u[2:]


def ring_sum(u):
    below, above = beside(u, 2)
    return neighbours(slabs(u), slabs(below + above), rows_beside)


def ring_apply(v, k, diag, half):
    k, k_below, k_above = k
    below, above = beside(v, 2)
    s1 = neighbours(slabs(v), slabs(below + above), rows_beside)
    s2 = neighbours(slabs(k * v), slabs(k_below * below + k_above * above), rows_beside)
    return diag * v[1:-1] - half * (k[1:-1] * s1 + s2)


def cut_planes(k, lo, hi):
    return tuple(part[lo:hi] for part in k)


def dot(a, b):
    return lax.dot_general(a, b, (((1,), (0,)), ((), ())), precision=lax.Precision.HIGHEST, preferred_element_type=F32)


def ring_map(fine_of, coarse_cut, transpose=False):
    f_dim = 1 if transpose else 0
    i, j = iota((128, 128), f_dim), iota((128, 128), 1 - f_dim)
    return ((fine_of(i) >> 1) == jnp.where(j < coarse_cut, j, j - 128)).astype(F32)


def cut(c):
    return lambda i: jnp.where(i < c, i, i - 128)


def main_z(i):
    return i


def strip_z(i):
    r = i & 31
    return jnp.where(r < 16, r + 122, r - 26)


def strip_halo_z(i):
    r = i & 31
    return jnp.where(jnp.logical_or(r < 6, r >= 26), 4096, strip_z(i))


def halve_rows(ref, n):
    return ref[pl.ds(0, n, stride=2), :] + ref[pl.ds(1, n, stride=2), :]


def double_rows(ref, x):
    n = x.shape[0]
    ref[pl.ds(0, n, stride=2), :] = x
    ref[pl.ds(1, n, stride=2), :] = x


def kernel(
    nw, nz, f_hbm, k_hbm, l_hbm, out_ref,
    km, ks, pkm, pks, kbm, kbs, kam, kas, fm, fs, lm, ls, dgm, dgs, dm, ds_,
    avm, avs, apm, aps, aqm, aqs, arm, ars, bvm, bvs, bpm, bps, bqm, bqs, brm, brs, tm, ts,
    pack0, rs0, packv, rsv, kd1, kd1x, gg1, gg1x, pack1, rs1, pv1, rsv1, vv1, vv1x,
    k1l, k1, dg1, f1, va1, t1, kd2, kd2x, gl2, gl2x, k2, dg2, f2, l2, t2, t3, loc_sem, send_sem, recv_sem,
):
    w, z = lax.axis_index("wide"), lax.axis_index("narrow")

    def device(a, b):
        return (lax.rem(w + (a + nw), nw), lax.rem(z + (b + nz), nz))

    def in_grid(a, b):
        ok = jnp.logical_and(w + a >= 0, w + a < nw)
        return ok if b == 0 else jnp.logical_and(ok, jnp.logical_and(z + b >= 0, z + b < nz))

    has_left, has_right = (z > 0).astype(jnp.int32), (z < nz - 1).astype(jnp.int32)

    def inside(step):
        return jnp.logical_and(w + step >= 0, w + step < nw).astype(jnp.int32)

    class Message:
        def __init__(self, n, src, dst, a, b):
            self.to, self.origin = (a, b), (-a, -b)
            self.copy = pltpu.make_async_remote_copy(
                src_ref=src, dst_ref=dst, send_sem=send_sem.at[n], recv_sem=recv_sem.at[n],
                device_id=device(a, b), device_id_type=MESH,
            )
            pl.when(in_grid(*self.to))(self.copy.start)

        def arrived(self):
            pl.when(in_grid(*self.origin))(self.copy.wait_recv)

        def left(self):
            pl.when(in_grid(*self.to))(self.copy.wait_send)

    started = []

    def send(src, dst, a, b):
        started.append(Message(len(started), src, dst, a, b))
        return started[-1]

    def loop(lo, hi, body):
        for i in range(lo, hi):
            body(i)

    lane, row = lanes(), iota((8, 128), 0)
    group, place = lane >> 5, lane & 31

    for ref in (rs0, rsv, rs1, rsv1, kd1x, gg1x, vv1x, kd2x, gl2x):
        ref[...] = jnp.zeros_like(ref)

    def clear(k_planes, planes, v_plane):
        def body():
            km[k_planes] = jnp.zeros((4, 32, 128), F32)
            fm[planes] = jnp.zeros((2, 32, 128), F32)
            lm[planes] = jnp.zeros((2, 32, 128), F32)
            bvm[v_plane] = jnp.zeros((32, 128), F32)

        return body

    pl.when(w == 0)(clear(slice(0, 4), slice(0, 2), 0))
    pl.when(w == nw - 1)(clear(slice(12, 16), slice(10, 12), 11))

    barrier = pltpu.get_barrier_semaphore()

    def greet(a, b):
        def body():
            pl.semaphore_signal(barrier, inc=1, device_id=device(a, b), device_id_type=MESH)

        return body

    for a, b in FAR:
        pl.when(in_grid(a, b))(greet(a, b))
    loads = []
    for n, (src, dst) in enumerate(((k_hbm, km.at[4:12]), (f_hbm, fm.at[2:10]), (l_hbm, lm.at[2:10]))):
        loads.append(pltpu.make_async_copy(src, dst, loc_sem.at[n]))
        loads[-1].start()

    def own_strip(m):
        out = rot(m[0:8, :], 6, 1)
        for t in range(1, 4):
            out = jnp.where(group == t, rot(m[8 * t : 8 * t + 8, :], 32 * t + 6, 1), out)
        return jnp.where(place < 16, out, rot(out, 20, 1))

    def pack_strips(strips):
        left, right = jnp.zeros((8, 128), F32), jnp.zeros((8, 128), F32)
        for x, s in enumerate(strips):
            r = rot(s, 4 * x - 26, 1)
            left = jnp.where((place >> 2) == x, r, left)
            right = jnp.where((place >> 2) == (x + 2) % 8, r, right)
        return left, right

    def halves(rs, n):
        out = []
        for step in range(3):
            left, right = rs[step, 0, n], rot(rs[step, 1, n], 40, 1)
            out.append((jnp.where(place < 16, left, right), jnp.where(place < 16, right, left)))
        return out

    own_lanes = jnp.logical_or(place < 6, place >= 26)
    used_lanes = jnp.logical_or(place < 10, place >= 22)

    def whole_strip(own, merged, x):
        step, at = (x + 8) // 8, x % 8
        halo = rot(merged[step][at // 4], 6 - 4 * at, 1)
        return jnp.where(own_lanes, own, jnp.where(used_lanes, halo, 0.0))

    for n, (ref, strip, off) in enumerate(((km, ks, 4), (fm, fs, 2), (lm, ls, 2))):
        loads[n].wait()
        own = [own_strip(ref[x + off]) for x in range(8)]
        for x in range(8):
            strip[x + off] = own[x]
        pack0[0, n], pack0[1, n] = pack_strips(own)

    def count(pos, reach, size):
        return jnp.minimum(pos, reach) + 1 + jnp.minimum(size - 1 - pos, reach)

    pl.semaphore_wait(barrier, count(w, 4, nw) * count(z, 1, nz) - 1)

    def send_planes(src_lo, dst_hi, src_hi, dst_lo):
        return [send(src_hi, dst_lo, 1, 0), send(src_lo, dst_hi, -1, 0)]

    def send_sides(pack, rs):
        return [send(pack.at[0 if b < 0 else 1], rs.at[1 - a, 0 if b < 0 else 1], a, b) for a, b in SIDES]

    def send_far(src, dst):
        return [send(src, dst.at[4 - a, 1 - b], a, b) for a, b in FAR]

    e0k = send_planes(km.at[4:8], km.at[12:16], km.at[8:12], km.at[0:4])
    e0s = send_sides(pack0, rs0)
    e0f = send_planes(fm.at[2:4], fm.at[10:12], fm.at[8:10], fm.at[0:2])
    e0l = send_planes(lm.at[2:4], lm.at[10:12], lm.at[8:10], lm.at[0:2])

    rm01, rs01 = ring_map(main_z, 96), ring_map(strip_halo_z, 96)
    r12, r23 = ring_map(cut(96), 64), ring_map(cut(64), 64)

    for c in e0k + e0s:
        c.arrived()
    merged = halves(rs0, 0)
    for p in range(16):
        own = ks[p] if 4 <= p < 12 else own_strip(km[p])
        ks[p] = whole_strip(own, merged, p - 4)

    def k_lanes(i):
        for p in (2 * i, 2 * i + 1):
            m, s = km[p], ks[p]
            below, above = beside_main(m, s)
            kbm[p], kam[p], pkm[p] = below, above, below + above
            below, above = beside(s)
            kbs[p], kas[p], pks[p] = below, above, below + above
        tm[32 * i : 32 * i + 32, :] = km[2 * i] + km[2 * i + 1]
        pair = ks[2 * i] + ks[2 * i + 1]
        parts = [jnp.where(group == t, pair, 0.0) for t in range(4)]
        ts[32 * i : 32 * i + 32, :] = jnp.concatenate(parts, axis=0)

    loop(0, 8, k_lanes)

    coarse = dot(halve_rows(tm, 128), rm01) + dot(halve_rows(ts, 128), rs01)
    k1l[...] = (0.125 * coarse).reshape(8, 16, 128)

    def l_pairs(i):
        tm[32 * i : 32 * i + 32, :] = lm[2 * i + 2] + lm[2 * i + 3]

    loop(0, 4, l_pairs)
    l1 = (0.125 * dot(halve_rows(tm, 64), rm01)).reshape(4, 16, 128)
    own1 = k1l[2:6]
    half1 = 0.5 * 0.25
    diag1 = l1 + half1 * (CALL * own1 + ring_sum(k1l[1:7]))
    lane16 = iota((4, 16, 128), 2)
    kd1[...] = jnp.where(lane16 < 64, own1, rot(diag1, 64, 2))
    ekd = send_planes(kd1.at[0:3], kd1x.at[1], kd1.at[1:4], kd1x.at[0])

    for c in e0f + e0l:
        c.arrived()
    for n, (ref, strip) in ((1, (fm, fs)), (2, (lm, ls))):
        merged = halves(rs0, n)
        for p in range(12):
            own = strip[p] if 2 <= p < 10 else own_strip(ref[p])
            strip[p] = whole_strip(own, merged, p - 2)

    lane32 = iota((32, 128), 1)

    def three(ref, i):
        return ref[i - 1], ref[i], ref[i + 1]

    def ready(v, i, m, s, strips):
        vm, vs, pm, ps, qm, qs, rm, rs = v
        vm[i], vs[i] = m, s
        below, above = beside_main(m, s)
        pm[i], qm[i] = below + above, m * km[i + 2]
        rm[i] = below * kbm[i + 2] + above * kam[i + 2]
        if strips:
            below, above = beside(s)
            ps[i], qs[i] = below + above, s * ks[i + 2]
            rs[i] = below * kbs[i + 2] + above * kas[i + 2]

    field_a = (avm, avs, apm, aps, aqm, aqs, arm, ars)
    field_b = (bvm, bvs, bpm, bps, bqm, bqs, brm, brs)

    def resid_main(v, i):
        vm, vs, pm, ps, qm, qs, rm, rs = v
        s1 = neighbours(three(vm, i), three(pm, i), rows_beside)
        s2 = neighbours(three(qm, i), three(rm, i), rows_beside)
        return fm[i] - dgm[i] * vm[i] + 0.5 * (km[i + 2] * s1 + s2)

    def resid_strip(v, i):
        vm, vs, pm, ps, qm, qs, rm, rs = v
        s1 = neighbours(three(vs, i), three(ps, i), rows_strip)
        s2 = neighbours(three(qs, i), three(rs, i), rows_strip)
        return fs[i] - dgs[i] * vs[i] + 0.5 * (ks[i + 2] * s1 + s2)

    def first(i):
        there = inside(-1) if i < 2 else inside(1) if i >= 10 else 1
        around = neighbours(three(km, i + 2), three(pkm, i + 2), rows_beside)
        diag = lm[i] + 0.5 * (CALL * km[i + 2] + around)
        inv = jnp.where(lane32 < 128 * there, OMEGA / diag, 0.0)
        dgm[i], dm[i] = diag, inv
        m = inv * fm[i]
        around = neighbours(three(ks, i + 2), three(pks, i + 2), rows_strip)
        diag = ls[i] + 0.5 * (CALL * ks[i + 2] + around)
        keep = jnp.logical_or(place < (6 + 4 * has_right) * there, place >= 32 - (6 + 4 * has_left) * there)
        inv = jnp.where(keep, OMEGA / diag, 0.0)
        dgs[i], ds_[i] = diag, inv
        ready(field_a, i, m, inv * fs[i], True)

    loop(0, 12, first)

    def sweep(i):
        m = avm[i] + dm[i] * resid_main(field_a, i)
        s = avs[i] + ds_[i] * resid_strip(field_a, i)
        ready(field_b, i, m, s, False)

    loop(1, 11, sweep)

    def resid_pairs(i):
        pair = resid_main(field_b, 2 * i + 2) + resid_main(field_b, 2 * i + 3)
        tm[32 * i : 32 * i + 32, :] = pair

    loop(0, 4, resid_pairs)
    gg1[...] = (0.125 * dot(halve_rows(tm, 64), rm01)).reshape(4, 16, 128)

    def pack_sides1(arrays):
        left, right = jnp.zeros((8, 128), F32), jnp.zeros((8, 128), F32)
        for n, arr in enumerate(arrays):
            for x in range(4):
                for t in range(2):
                    slot = 8 * n + 2 * x + t
                    tile = arr[x, 8 * t : 8 * t + 8, :]
                    r = rot(tile, 4 * slot, 1)
                    left = jnp.where((lane >> 2) == slot, r, left)
                    right = jnp.where((lane >> 2) == (slot + 15) % 32, r, right)
        return left, right

    e1x = send_planes(gg1.at[0:2], gg1x.at[1], gg1.at[2:4], gg1x.at[0])
    pack1[0], pack1[1] = pack_sides1([own1, diag1, gg1[...]])
    e1s = send_sides(pack1, rs1)

    kk = k1l[...]
    for i in range(4):
        t1[16 * i : 16 * i + 16, :] = kk[2 * i] + kk[2 * i + 1]
    k2l = (0.125 * dot(halve_rows(t1, 32), r12)).reshape(4, 8, 128)
    for i in range(2):
        t1[16 * i : 16 * i + 16, :] = l1[2 * i] + l1[2 * i + 1]
    l2own = (0.125 * dot(halve_rows(t1, 16), r12)).reshape(2, 8, 128)
    half2 = 0.5 * 0.0625
    diag2 = l2own + half2 * (CALL * k2l[1:3] + ring_sum(k2l))
    both = (k2l[1], k2l[2], diag2[0], diag2[1])
    low = jnp.where(lane < 32, both[0], rot(both[1], 32, 1))
    high = jnp.where(lane < 96, rot(both[2], 64, 1), rot(both[3], 96, 1))
    kd2[...] = jnp.where(lane < 64, low, high)
    l2sum = rot(l2own[0] + l2own[1], 64, 1)
    ekd2 = send_far(kd2, kd2x)

    packv[0, 0], packv[1, 0] = pack_strips([bvs[x + 2] for x in range(8)])
    evx = [send(bvm.at[8], bvm.at[0], 1, 0), send(bvm.at[3], bvm.at[11], -1, 0)]
    evs = send_sides(packv, rsv)

    def fill1(ref, depth, own, x_ref, x_depth, shift, rs, n):
        merged = [jnp.where(group == n, rs[step, 0], rs[step, 1]) for step in range(3)]
        for p in range(4 + 2 * depth):
            x = p - depth
            for t in range(2):
                slot = 8 * n + 2 * (x % 4) + t
                side = rot(merged[(x + 4) // 4], 64 - 4 * slot, 1)
                rows = slice(8 * t, 8 * t + 8)
                if x < 0:
                    center = rot(x_ref[0, x + x_depth, rows, :], shift, 1)
                elif x > 3:
                    center = rot(x_ref[1, x - 4, rows, :], shift, 1)
                else:
                    center = own[x, rows, :]
                side = jnp.where(jnp.logical_or(lane < 68, lane >= 124), side, 0.0)
                ref[p, 8 * t : 8 * t + 8, :] = jnp.where(lane < 64, center, side)

    for c in ekd + e1x + e1s:
        c.arrived()
    fill1(k1, 3, own1, kd1x, 3, 0, rs1, 0)
    fill1(dg1, 2, diag1, kd1x, 3, 64, rs1, 1)
    fill1(f1, 2, gg1, gg1x, 2, 0, rs1, 2)
    k1_all = k1[...]
    k1_all = (k1_all,) + beside(k1_all, 2)

    lane1 = iota((2, 16, 128), 2)

    def inverse1(lo, hi, step):
        there = inside(step)
        keep = jnp.logical_or(lane1 < (64 + 4 * has_right) * there, lane1 >= 128 - 4 * has_left * there)
        return jnp.where(keep, OMEGA / dg1[lo:hi], 0.0)

    def sweep1(v, depth, inv):
        kk = cut_planes(k1_all, 3 - depth, 7 + depth)
        lo, hi = 3 - depth, 5 + depth
        rest = f1[lo:hi] - ring_apply(v, kk, dg1[lo:hi], half1)
        return v[1:-1] + inv[lo:hi] * rest

    inv1 = jnp.concatenate([inverse1(0, 2, -1), inverse1(2, 4, 0), inverse1(4, 6, 0), inverse1(6, 8, 1)], axis=0)
    v = sweep1(inv1 * f1[...], 2, inv1)
    r = f1[2:6] - ring_apply(v, cut_planes(k1_all, 2, 8), dg1[2:6], half1)
    for i in range(2):
        t1[16 * i : 16 * i + 16, :] = r[2 * i] + r[2 * i + 1]
    rhs2 = (0.125 * dot(halve_rows(t1, 16), r12)).reshape(2, 8, 128)

    gl2[...] = jnp.where(lane < 32, rhs2[0], jnp.where(lane < 64, rot(rhs2[1], 32, 1), l2sum))
    e2 = send_far(gl2, gl2x)
    vv1[...] = v[1:5]
    pv1[0], pv1[1] = pack_sides1([v[1:5]])
    ev1x = send_planes(vv1.at[0:3], vv1x.at[1], vv1.at[1:4], vv1x.at[0])
    ev1s = send_sides(pv1, rsv1)

    def around2(mine, ref, step):
        mid = mine if step == 4 else ref[step, 1]
        return mid, rot(ref[step, 2], 32, 1), rot(ref[step, 0], -32, 1)

    def near2(parts, n):
        mid, right, left = parts
        at = (lane - 32 * n) & 127
        side = jnp.where(at < 40, right, jnp.where(at >= 120, left, 0.0))
        return rot(jnp.where(at < 32, mid, side), -32 * n, 1)

    for c in ekd2:
        c.arrived()
    mine = kd2[...]
    for step in range(9):
        there = inside(step - 4)
        keep = jnp.logical_or(lane < (32 + 8 * has_right) * there, lane >= 128 - 8 * has_left * there)
        parts = around2(mine, kd2x, step)
        for x in range(2):
            k2[2 * step + x] = near2(parts, x)
            diag = near2(parts, 2 + x)
            dg2[2 * step + x] = diag
            t2[2 * step + x] = jnp.where(keep, OMEGA / diag, 0.0)

    def to_level3(pairs):
        n = len(pairs)
        for i, pair in enumerate(pairs):
            t1[8 * i : 8 * i + 8, :] = pair
        y = 0.125 * dot(halve_rows(t1, 4 * n), r23)
        for i in range(n):
            t3[i, 0:4, :] = y[4 * i : 4 * i + 4, :]
        return t3[0:n]

    k2_all = k2[...]
    k2_all = (k2_all,) + beside(k2_all, 2)
    t3[...] = jnp.zeros_like(t3)
    half3 = 0.5 * 0.015625
    k3 = to_level3([k2[2 * i] + k2[2 * i + 1] for i in range(9)])
    most3 = half3 * (CALL * k3[1:-1] + ring_sum(k3))

    for c in e2:
        c.arrived()
    mine = gl2[...]
    for step in range(9):
        parts = around2(mine, gl2x, step)
        for x in range(2):
            f2[2 * step + x] = near2(parts, x)
        l2[step] = near2(parts, 2)

    def sweep2(v, depth):
        lo, hi = 9 - depth, 9 + depth
        rest = f2[lo:hi] - ring_apply(v, cut_planes(k2_all, lo - 1, hi + 1), dg2[lo:hi], half2)
        return v[1:-1] + t2[lo:hi] * rest

    vb = sweep2(t2[...] * f2[...], 8)
    r = f2[2:16] - ring_apply(vb, cut_planes(k2_all, 1, 17), dg2[2:16], half2)
    l3 = to_level3([l2[i + 1] for i in range(7)])
    f3 = to_level3([r[2 * i] + r[2 * i + 1] for i in range(7)])
    diag3 = l3 + most3
    inv3 = []
    for i in range(7):
        there = inside(i - 3)
        keep = jnp.logical_or(lane < (16 + 4 * has_right) * there, lane >= 128 - 4 * has_left * there)
        inv3.append(jnp.where(jnp.logical_and(keep, row < 4), OMEGA / diag3[i], 0.0)[None])
    inv3 = jnp.concatenate(inv3, axis=0)
    v3 = inv3 * f3
    rest = f3[1:-1] - ring_apply(v3, cut_planes((k3,) + beside(k3, 2), 1, 8), diag3[1:-1], half3)
    v3 = v3[1:-1] + inv3[1:-1] * rest

    p32 = ring_map(cut(64), 64, True)
    wide3 = dot(v3.reshape(40, 128), p32)
    for i in range(5):
        double_rows(t1.at[8 * i : 8 * i + 8, :], wide3[8 * i : 8 * i + 4, :])
    e3 = t1[0:40, :].reshape(5, 8, 128)
    e3 = jnp.concatenate([e3[i // 2][None] for i in range(10)], axis=0)
    vb = vb[3:13] + e3
    vb = sweep2(vb, 4)
    vb = sweep2(vb, 3)

    for c in ev1x + ev1s:
        c.arrived()
    fill1(va1, 3, vv1, vv1x, 3, 0, rsv1, 0)
    p21 = ring_map(cut(96), 64, True)
    double_rows(tm.at[0:96, :], dot(vb.reshape(48, 128), p21))
    e2v = tm[0:96, :].reshape(6, 16, 128)
    inner = jnp.logical_or(lane < 68, lane >= 124)
    inner = jnp.concatenate([inner, inner], axis=0)
    v = [jnp.where(inner, va1[p] + e2v[(p - 3) // 2 + 2], 0.0)[None] for p in range(10)]
    v = sweep1(jnp.concatenate(v, axis=0), 3, inv1)
    v = sweep1(v, 2, inv1)

    e1 = v.reshape(96, 128)
    double_rows(tm.at[0:192, :], dot(e1, ring_map(main_z, 96, True)))
    double_rows(ts.at[0:192, :], dot(e1, ring_map(strip_z, 96, True)))
    for c in evx + evs:
        c.arrived()
        c.left()
    merged = halves(rsv, 0)
    for p in range(12):
        own = bvs[p] if 1 <= p < 11 else own_strip(bvm[p])
        bvs[p] = whole_strip(own, merged, p - 2)

    def correct(i):
        at = 32 * (i // 2)
        m = bvm[i] + tm[at : at + 32, :]
        s = ts[at : at + 8, :]
        for t in range(1, 4):
            s = jnp.where(group == t, ts[at + 8 * t : at + 8 * t + 8, :], s)
        s = jnp.where(used_lanes, bvs[i] + s, 0.0)
        ready(field_a, i, m, s, True)

    loop(0, 12, correct)
    loop(1, 11, sweep)

    def last(i):
        out_ref[i - 2] = bvm[i] + dm[i] * resid_main(field_b, i)

    loop(2, 10, last)
    for c in started:
        if not any(c is done for done in evx + evs):
            c.left()


def solution(mesh):
    nw, nz = mesh.shape["wide"], mesh.shape["narrow"]

    def on_device(source, permeability, leakage):
        def vm(*shape):
            return pltpu.VMEM(shape, F32)

        def pair(n):
            return [vm(n, 32, 128), vm(n, 8, 128)]

        scratch = pair(16) * 4 + pair(12) * 4 + pair(12) * 8 + [vm(256, 128), vm(256, 128)]
        scratch += [vm(2, 3, 8, 128), vm(3, 2, 3, 8, 128), vm(2, 1, 8, 128), vm(3, 2, 1, 8, 128)]
        scratch += [vm(4, 16, 128), vm(2, 3, 16, 128), vm(4, 16, 128), vm(2, 2, 16, 128)]
        scratch += [vm(2, 8, 128), vm(3, 2, 8, 128), vm(2, 8, 128), vm(3, 2, 8, 128)]
        scratch += [vm(4, 16, 128), vm(2, 3, 16, 128)]
        scratch += [vm(8, 16, 128), vm(10, 16, 128), vm(8, 16, 128), vm(8, 16, 128), vm(10, 16, 128), vm(128, 128)]
        scratch += [vm(8, 128), vm(9, 3, 8, 128), vm(8, 128), vm(9, 3, 8, 128)]
        scratch += [vm(18, 8, 128), vm(18, 8, 128), vm(18, 8, 128), vm(9, 8, 128), vm(18, 8, 128), vm(9, 8, 128)]
        n = 12 + 2 + 8 + 26 + 8 + 26 + 8
        scratch += [pltpu.SemaphoreType.DMA((3,)), pltpu.SemaphoreType.DMA((n,)), pltpu.SemaphoreType.DMA((n,))]

        def body(*refs):
            kernel(nw, nz, *refs)

        return pl.pallas_call(
            body,
            out_shape=pltpu.VMEM(source.shape, F32),
            in_specs=[pl.BlockSpec(memory_space=pltpu.HBM)] * 3,
            out_specs=pl.BlockSpec(memory_space=pltpu.VMEM),
            scratch_shapes=scratch,
            compiler_params=pltpu.CompilerParams(
                collective_id=0, has_side_effects=True, vmem_limit_bytes=60 * 2**20
            ),
            name="vcycle",
        )(source, permeability, leakage)

    spec = P("wide", None, "narrow")
    return jax.shard_map(on_device, mesh=mesh, in_specs=(spec, spec, spec), out_specs=spec, check_vma=False)
```

```python
import jax
import jax.numpy as jnp
from jax import lax
from jax.experimental import pallas as pl
from jax.experimental.pallas import tpu as pltpu
from jax.sharding import PartitionSpec as P

MESH = pl.DeviceIdType.MESH
OMEGA = 0.8
F32 = jnp.float32


def weight(a, b, c):
    n = a + b + c
    return (a * 1.0 + b * 0.7 + c * 0.4) / n * {1: 1.0, 2: 0.25, 3: 0.1}[n]


CX, CY, CZ = weight(1, 0, 0), weight(0, 1, 0), weight(0, 0, 1)
CXY, CXZ, CYZ, CXYZ = weight(1, 1, 0), weight(1, 0, 1), weight(0, 1, 1), weight(1, 1, 1)
CALL = 2 * (CX + CY + CZ) + 4 * (CXY + CXZ + CYZ) + 8 * CXYZ

SIDES = [(a, b) for b in (-1, 1) for a in (-1, 0, 1)]
FAR = [(a, b) for a in range(-4, 5) for b in (-1, 0, 1) if (a, b) != (0, 0)]


def iota(shape, dim):
    return lax.broadcasted_iota(jnp.int32, shape, dim)


def lanes():
    return iota((8, 128), 1)


def rot(x, shift, axis):
    shift %= x.shape[axis]
    return x if shift == 0 else pltpu.roll(x, shift, axis)


def rows_beside(t):
    axis = t.ndim - 2
    n = t.shape[axis]
    row = iota(t.shape, axis)
    up = jnp.where(row == 0, 0.0, rot(t, 1, axis))
    down = jnp.where(row == n - 1, 0.0, rot(t, n - 1, axis))
    return up + down


def neighbours(u, p, y):
    x, xp = u[0] + u[2], p[0] + p[2]
    inner = CXY * x + CXYZ * xp + CY * u[1] + CYZ * p[1]
    return CX * x + CXZ * xp + CZ * p[1] + y(inner)


def beside_main(m, s):
    lane = iota(m.shape, 1)
    edge = jnp.where((iota(s.shape, 1) & 31) < 9, s, rot(s, -14, 1))
    edge = jnp.concatenate([rot(edge, 119 - 32 * t, 1) for t in range(4)], axis=0)
    return jnp.where(lane == 0, edge, rot(m, 1, 1)), jnp.where(lane == 127, edge, rot(m, 127, 1))


def beside(u, axis=1):
    return rot(u, 1, axis), rot(u, 127, axis)


def rows_strip(c):
    row, lane = iota((8, 128), 0), iota((8, 128), 1)
    up, down = rot(c, 1, 0), rot(c, 7, 0)
    up = jnp.where(row == 0, jnp.where(lane < 32, 0.0, rot(up, 32, 1)), up)
    down = jnp.where(row == 7, jnp.where(lane >= 96, 0.0, rot(down, 96, 1)), down)
    return up + down


def slabs(u):
    return u[:-2], u[1:-1], u[2:]


def ring_sum(u):
    below, above = beside(u, 2)
    return neighbours(slabs(u), slabs(below + above), rows_beside)


def ring_apply(v, k, diag, half):
    k, k_below, k_above = k
    below, above = beside(v, 2)
    s1 = neighbours(slabs(v), slabs(below + above), rows_beside)
    s2 = neighbours(slabs(k * v), slabs(k_below * below + k_above * above), rows_beside)
    return diag * v[1:-1] - half * (k[1:-1] * s1 + s2)


def cut_planes(k, lo, hi):
    return tuple(part[lo:hi] for part in k)


def dot(a, b):
    return lax.dot_general(a, b, (((1,), (0,)), ((), ())), precision=lax.Precision.HIGHEST, preferred_element_type=F32)


def ring_map(fine_of, coarse_cut, transpose=False):
    f_dim = 1 if transpose else 0
    i, j = iota((128, 128), f_dim), iota((128, 128), 1 - f_dim)
    return ((fine_of(i) >> 1) == jnp.where(j < coarse_cut, j, j - 128)).astype(F32)


def cut(c):
    return lambda i: jnp.where(i < c, i, i - 128)


def main_z(i):
    return i


def strip_z(i):
    r = i & 31
    return jnp.where(r < 16, r + 120, r - 24)


def strip_halo_z(i):
    r = i & 31
    return jnp.where(jnp.logical_or(r < 8, r >= 24), 4096, strip_z(i))


def halve_rows(ref, n):
    return ref[pl.ds(0, n, stride=2), :] + ref[pl.ds(1, n, stride=2), :]


def double_rows(ref, x):
    n = x.shape[0]
    ref[pl.ds(0, n, stride=2), :] = x
    ref[pl.ds(1, n, stride=2), :] = x


def kernel(
    nw, nz, f_hbm, k_hbm, l_hbm, out_ref,
    km, ks, pkm, pks, kbm, kbs, kam, kas, fm, fs, lm, ls, dgm, dgs, dm, ds_,
    avm, avs, apm, aps, aqm, aqs, arm, ars, bvm, bvs, bpm, bps, bqm, bqs, brm, brs, tm, ts,
    pack0, rs0, kd1, kd1x, gg1, gg1x, pv1, rsv1, vv1, vv1x,
    k1l, k1, dg1, f1, va1, t1, kd2, kd2x, gl2, gl2x, k2, dg2, f2, l2, t2, t3, loc_sem, send_sem, recv_sem,
):
    w, z = lax.axis_index("wide"), lax.axis_index("narrow")

    def device(a, b):
        return (lax.rem(w + (a + nw), nw), lax.rem(z + (b + nz), nz))

    def in_grid(a, b):
        ok = jnp.logical_and(w + a >= 0, w + a < nw)
        return ok if b == 0 else jnp.logical_and(ok, jnp.logical_and(z + b >= 0, z + b < nz))

    has_left, has_right = (z > 0).astype(jnp.int32), (z < nz - 1).astype(jnp.int32)

    def inside(step):
        return jnp.logical_and(w + step >= 0, w + step < nw).astype(jnp.int32)

    class Message:
        def __init__(self, n, src, dst, a, b):
            self.to, self.origin = (a, b), (-a, -b)
            self.copy = pltpu.make_async_remote_copy(
                src_ref=src, dst_ref=dst, send_sem=send_sem.at[n], recv_sem=recv_sem.at[n],
                device_id=device(a, b), device_id_type=MESH,
            )
            pl.when(in_grid(*self.to))(self.copy.start)

        def arrived(self):
            pl.when(in_grid(*self.origin))(self.copy.wait_recv)

        def left(self):
            pl.when(in_grid(*self.to))(self.copy.wait_send)

    started = []

    def send(src, dst, a, b):
        started.append(Message(len(started), src, dst, a, b))
        return started[-1]

    def loop(lo, hi, body):
        for i in range(lo, hi):
            body(i)

    lane, row = lanes(), iota((8, 128), 0)
    group, place = lane >> 5, lane & 31

    for ref in (rs0, rsv1, kd1x, gg1x, vv1x, kd2x, gl2x):
        ref[...] = jnp.zeros_like(ref)

    def clear(k_planes, planes, v_plane):
        def body():
            km[k_planes] = jnp.zeros((4, 32, 128), F32)
            fm[planes] = jnp.zeros((2, 32, 128), F32)
            lm[planes] = jnp.zeros((2, 32, 128), F32)
            bvm[v_plane] = jnp.zeros((32, 128), F32)
            bvs[v_plane] = jnp.zeros((8, 128), F32)

        return body

    pl.when(w == 0)(clear(slice(0, 4), slice(0, 2), 0))
    pl.when(w == nw - 1)(clear(slice(12, 16), slice(10, 12), 11))

    barrier = pltpu.get_barrier_semaphore()

    def greet(a, b):
        def body():
            pl.semaphore_signal(barrier, inc=1, device_id=device(a, b), device_id_type=MESH)

        return body

    for a, b in FAR:
        pl.when(in_grid(a, b))(greet(a, b))
    loads = []
    for n, (src, dst) in enumerate(((k_hbm, km.at[4:12]), (f_hbm, fm.at[2:10]), (l_hbm, lm.at[2:10]))):
        loads.append(pltpu.make_async_copy(src, dst, loc_sem.at[n]))
        loads[-1].start()

    def own_strip(m):
        out = rot(m[0:8, :], 8, 1)
        for t in range(1, 4):
            out = jnp.where(group == t, rot(m[8 * t : 8 * t + 8, :], 32 * t + 8, 1), out)
        return jnp.where(place < 16, out, rot(out, 16, 1))

    eighth = place >> 3
    even = (eighth & 1) == 0
    spot = (0, 16, 8, 24)

    def pack_strips(strips):
        left, right = jnp.zeros((8, 128), F32), jnp.zeros((8, 128), F32)
        for x, s in enumerate(strips):
            r = rot(s, spot[x] - 24, 1)
            left = jnp.where(eighth == spot[x] // 8, r, left)
            right = jnp.where(eighth == (spot[x] // 8 + 1) % 4, r, right)
        return left, rot(right, 32, 1)

    def merge(rs, n):
        out = {}
        for step, half in ((0, 1), (1, 0), (1, 1), (2, 0)):
            left, right = rs[step, 0, half, n], rs[step, 1, half, n]
            out[step, half] = (jnp.where(even, left, right), jnp.where(even, right, left))
        return out

    own_lanes = jnp.logical_or(place < 8, place >= 24)

    def whole_strip(own, merged, x):
        at = x % 8
        halo = merged[(x + 8) // 8, at // 4][at % 4 // 2]
        return jnp.where(own_lanes, own, rot(halo, 8 - spot[at % 4], 1))

    for n, (ref, strip, off) in enumerate(((km, ks, 4), (fm, fs, 2), (lm, ls, 2))):
        loads[n].wait()
        own = [own_strip(ref[x + off]) for x in range(8)]
        for x in range(8):
            strip[x + off] = own[x]
        for half in range(2):
            pack0[0, half, n], pack0[1, half, n] = pack_strips(own[4 * half : 4 * half + 4])

    def count(pos, reach, size):
        return jnp.minimum(pos, reach) + 1 + jnp.minimum(size - 1 - pos, reach)

    pl.semaphore_wait(barrier, count(w, 4, nw) * count(z, 1, nz) - 1)

    def send_planes(src_lo, dst_hi, src_hi, dst_lo):
        return [send(src_hi, dst_lo, 1, 0), send(src_lo, dst_hi, -1, 0)]

    def send_sides(pack, rs):
        return [send(pack.at[0 if b < 0 else 1], rs.at[1 - a, 0 if b < 0 else 1], a, b) for a, b in SIDES]

    def send_far(src, dst):
        return [send(src, dst.at[4 - a, 1 - b], a, b) for a, b in FAR]

    e0k = send_planes(km.at[4:8], km.at[12:16], km.at[8:12], km.at[0:4])
    e0s = []
    for a, b in SIDES:
        side = 0 if b < 0 else 1
        if a == 0:
            e0s.append(send(pack0.at[side], rs0.at[1, side], a, b))
        else:
            half = 0 if a < 0 else 1
            e0s.append(send(pack0.at[side, half], rs0.at[1 - a, side, half], a, b))
    e0f = send_planes(fm.at[2:4], fm.at[10:12], fm.at[8:10], fm.at[0:2])
    e0l = send_planes(lm.at[2:4], lm.at[10:12], lm.at[8:10], lm.at[0:2])

    rm01, rs01 = ring_map(main_z, 96), ring_map(strip_halo_z, 96)
    r12, r23 = ring_map(cut(96), 64), ring_map(cut(64), 64)

    for c in e0k + e0s:
        c.arrived()
    merged = merge(rs0, 0)
    for p in range(16):
        own = ks[p] if 4 <= p < 12 else own_strip(km[p])
        ks[p] = whole_strip(own, merged, p - 4)

    def spread(strip):
        return jnp.concatenate([jnp.where(group == t, strip, 0.0) for t in range(4)], axis=0)

    def k_lanes(i):
        for p in (2 * i, 2 * i + 1):
            m, s = km[p], ks[p]
            below, above = beside_main(m, s)
            kbm[p], kam[p], pkm[p] = below, above, below + above
            below, above = beside(s)
            kbs[p], kas[p], pks[p] = below, above, below + above
        tm[32 * i : 32 * i + 32, :] = km[2 * i] + km[2 * i + 1]
        ts[32 * i : 32 * i + 32, :] = spread(ks[2 * i] + ks[2 * i + 1])

    loop(0, 8, k_lanes)

    coarse = dot(halve_rows(tm, 128), rm01) + dot(halve_rows(ts, 128), rs01)
    k1l[...] = (0.125 * coarse).reshape(8, 16, 128)

    for c in e0f + e0l:
        c.arrived()
    for n, (ref, strip) in ((1, (fm, fs)), (2, (lm, ls))):
        merged = merge(rs0, n)
        for p in range(12):
            own = strip[p] if 2 <= p < 10 else own_strip(ref[p])
            strip[p] = whole_strip(own, merged, p - 2)

    def l_pairs(i):
        tm[32 * i : 32 * i + 32, :] = lm[2 * i + 2] + lm[2 * i + 3]
        ts[32 * i : 32 * i + 32, :] = spread(ls[2 * i + 2] + ls[2 * i + 3])

    loop(0, 4, l_pairs)
    l1 = dot(halve_rows(tm, 64), rm01) + dot(halve_rows(ts, 64), rs01)
    l1 = (0.125 * l1).reshape(4, 16, 128)
    own1 = k1l[2:6]
    half1 = 0.5 * 0.25
    diag1 = l1 + half1 * (CALL * own1 + ring_sum(k1l[1:7]))
    kd1[:, 0], kd1[:, 1] = own1, diag1
    ekd = send_planes(kd1.at[0:3], kd1x.at[1], kd1.at[1:4], kd1x.at[0])

    lane32 = iota((32, 128), 1)

    def three(ref, i):
        return ref[i - 1], ref[i], ref[i + 1]

    def ready(v, i, m, s, strips):
        vm, vs, pm, ps, qm, qs, rm, rs = v
        vm[i], vs[i] = m, s
        below, above = beside_main(m, s)
        pm[i], qm[i] = below + above, m * km[i + 2]
        rm[i] = below * kbm[i + 2] + above * kam[i + 2]
        if strips:
            below, above = beside(s)
            ps[i], qs[i] = below + above, s * ks[i + 2]
            rs[i] = below * kbs[i + 2] + above * kas[i + 2]

    field_a = (avm, avs, apm, aps, aqm, aqs, arm, ars)
    field_b = (bvm, bvs, bpm, bps, bqm, bqs, brm, brs)

    def resid_main(v, i):
        vm, vs, pm, ps, qm, qs, rm, rs = v
        s1 = neighbours(three(vm, i), three(pm, i), rows_beside)
        s2 = neighbours(three(qm, i), three(rm, i), rows_beside)
        return fm[i] - dgm[i] * vm[i] + 0.5 * (km[i + 2] * s1 + s2)

    def resid_strip(v, i):
        vm, vs, pm, ps, qm, qs, rm, rs = v
        s1 = neighbours(three(vs, i), three(ps, i), rows_strip)
        s2 = neighbours(three(qs, i), three(rs, i), rows_strip)
        return fs[i] - dgs[i] * vs[i] + 0.5 * (ks[i + 2] * s1 + s2)

    def first(i):
        there = inside(-1) if i < 2 else inside(1) if i >= 10 else 1
        around = neighbours(three(km, i + 2), three(pkm, i + 2), rows_beside)
        diag = lm[i] + 0.5 * (CALL * km[i + 2] + around)
        inv = jnp.where(lane32 < 128 * there, OMEGA / diag, 0.0)
        dgm[i], dm[i] = diag, inv
        m = inv * fm[i]
        around = neighbours(three(ks, i + 2), three(pks, i + 2), rows_strip)
        diag = ls[i] + 0.5 * (CALL * ks[i + 2] + around)
        keep = jnp.logical_or(place < (8 + 8 * has_right) * there, place >= 32 - (8 + 8 * has_left) * there)
        inv = jnp.where(keep, OMEGA / diag, 0.0)
        dgs[i], ds_[i] = diag, inv
        ready(field_a, i, m, inv * fs[i], True)

    loop(0, 12, first)

    def sweep(i, strips):
        m = avm[i] + dm[i] * resid_main(field_a, i)
        s = avs[i] + ds_[i] * resid_strip(field_a, i)
        ready(field_b, i, m, s, strips)

    loop(1, 11, lambda i: sweep(i, True))

    def resid_pairs(i):
        pair = resid_main(field_b, 2 * i + 2) + resid_main(field_b, 2 * i + 3)
        tm[32 * i : 32 * i + 32, :] = pair
        pair = resid_strip(field_b, 2 * i + 2) + resid_strip(field_b, 2 * i + 3)
        ts[32 * i : 32 * i + 32, :] = spread(pair)

    loop(0, 4, resid_pairs)
    rhs1 = dot(halve_rows(tm, 64), rm01) + dot(halve_rows(ts, 64), rs01)
    gg1[...] = (0.125 * rhs1).reshape(4, 16, 128)

    e1x = send_planes(gg1.at[0:2], gg1x.at[1], gg1.at[2:4], gg1x.at[0])

    kk = k1l[...]
    for i in range(4):
        t1[16 * i : 16 * i + 16, :] = kk[2 * i] + kk[2 * i + 1]
    k2l = (0.125 * dot(halve_rows(t1, 32), r12)).reshape(4, 8, 128)
    for i in range(2):
        t1[16 * i : 16 * i + 16, :] = l1[2 * i] + l1[2 * i + 1]
    l2own = (0.125 * dot(halve_rows(t1, 16), r12)).reshape(2, 8, 128)
    half2 = 0.5 * 0.0625
    diag2 = l2own + half2 * (CALL * k2l[1:3] + ring_sum(k2l))
    both = (k2l[1], k2l[2], diag2[0], diag2[1])
    low = jnp.where(lane < 32, both[0], rot(both[1], 32, 1))
    high = jnp.where(lane < 96, rot(both[2], 64, 1), rot(both[3], 96, 1))
    kd2[...] = jnp.where(lane < 64, low, high)
    l2sum = rot(l2own[0] + l2own[1], 64, 1)
    ekd2 = send_far(kd2, kd2x)

    evx = []
    for ref in (bvm, bvs):
        evx += [send(ref.at[8], ref.at[0], 1, 0), send(ref.at[3], ref.at[11], -1, 0)]

    def pack_sides1(arr):
        left, right = jnp.zeros((8, 128), F32), jnp.zeros((8, 128), F32)
        for x in range(4):
            for t in range(2):
                slot = 2 * x + t
                r = rot(arr[x, 8 * t : 8 * t + 8, :], 4 * slot, 1)
                left = jnp.where((lane >> 2) == slot, r, left)
                right = jnp.where((lane >> 2) == slot + 15, r, right)
        return left, right

    def fill1(ref, own, x_ref, rs):
        merged = [jnp.where(group == 0, rs[step, 0], rs[step, 1]) for step in range(3)]
        for p in range(10):
            x = p - 3
            for t in range(2):
                side = rot(merged[(x + 4) // 4], 64 - 4 * (2 * (x % 4) + t), 1)
                side = jnp.where(jnp.logical_or(lane < 68, lane >= 124), side, 0.0)
                rows = slice(8 * t, 8 * t + 8)
                center = x_ref[0, x + 3, rows, :] if x < 0 else x_ref[1, x - 4, rows, :] if x > 3 else own[x, rows, :]
                ref[p, 8 * t : 8 * t + 8, :] = jnp.where(lane < 64, center, side)

    for c in ekd + e1x:
        c.arrived()
    k1[0:3], k1[3:7], k1[7:10] = kd1x[0, :, 0], own1, kd1x[1, :, 0]
    dg1[0:2], dg1[2:6], dg1[6:8] = kd1x[0, 1:3, 1], diag1, kd1x[1, 0:2, 1]
    f1[0:2], f1[2:6], f1[6:8] = gg1x[0], gg1[...], gg1x[1]
    k1_all = k1[...]
    k1_all = (k1_all,) + beside(k1_all, 2)

    lane1 = iota((2, 16, 128), 2)

    def inverse1(lo, hi, step):
        there = inside(step)
        keep = jnp.logical_or(lane1 < (64 + 4 * has_right) * there, lane1 >= 128 - 4 * has_left * there)
        return jnp.where(keep, OMEGA / dg1[lo:hi], 0.0)

    def sweep1(v, depth, inv):
        kk = cut_planes(k1_all, 3 - depth, 7 + depth)
        lo, hi = 3 - depth, 5 + depth
        rest = f1[lo:hi] - ring_apply(v, kk, dg1[lo:hi], half1)
        return v[1:-1] + inv[lo:hi] * rest

    inv1 = jnp.concatenate([inverse1(0, 2, -1), inverse1(2, 4, 0), inverse1(4, 6, 0), inverse1(6, 8, 1)], axis=0)
    v = sweep1(inv1 * f1[...], 2, inv1)
    r = f1[2:6] - ring_apply(v, cut_planes(k1_all, 2, 8), dg1[2:6], half1)
    for i in range(2):
        t1[16 * i : 16 * i + 16, :] = r[2 * i] + r[2 * i + 1]
    rhs2 = (0.125 * dot(halve_rows(t1, 16), r12)).reshape(2, 8, 128)

    gl2[...] = jnp.where(lane < 32, rhs2[0], jnp.where(lane < 64, rot(rhs2[1], 32, 1), l2sum))
    e2 = send_far(gl2, gl2x)
    vv1[...] = v[1:5]
    pv1[0], pv1[1] = pack_sides1(v[1:5])
    ev1x = send_planes(vv1.at[0:3], vv1x.at[1], vv1.at[1:4], vv1x.at[0])
    ev1s = send_sides(pv1, rsv1)

    def around2(mine, ref, step):
        mid = mine if step == 4 else ref[step, 1]
        return mid, rot(ref[step, 2], 32, 1), rot(ref[step, 0], -32, 1)

    def near2(parts, n):
        mid, right, left = parts
        at = (lane - 32 * n) & 127
        side = jnp.where(at < 40, right, jnp.where(at >= 120, left, 0.0))
        return rot(jnp.where(at < 32, mid, side), -32 * n, 1)

    for c in ekd2:
        c.arrived()
    mine = kd2[...]
    for step in range(9):
        there = inside(step - 4)
        keep = jnp.logical_or(lane < (32 + 8 * has_right) * there, lane >= 128 - 8 * has_left * there)
        parts = around2(mine, kd2x, step)
        for x in range(2):
            k2[2 * step + x] = near2(parts, x)
            diag = near2(parts, 2 + x)
            dg2[2 * step + x] = diag
            t2[2 * step + x] = jnp.where(keep, OMEGA / diag, 0.0)

    def to_level3(pairs):
        n = len(pairs)
        for i, pair in enumerate(pairs):
            t1[8 * i : 8 * i + 8, :] = pair
        y = 0.125 * dot(halve_rows(t1, 4 * n), r23)
        for i in range(n):
            t3[i, 0:4, :] = y[4 * i : 4 * i + 4, :]
        return t3[0:n]

    k2_all = k2[...]
    k2_all = (k2_all,) + beside(k2_all, 2)
    t3[...] = jnp.zeros_like(t3)
    half3 = 0.5 * 0.015625
    k3 = to_level3([k2[2 * i] + k2[2 * i + 1] for i in range(9)])
    most3 = half3 * (CALL * k3[1:-1] + ring_sum(k3))

    for c in e2:
        c.arrived()
    mine = gl2[...]
    for step in range(9):
        parts = around2(mine, gl2x, step)
        for x in range(2):
            f2[2 * step + x] = near2(parts, x)
        l2[step] = near2(parts, 2)

    def sweep2(v, depth):
        lo, hi = 9 - depth, 9 + depth
        rest = f2[lo:hi] - ring_apply(v, cut_planes(k2_all, lo - 1, hi + 1), dg2[lo:hi], half2)
        return v[1:-1] + t2[lo:hi] * rest

    vb = sweep2(t2[...] * f2[...], 8)
    r = f2[2:16] - ring_apply(vb, cut_planes(k2_all, 1, 17), dg2[2:16], half2)
    l3 = to_level3([l2[i + 1] for i in range(7)])
    f3 = to_level3([r[2 * i] + r[2 * i + 1] for i in range(7)])
    diag3 = l3 + most3
    inv3 = []
    for i in range(7):
        there = inside(i - 3)
        keep = jnp.logical_or(lane < (16 + 4 * has_right) * there, lane >= 128 - 4 * has_left * there)
        inv3.append(jnp.where(jnp.logical_and(keep, row < 4), OMEGA / diag3[i], 0.0)[None])
    inv3 = jnp.concatenate(inv3, axis=0)
    v3 = inv3 * f3
    rest = f3[1:-1] - ring_apply(v3, cut_planes((k3,) + beside(k3, 2), 1, 8), diag3[1:-1], half3)
    v3 = v3[1:-1] + inv3[1:-1] * rest

    p32 = ring_map(cut(64), 64, True)
    wide3 = dot(v3.reshape(40, 128), p32)
    for i in range(5):
        double_rows(t1.at[8 * i : 8 * i + 8, :], wide3[8 * i : 8 * i + 4, :])
    e3 = t1[0:40, :].reshape(5, 8, 128)
    e3 = jnp.concatenate([e3[i // 2][None] for i in range(10)], axis=0)
    vb = vb[3:13] + e3
    vb = sweep2(vb, 4)
    vb = sweep2(vb, 3)

    for c in ev1x + ev1s:
        c.arrived()
    fill1(va1, vv1, vv1x, rsv1)
    p21 = ring_map(cut(96), 64, True)
    double_rows(tm.at[0:96, :], dot(vb.reshape(48, 128), p21))
    e2v = tm[0:96, :].reshape(6, 16, 128)
    inner = jnp.logical_or(lane < 68, lane >= 124)
    inner = jnp.concatenate([inner, inner], axis=0)
    v = [jnp.where(inner, va1[p] + e2v[(p - 3) // 2 + 2], 0.0)[None] for p in range(10)]
    v = sweep1(jnp.concatenate(v, axis=0), 3, inv1)
    v = sweep1(v, 2, inv1)

    e1 = v.reshape(96, 128)
    double_rows(tm.at[0:192, :], dot(e1, ring_map(main_z, 96, True)))
    double_rows(ts.at[0:192, :], dot(e1, ring_map(strip_z, 96, True)))
    for c in evx:
        c.arrived()
        c.left()
    def correct(i):
        at = 32 * (i // 2)
        m = bvm[i] + tm[at : at + 32, :]
        s = ts[at : at + 8, :]
        for t in range(1, 4):
            s = jnp.where(group == t, ts[at + 8 * t : at + 8 * t + 8, :], s)
        ready(field_a, i, m, bvs[i] + s, True)

    loop(0, 12, correct)
    loop(1, 11, lambda i: sweep(i, False))

    def last(i):
        out_ref[i - 2] = bvm[i] + dm[i] * resid_main(field_b, i)

    loop(2, 10, last)
    for c in started:
        if not any(c is done for done in evx):
            c.left()


def solution(mesh):
    nw, nz = mesh.shape["wide"], mesh.shape["narrow"]

    def on_device(source, permeability, leakage):
        def vm(*shape):
            return pltpu.VMEM(shape, F32)

        def pair(n):
            return [vm(n, 32, 128), vm(n, 8, 128)]

        scratch = pair(16) * 4 + pair(12) * 4 + pair(12) * 8 + [vm(256, 128), vm(256, 128)]
        scratch += [vm(2, 2, 3, 8, 128), vm(3, 2, 2, 3, 8, 128)]
        scratch += [vm(4, 2, 16, 128), vm(2, 3, 2, 16, 128), vm(4, 16, 128), vm(2, 2, 16, 128)]
        scratch += [vm(2, 8, 128), vm(3, 2, 8, 128)]
        scratch += [vm(4, 16, 128), vm(2, 3, 16, 128)]
        scratch += [vm(8, 16, 128), vm(10, 16, 128), vm(8, 16, 128), vm(8, 16, 128), vm(10, 16, 128), vm(128, 128)]
        scratch += [vm(8, 128), vm(9, 3, 8, 128), vm(8, 128), vm(9, 3, 8, 128)]
        scratch += [vm(18, 8, 128), vm(18, 8, 128), vm(18, 8, 128), vm(9, 8, 128), vm(18, 8, 128), vm(9, 8, 128)]
        n = 12 + 2 + 2 + 26 + 4 + 26 + 8
        scratch += [pltpu.SemaphoreType.DMA((3,)), pltpu.SemaphoreType.DMA((n,)), pltpu.SemaphoreType.DMA((n,))]

        def body(*refs):
            kernel(nw, nz, *refs)

        return pl.pallas_call(
            body,
            out_shape=pltpu.VMEM(source.shape, F32),
            in_specs=[pl.BlockSpec(memory_space=pltpu.HBM)] * 3,
            out_specs=pl.BlockSpec(memory_space=pltpu.VMEM),
            scratch_shapes=scratch,
            compiler_params=pltpu.CompilerParams(
                collective_id=0, has_side_effects=True, vmem_limit_bytes=60 * 2**20
            ),
            name="vcycle",
        )(source, permeability, leakage)

    spec = P("wide", None, "narrow")
    return jax.shard_map(on_device, mesh=mesh, in_specs=(spec, spec, spec), out_specs=spec, check_vma=False)
```

```python
import jax
import jax.numpy as jnp
from jax import lax
from jax.experimental import pallas as pl
from jax.experimental.pallas import tpu as pltpu
from jax.sharding import PartitionSpec as P

MESH = pl.DeviceIdType.MESH
OMEGA = 0.8
F32 = jnp.float32


def weight(a, b, c):
    n = a + b + c
    return (a * 1.0 + b * 0.7 + c * 0.4) / n * {1: 1.0, 2: 0.25, 3: 0.1}[n]


CX, CY, CZ = weight(1, 0, 0), weight(0, 1, 0), weight(0, 0, 1)
CXY, CXZ, CYZ, CXYZ = weight(1, 1, 0), weight(1, 0, 1), weight(0, 1, 1), weight(1, 1, 1)
CALL = 2 * (CX + CY + CZ) + 4 * (CXY + CXZ + CYZ) + 8 * CXYZ

SIDES = [(a, b) for b in (-1, 1) for a in (-1, 0, 1)]
FAR = [(a, b) for a in range(-4, 5) for b in (-1, 0, 1) if (a, b) != (0, 0)]


def iota(shape, dim):
    return lax.broadcasted_iota(jnp.int32, shape, dim)


def lanes():
    return iota((8, 128), 1)


def rot(x, shift, axis):
    shift %= x.shape[axis]
    return x if shift == 0 else pltpu.roll(x, shift, axis)


def rows_beside(t):
    axis = t.ndim - 2
    n = t.shape[axis]
    row = iota(t.shape, axis)
    up = jnp.where(row == 0, 0.0, rot(t, 1, axis))
    down = jnp.where(row == n - 1, 0.0, rot(t, n - 1, axis))
    return up + down


def neighbours(u, p, y):
    x, xp = u[0] + u[2], p[0] + p[2]
    inner = CXY * x + CXYZ * xp + CY * u[1] + CYZ * p[1]
    return CX * x + CXZ * xp + CZ * p[1] + y(inner)


def beside_main(m, s):
    lane = iota(m.shape, 1)
    edge = jnp.where((iota(s.shape, 1) & 31) < 9, s, rot(s, -14, 1))
    edge = jnp.concatenate([rot(edge, 119 - 32 * t, 1) for t in range(4)], axis=0)
    return jnp.where(lane == 0, edge, rot(m, 1, 1)), jnp.where(lane == 127, edge, rot(m, 127, 1))


def beside(u, axis=1):
    return rot(u, 1, axis), rot(u, 127, axis)


def rows_strip(c):
    row, lane = iota((8, 128), 0), iota((8, 128), 1)
    up, down = rot(c, 1, 0), rot(c, 7, 0)
    up = jnp.where(row == 0, jnp.where(lane < 32, 0.0, rot(up, 32, 1)), up)
    down = jnp.where(row == 7, jnp.where(lane >= 96, 0.0, rot(down, 96, 1)), down)
    return up + down


def slabs(u):
    return u[:-2], u[1:-1], u[2:]


def ring_sum(u):
    below, above = beside(u, 2)
    return neighbours(slabs(u), slabs(below + above), rows_beside)


def ring_apply(v, k, diag, half):
    k, k_below, k_above = k
    below, above = beside(v, 2)
    s1 = neighbours(slabs(v), slabs(below + above), rows_beside)
    s2 = neighbours(slabs(k * v), slabs(k_below * below + k_above * above), rows_beside)
    return diag * v[1:-1] - half * (k[1:-1] * s1 + s2)


def cut_planes(k, lo, hi):
    return tuple(part[lo:hi] for part in k)


def dot(a, b):
    return lax.dot_general(a, b, (((1,), (0,)), ((), ())), precision=lax.Precision.HIGHEST, preferred_element_type=F32)


def ring_map(fine_of, coarse_cut, transpose=False):
    f_dim = 1 if transpose else 0
    i, j = iota((128, 128), f_dim), iota((128, 128), 1 - f_dim)
    return ((fine_of(i) >> 1) == jnp.where(j < coarse_cut, j, j - 128)).astype(F32)


def cut(c):
    return lambda i: jnp.where(i < c, i, i - 128)


def main_z(i):
    return i


def strip_z(i):
    r = i & 31
    return jnp.where(r < 16, r + 120, r - 24)


def strip_halo_z(i):
    r = i & 31
    return jnp.where(jnp.logical_or(r < 8, r >= 24), 4096, strip_z(i))


def halve_rows(ref, n):
    return ref[pl.ds(0, n, stride=2), :] + ref[pl.ds(1, n, stride=2), :]


def double_rows(ref, x):
    n = x.shape[0]
    ref[pl.ds(0, n, stride=2), :] = x
    ref[pl.ds(1, n, stride=2), :] = x


def kernel(
    nw, nz, f_hbm, k_hbm, l_hbm, out_ref,
    km, ks, pkm, pks, kbm, kbs, kam, kas, fm, fs, lm, ls, dgm, dgs, dm, ds_,
    avm, avs, apm, aps, aqm, aqs, arm, ars, bvm, bvs, bpm, bps, bqm, bqs, brm, brs, tm, ts,
    pack0, rs0, kd1, kd1x, gg1, gg1x, pv1, rsv1, vv1, vv1x,
    k1l, k1, dg1, f1, va1, t1, kd2, kd2x, gl2, gl2x, k2, dg2, f2, l2, t2, t3, hello, loc_sem, send_sem, recv_sem,
):
    w, z = lax.axis_index("wide"), lax.axis_index("narrow")

    def device(a, b):
        return (lax.rem(w + (a + nw), nw), lax.rem(z + (b + nz), nz))

    def in_grid(a, b):
        ok = jnp.logical_and(w + a >= 0, w + a < nw)
        return ok if b == 0 else jnp.logical_and(ok, jnp.logical_and(z + b >= 0, z + b < nz))

    has_left, has_right = (z > 0).astype(jnp.int32), (z < nz - 1).astype(jnp.int32)

    def inside(step):
        return jnp.logical_and(w + step >= 0, w + step < nw).astype(jnp.int32)

    class Message:
        def __init__(self, n, src, dst, a, b):
            self.to, self.origin = (a, b), (-a, -b)
            self.copy = pltpu.make_async_remote_copy(
                src_ref=src, dst_ref=dst, send_sem=send_sem.at[n], recv_sem=recv_sem.at[n],
                device_id=device(a, b), device_id_type=MESH,
            )
            pl.when(in_grid(*self.to))(self.copy.start)

        def arrived(self):
            pl.when(in_grid(*self.origin))(self.copy.wait_recv)

        def left(self):
            pl.when(in_grid(*self.to))(self.copy.wait_send)

    started = []

    def send(src, dst, a, b):
        started.append(Message(len(started), src, dst, a, b))
        return started[-1]

    def loop(lo, hi, body):
        for i in range(lo, hi):
            body(i)

    lane, row = lanes(), iota((8, 128), 0)
    group, place = lane >> 5, lane & 31

    for ref in (rs0, rsv1, kd1x, gg1x, vv1x, kd2x, gl2x):
        ref[...] = jnp.zeros_like(ref)

    def clear(k_planes, planes, v_plane):
        def body():
            km[k_planes] = jnp.zeros((4, 32, 128), F32)
            fm[planes] = jnp.zeros((2, 32, 128), F32)
            lm[planes] = jnp.zeros((2, 32, 128), F32)
            bvm[v_plane] = jnp.zeros((32, 128), F32)
            bvs[v_plane] = jnp.zeros((8, 128), F32)

        return body

    pl.when(w == 0)(clear(slice(0, 4), slice(0, 2), 0))
    pl.when(w == nw - 1)(clear(slice(12, 16), slice(10, 12), 11))

    barrier = pltpu.get_barrier_semaphore()

    def greet(a, b):
        def body():
            pl.semaphore_signal(barrier, inc=1, device_id=device(a, b), device_id_type=MESH)

        return body

    for a, b in FAR:
        if b >= 0:
            pl.when(in_grid(a, b))(greet(a, b))
    loads = []
    for n, (src, dst) in enumerate(((k_hbm, km.at[4:12]), (f_hbm, fm.at[2:10]), (l_hbm, lm.at[2:10]))):
        loads.append(pltpu.make_async_copy(src, dst, loc_sem.at[n]))
        loads[-1].start()

    def own_strip(m):
        out = rot(m[0:8, :], 8, 1)
        for t in range(1, 4):
            out = jnp.where(group == t, rot(m[8 * t : 8 * t + 8, :], 32 * t + 8, 1), out)
        return jnp.where(place < 16, out, rot(out, 16, 1))

    eighth = place >> 3
    even = (eighth & 1) == 0
    spot = (0, 16, 8, 24)

    def pack_strips(strips):
        left, right = jnp.zeros((8, 128), F32), jnp.zeros((8, 128), F32)
        for x, s in enumerate(strips):
            r = rot(s, spot[x] - 24, 1)
            left = jnp.where(eighth == spot[x] // 8, r, left)
            right = jnp.where(eighth == (spot[x] // 8 + 1) % 4, r, right)
        return left, rot(right, 32, 1)

    def merge(rs, n):
        out = {}
        for step, half in ((0, 1), (1, 0), (1, 1), (2, 0)):
            left, right = rs[step, 0, half, n], rs[step, 1, half, n]
            out[step, half] = (jnp.where(even, left, right), jnp.where(even, right, left))
        return out

    own_lanes = jnp.logical_or(place < 8, place >= 24)

    def whole_strip(own, merged, x):
        at = x % 8
        halo = merged[(x + 8) // 8, at // 4][at % 4 // 2]
        return jnp.where(own_lanes, own, rot(halo, 8 - spot[at % 4], 1))

    def count(pos, reach, size):
        return jnp.minimum(pos, reach) + 1 + jnp.minimum(size - 1 - pos, reach)

    pl.semaphore_wait(barrier, count(w, 4, nw) * (1 + has_left) - 1)

    def say_hello():
        pl.semaphore_signal(hello, inc=1, device_id=device(0, -1), device_id_type=MESH)

    pl.when(z > 0)(say_hello)

    def send_planes(src_lo, dst_hi, src_hi, dst_lo):
        return [send(src_hi, dst_lo, 1, 0), send(src_lo, dst_hi, -1, 0)]

    def send_sides(pack, rs):
        return [send(pack.at[0 if b < 0 else 1], rs.at[1 - a, 0 if b < 0 else 1], a, b) for a, b in SIDES]

    def send_far(src, dst):
        return [send(src, dst.at[4 - a, 1 - b], a, b) for a, b in FAR]

    e0k = send_planes(k_hbm.at[0:4], km.at[12:16], k_hbm.at[4:8], km.at[0:4])
    e0f = send_planes(f_hbm.at[0:2], fm.at[10:12], f_hbm.at[6:8], fm.at[0:2])
    e0l = send_planes(l_hbm.at[0:2], lm.at[10:12], l_hbm.at[6:8], lm.at[0:2])

    for n, (ref, strip, off) in enumerate(((km, ks, 4), (fm, fs, 2), (lm, ls, 2))):
        loads[n].wait()
        own = [own_strip(ref[x + off]) for x in range(8)]
        for x in range(8):
            strip[x + off] = own[x]
        for half in range(2):
            pack0[0, half, n], pack0[1, half, n] = pack_strips(own[4 * half : 4 * half + 4])

    def send_strips(b):
        side = 0 if b < 0 else 1
        out = []
        for a in (0, -1, 1):
            if a == 0:
                out.append(send(pack0.at[side], rs0.at[1, side], a, b))
            else:
                half = 0 if a < 0 else 1
                out.append(send(pack0.at[side, half], rs0.at[1 - a, side, half], a, b))
        return out

    e0s = send_strips(-1)
    def hear_hello():
        pl.semaphore_wait(hello, 1)

    pl.when(z < nz - 1)(hear_hello)
    e0s += send_strips(1)

    rm01, rs01 = ring_map(main_z, 96), ring_map(strip_halo_z, 96)
    r12, r23 = ring_map(cut(96), 64), ring_map(cut(64), 64)

    for c in e0k + e0s:
        c.arrived()
    merged = merge(rs0, 0)
    for p in range(16):
        own = ks[p] if 4 <= p < 12 else own_strip(km[p])
        ks[p] = whole_strip(own, merged, p - 4)

    def spread(strip):
        return jnp.concatenate([jnp.where(group == t, strip, 0.0) for t in range(4)], axis=0)

    def k_lanes(i):
        for p in (2 * i, 2 * i + 1):
            m, s = km[p], ks[p]
            below, above = beside_main(m, s)
            kbm[p], kam[p], pkm[p] = below, above, below + above
            below, above = beside(s)
            kbs[p], kas[p], pks[p] = below, above, below + above
        tm[32 * i : 32 * i + 32, :] = km[2 * i] + km[2 * i + 1]
        ts[32 * i : 32 * i + 32, :] = spread(ks[2 * i] + ks[2 * i + 1])

    loop(0, 8, k_lanes)

    coarse = dot(halve_rows(tm, 128), rm01) + dot(halve_rows(ts, 128), rs01)
    k1l[...] = (0.125 * coarse).reshape(8, 16, 128)

    for c in e0f + e0l:
        c.arrived()
    for n, (ref, strip) in ((1, (fm, fs)), (2, (lm, ls))):
        merged = merge(rs0, n)
        for p in range(12):
            own = strip[p] if 2 <= p < 10 else own_strip(ref[p])
            strip[p] = whole_strip(own, merged, p - 2)

    def l_pairs(i):
        tm[32 * i : 32 * i + 32, :] = lm[2 * i + 2] + lm[2 * i + 3]
        ts[32 * i : 32 * i + 32, :] = spread(ls[2 * i + 2] + ls[2 * i + 3])

    loop(0, 4, l_pairs)
    l1 = dot(halve_rows(tm, 64), rm01) + dot(halve_rows(ts, 64), rs01)
    l1 = (0.125 * l1).reshape(4, 16, 128)
    own1 = k1l[2:6]
    half1 = 0.5 * 0.25
    diag1 = l1 + half1 * (CALL * own1 + ring_sum(k1l[1:7]))
    kd1[:, 0], kd1[:, 1] = own1, diag1
    ekd = send_planes(kd1.at[0:3], kd1x.at[1], kd1.at[1:4], kd1x.at[0])

    lane32 = iota((32, 128), 1)

    def three(ref, i):
        return ref[i - 1], ref[i], ref[i + 1]

    def ready(v, i, m, s, strips):
        vm, vs, pm, ps, qm, qs, rm, rs = v
        vm[i], vs[i] = m, s
        below, above = beside_main(m, s)
        pm[i], qm[i] = below + above, m * km[i + 2]
        rm[i] = below * kbm[i + 2] + above * kam[i + 2]
        if strips:
            below, above = beside(s)
            ps[i], qs[i] = below + above, s * ks[i + 2]
            rs[i] = below * kbs[i + 2] + above * kas[i + 2]

    field_a = (avm, avs, apm, aps, aqm, aqs, arm, ars)
    field_b = (bvm, bvs, bpm, bps, bqm, bqs, brm, brs)

    def resid_main(v, i):
        vm, vs, pm, ps, qm, qs, rm, rs = v
        s1 = neighbours(three(vm, i), three(pm, i), rows_beside)
        s2 = neighbours(three(qm, i), three(rm, i), rows_beside)
        return fm[i] - dgm[i] * vm[i] + 0.5 * (km[i + 2] * s1 + s2)

    def resid_strip(v, i):
        vm, vs, pm, ps, qm, qs, rm, rs = v
        s1 = neighbours(three(vs, i), three(ps, i), rows_strip)
        s2 = neighbours(three(qs, i), three(rs, i), rows_strip)
        return fs[i] - dgs[i] * vs[i] + 0.5 * (ks[i + 2] * s1 + s2)

    def first(i):
        there = inside(-1) if i < 2 else inside(1) if i >= 10 else 1
        around = neighbours(three(km, i + 2), three(pkm, i + 2), rows_beside)
        diag = lm[i] + 0.5 * (CALL * km[i + 2] + around)
        inv = jnp.where(lane32 < 128 * there, OMEGA / diag, 0.0)
        dgm[i], dm[i] = diag, inv
        m = inv * fm[i]
        around = neighbours(three(ks, i + 2), three(pks, i + 2), rows_strip)
        diag = ls[i] + 0.5 * (CALL * ks[i + 2] + around)
        keep = jnp.logical_or(place < (8 + 8 * has_right) * there, place >= 32 - (8 + 8 * has_left) * there)
        inv = jnp.where(keep, OMEGA / diag, 0.0)
        dgs[i], ds_[i] = diag, inv
        ready(field_a, i, m, inv * fs[i], True)

    loop(0, 12, first)

    def sweep(i, strips):
        m = avm[i] + dm[i] * resid_main(field_a, i)
        s = avs[i] + ds_[i] * resid_strip(field_a, i)
        ready(field_b, i, m, s, strips)

    loop(1, 11, lambda i: sweep(i, True))

    def resid_pairs(i):
        pair = resid_main(field_b, 2 * i + 2) + resid_main(field_b, 2 * i + 3)
        tm[32 * i : 32 * i + 32, :] = pair
        pair = resid_strip(field_b, 2 * i + 2) + resid_strip(field_b, 2 * i + 3)
        ts[32 * i : 32 * i + 32, :] = spread(pair)

    loop(0, 4, resid_pairs)
    rhs1 = dot(halve_rows(tm, 64), rm01) + dot(halve_rows(ts, 64), rs01)
    gg1[...] = (0.125 * rhs1).reshape(4, 16, 128)

    e1x = send_planes(gg1.at[0:2], gg1x.at[1], gg1.at[2:4], gg1x.at[0])

    kk = k1l[...]
    for i in range(4):
        t1[16 * i : 16 * i + 16, :] = kk[2 * i] + kk[2 * i + 1]
    k2l = (0.125 * dot(halve_rows(t1, 32), r12)).reshape(4, 8, 128)
    for i in range(2):
        t1[16 * i : 16 * i + 16, :] = l1[2 * i] + l1[2 * i + 1]
    l2own = (0.125 * dot(halve_rows(t1, 16), r12)).reshape(2, 8, 128)
    half2 = 0.5 * 0.0625
    diag2 = l2own + half2 * (CALL * k2l[1:3] + ring_sum(k2l))
    both = (k2l[1], k2l[2], diag2[0], diag2[1])
    low = jnp.where(lane < 32, both[0], rot(both[1], 32, 1))
    high = jnp.where(lane < 96, rot(both[2], 64, 1), rot(both[3], 96, 1))
    kd2[...] = jnp.where(lane < 64, low, high)
    l2sum = rot(l2own[0] + l2own[1], 64, 1)
    ekd2 = send_far(kd2, kd2x)

    evx = []
    for ref in (bvm, bvs):
        evx += [send(ref.at[8], ref.at[0], 1, 0), send(ref.at[3], ref.at[11], -1, 0)]

    def pack_sides1(arr):
        left, right = jnp.zeros((8, 128), F32), jnp.zeros((8, 128), F32)
        for x in range(4):
            for t in range(2):
                slot = 2 * x + t
                r = rot(arr[x, 8 * t : 8 * t + 8, :], 4 * slot, 1)
                left = jnp.where((lane >> 2) == slot, r, left)
                right = jnp.where((lane >> 2) == slot + 15, r, right)
        return left, right

    def fill1(ref, own, x_ref, rs):
        merged = [jnp.where(group == 0, rs[step, 0], rs[step, 1]) for step in range(3)]
        for p in range(10):
            x = p - 3
            for t in range(2):
                side = rot(merged[(x + 4) // 4], 64 - 4 * (2 * (x % 4) + t), 1)
                side = jnp.where(jnp.logical_or(lane < 68, lane >= 124), side, 0.0)
                rows = slice(8 * t, 8 * t + 8)
                center = x_ref[0, x + 3, rows, :] if x < 0 else x_ref[1, x - 4, rows, :] if x > 3 else own[x, rows, :]
                ref[p, 8 * t : 8 * t + 8, :] = jnp.where(lane < 64, center, side)

    for c in ekd + e1x:
        c.arrived()
    k1[0:3], k1[3:7], k1[7:10] = kd1x[0, :, 0], own1, kd1x[1, :, 0]
    dg1[0:2], dg1[2:6], dg1[6:8] = kd1x[0, 1:3, 1], diag1, kd1x[1, 0:2, 1]
    f1[0:2], f1[2:6], f1[6:8] = gg1x[0], gg1[...], gg1x[1]
    k1_all = k1[...]
    k1_all = (k1_all,) + beside(k1_all, 2)

    lane1 = iota((2, 16, 128), 2)

    def inverse1(lo, hi, step):
        there = inside(step)
        keep = jnp.logical_or(lane1 < (64 + 4 * has_right) * there, lane1 >= 128 - 4 * has_left * there)
        return jnp.where(keep, OMEGA / dg1[lo:hi], 0.0)

    def sweep1(v, depth, inv):
        kk = cut_planes(k1_all, 3 - depth, 7 + depth)
        lo, hi = 3 - depth, 5 + depth
        rest = f1[lo:hi] - ring_apply(v, kk, dg1[lo:hi], half1)
        return v[1:-1] + inv[lo:hi] * rest

    inv1 = jnp.concatenate([inverse1(0, 2, -1), inverse1(2, 4, 0), inverse1(4, 6, 0), inverse1(6, 8, 1)], axis=0)
    v = sweep1(inv1 * f1[...], 2, inv1)
    r = f1[2:6] - ring_apply(v, cut_planes(k1_all, 2, 8), dg1[2:6], half1)
    for i in range(2):
        t1[16 * i : 16 * i + 16, :] = r[2 * i] + r[2 * i + 1]
    rhs2 = (0.125 * dot(halve_rows(t1, 16), r12)).reshape(2, 8, 128)

    gl2[...] = jnp.where(lane < 32, rhs2[0], jnp.where(lane < 64, rot(rhs2[1], 32, 1), l2sum))
    e2 = send_far(gl2, gl2x)
    vv1[...] = v[1:5]
    pv1[0], pv1[1] = pack_sides1(v[1:5])
    ev1x = send_planes(vv1.at[0:3], vv1x.at[1], vv1.at[1:4], vv1x.at[0])
    ev1s = send_sides(pv1, rsv1)

    def around2(mine, ref, step):
        mid = mine if step == 4 else ref[step, 1]
        return mid, rot(ref[step, 2], 32, 1), rot(ref[step, 0], -32, 1)

    def near2(parts, n):
        mid, right, left = parts
        at = (lane - 32 * n) & 127
        side = jnp.where(at < 40, right, jnp.where(at >= 120, left, 0.0))
        return rot(jnp.where(at < 32, mid, side), -32 * n, 1)

    for c in ekd2:
        c.arrived()
    mine = kd2[...]
    for step in range(9):
        there = inside(step - 4)
        keep = jnp.logical_or(lane < (32 + 8 * has_right) * there, lane >= 128 - 8 * has_left * there)
        parts = around2(mine, kd2x, step)
        for x in range(2):
            k2[2 * step + x] = near2(parts, x)
            diag = near2(parts, 2 + x)
            dg2[2 * step + x] = diag
            t2[2 * step + x] = jnp.where(keep, OMEGA / diag, 0.0)

    def to_level3(pairs):
        n = len(pairs)
        for i, pair in enumerate(pairs):
            t1[8 * i : 8 * i + 8, :] = pair
        y = 0.125 * dot(halve_rows(t1, 4 * n), r23)
        for i in range(n):
            t3[i, 0:4, :] = y[4 * i : 4 * i + 4, :]
        return t3[0:n]

    k2_all = k2[...]
    k2_all = (k2_all,) + beside(k2_all, 2)
    t3[...] = jnp.zeros_like(t3)
    half3 = 0.5 * 0.015625
    k3 = to_level3([k2[2 * i] + k2[2 * i + 1] for i in range(9)])
    most3 = half3 * (CALL * k3[1:-1] + ring_sum(k3))

    for c in e2:
        c.arrived()
    mine = gl2[...]
    for step in range(9):
        parts = around2(mine, gl2x, step)
        for x in range(2):
            f2[2 * step + x] = near2(parts, x)
        l2[step] = near2(parts, 2)

    def sweep2(v, depth):
        lo, hi = 9 - depth, 9 + depth
        rest = f2[lo:hi] - ring_apply(v, cut_planes(k2_all, lo - 1, hi + 1), dg2[lo:hi], half2)
        return v[1:-1] + t2[lo:hi] * rest

    vb = sweep2(t2[...] * f2[...], 8)
    r = f2[2:16] - ring_apply(vb, cut_planes(k2_all, 1, 17), dg2[2:16], half2)
    l3 = to_level3([l2[i + 1] for i in range(7)])
    f3 = to_level3([r[2 * i] + r[2 * i + 1] for i in range(7)])
    diag3 = l3 + most3
    inv3 = []
    for i in range(7):
        there = inside(i - 3)
        keep = jnp.logical_or(lane < (16 + 4 * has_right) * there, lane >= 128 - 4 * has_left * there)
        inv3.append(jnp.where(jnp.logical_and(keep, row < 4), OMEGA / diag3[i], 0.0)[None])
    inv3 = jnp.concatenate(inv3, axis=0)
    v3 = inv3 * f3
    rest = f3[1:-1] - ring_apply(v3, cut_planes((k3,) + beside(k3, 2), 1, 8), diag3[1:-1], half3)
    v3 = v3[1:-1] + inv3[1:-1] * rest

    p32 = ring_map(cut(64), 64, True)
    wide3 = dot(v3.reshape(40, 128), p32)
    for i in range(5):
        double_rows(t1.at[8 * i : 8 * i + 8, :], wide3[8 * i : 8 * i + 4, :])
    e3 = t1[0:40, :].reshape(5, 8, 128)
    e3 = jnp.concatenate([e3[i // 2][None] for i in range(10)], axis=0)
    vb = vb[3:13] + e3
    vb = sweep2(vb, 4)
    vb = sweep2(vb, 3)

    for c in ev1x + ev1s:
        c.arrived()
    fill1(va1, vv1, vv1x, rsv1)
    p21 = ring_map(cut(96), 64, True)
    double_rows(tm.at[0:96, :], dot(vb.reshape(48, 128), p21))
    e2v = tm[0:96, :].reshape(6, 16, 128)
    inner = jnp.logical_or(lane < 68, lane >= 124)
    inner = jnp.concatenate([inner, inner], axis=0)
    v = [jnp.where(inner, va1[p] + e2v[(p - 3) // 2 + 2], 0.0)[None] for p in range(10)]
    v = sweep1(jnp.concatenate(v, axis=0), 3, inv1)
    v = sweep1(v, 2, inv1)

    e1 = v.reshape(96, 128)
    double_rows(tm.at[0:192, :], dot(e1, ring_map(main_z, 96, True)))
    double_rows(ts.at[0:192, :], dot(e1, ring_map(strip_z, 96, True)))
    for c in evx:
        c.arrived()
        c.left()
    def correct(i):
        at = 32 * (i // 2)
        m = bvm[i] + tm[at : at + 32, :]
        s = ts[at : at + 8, :]
        for t in range(1, 4):
            s = jnp.where(group == t, ts[at + 8 * t : at + 8 * t + 8, :], s)
        ready(field_a, i, m, bvs[i] + s, True)

    loop(0, 12, correct)
    loop(1, 11, lambda i: sweep(i, False))

    def last(i):
        out_ref[i - 2] = bvm[i] + dm[i] * resid_main(field_b, i)

    loop(2, 10, last)
    for c in started:
        if not any(c is done for done in evx):
            c.left()


def solution(mesh):
    nw, nz = mesh.shape["wide"], mesh.shape["narrow"]

    def on_device(source, permeability, leakage):
        def vm(*shape):
            return pltpu.VMEM(shape, F32)

        def pair(n):
            return [vm(n, 32, 128), vm(n, 8, 128)]

        scratch = pair(16) * 4 + pair(12) * 4 + pair(12) * 8 + [vm(256, 128), vm(256, 128)]
        scratch += [vm(2, 2, 3, 8, 128), vm(3, 2, 2, 3, 8, 128)]
        scratch += [vm(4, 2, 16, 128), vm(2, 3, 2, 16, 128), vm(4, 16, 128), vm(2, 2, 16, 128)]
        scratch += [vm(2, 8, 128), vm(3, 2, 8, 128)]
        scratch += [vm(4, 16, 128), vm(2, 3, 16, 128)]
        scratch += [vm(8, 16, 128), vm(10, 16, 128), vm(8, 16, 128), vm(8, 16, 128), vm(10, 16, 128), vm(128, 128)]
        scratch += [vm(8, 128), vm(9, 3, 8, 128), vm(8, 128), vm(9, 3, 8, 128)]
        scratch += [vm(18, 8, 128), vm(18, 8, 128), vm(18, 8, 128), vm(9, 8, 128), vm(18, 8, 128), vm(9, 8, 128)]
        n = 12 + 2 + 2 + 26 + 4 + 26 + 8
        scratch += [pltpu.SemaphoreType.REGULAR, pltpu.SemaphoreType.DMA((3,)), pltpu.SemaphoreType.DMA((n,)), pltpu.SemaphoreType.DMA((n,))]

        def body(*refs):
            kernel(nw, nz, *refs)

        return pl.pallas_call(
            body,
            out_shape=pltpu.VMEM(source.shape, F32),
            in_specs=[pl.BlockSpec(memory_space=pltpu.HBM)] * 3,
            out_specs=pl.BlockSpec(memory_space=pltpu.VMEM),
            scratch_shapes=scratch,
            compiler_params=pltpu.CompilerParams(
                collective_id=0, has_side_effects=True, vmem_limit_bytes=60 * 2**20
            ),
            name="vcycle",
        )(source, permeability, leakage)

    spec = P("wide", None, "narrow")
    return jax.shard_map(on_device, mesh=mesh, in_specs=(spec, spec, spec), out_specs=spec, check_vma=False)
```

```python
import jax
import jax.numpy as jnp
from jax import lax
from jax.experimental import pallas as pl
from jax.experimental.pallas import tpu as pltpu
from jax.sharding import PartitionSpec as P

MESH = pl.DeviceIdType.MESH
OMEGA = 0.8
F32 = jnp.float32


def weight(a, b, c):
    n = a + b + c
    return (a * 1.0 + b * 0.7 + c * 0.4) / n * {1: 1.0, 2: 0.25, 3: 0.1}[n]


CX, CY, CZ = weight(1, 0, 0), weight(0, 1, 0), weight(0, 0, 1)
CXY, CXZ, CYZ, CXYZ = weight(1, 1, 0), weight(1, 0, 1), weight(0, 1, 1), weight(1, 1, 1)
CALL = 2 * (CX + CY + CZ) + 4 * (CXY + CXZ + CYZ) + 8 * CXYZ

SIDES = [(a, b) for b in (-1, 1) for a in (-1, 0, 1)]
FAR = [(a, b) for a in range(-4, 5) for b in (-1, 0, 1) if (a, b) != (0, 0)]


def iota(shape, dim):
    return lax.broadcasted_iota(jnp.int32, shape, dim)


def lanes():
    return iota((8, 128), 1)


def rot(x, shift, axis):
    shift %= x.shape[axis]
    return x if shift == 0 else pltpu.roll(x, shift, axis)


def rows_beside(t):
    axis = t.ndim - 2
    n = t.shape[axis]
    row = iota(t.shape, axis)
    up = jnp.where(row == 0, 0.0, rot(t, 1, axis))
    down = jnp.where(row == n - 1, 0.0, rot(t, n - 1, axis))
    return up + down


def neighbours(u, p, y):
    x, xp = u[0] + u[2], p[0] + p[2]
    inner = CXY * x + CXYZ * xp + CY * u[1] + CYZ * p[1]
    return CX * x + CXZ * xp + CZ * p[1] + y(inner)


def beside(u, axis=1):
    return rot(u, 1, axis), rot(u, 127, axis)


def rows_strip(c):
    row, lane = iota((8, 128), 0), iota((8, 128), 1)
    up, down = rot(c, 1, 0), rot(c, 7, 0)
    up = jnp.where(row == 0, jnp.where(lane < 32, 0.0, rot(up, 32, 1)), up)
    down = jnp.where(row == 7, jnp.where(lane >= 96, 0.0, rot(down, 96, 1)), down)
    return up + down


def slabs(u):
    return u[:-2], u[1:-1], u[2:]


def ring_sum(u):
    below, above = beside(u, 2)
    return neighbours(slabs(u), slabs(below + above), rows_beside)


def ring_apply(v, k, diag, half):
    k, k_below, k_above = k
    below, above = beside(v, 2)
    s1 = neighbours(slabs(v), slabs(below + above), rows_beside)
    s2 = neighbours(slabs(k * v), slabs(k_below * below + k_above * above), rows_beside)
    return diag * v[1:-1] - half * (k[1:-1] * s1 + s2)


def cut_planes(k, lo, hi):
    return tuple(part[lo:hi] for part in k)


def dot(a, b):
    return lax.dot_general(a, b, (((1,), (0,)), ((), ())), precision=lax.Precision.HIGHEST, preferred_element_type=F32)


def ring_map(fine_of, coarse_cut, transpose=False):
    f_dim = 1 if transpose else 0
    i, j = iota((128, 128), f_dim), iota((128, 128), 1 - f_dim)
    return ((fine_of(i) >> 1) == jnp.where(j < coarse_cut, j, j - 128)).astype(F32)


def cut(c):
    return lambda i: jnp.where(i < c, i, i - 128)


def main_z(i):
    return i


def inner_z(i):
    return jnp.where(jnp.logical_and(i >= 4, i < 124), i, 4096)


def strip_z(i):
    r = i & 31
    return jnp.where(r < 16, r + 120, r - 24)


def outer_z(i):
    r = i & 31
    return jnp.where(jnp.logical_or(r < 4, r >= 28), 4096, strip_z(i))


def halve_rows(ref, n):
    return ref[pl.ds(0, n, stride=2), :] + ref[pl.ds(1, n, stride=2), :]


def double_rows(ref, x):
    n = x.shape[0]
    ref[pl.ds(0, n, stride=2), :] = x
    ref[pl.ds(1, n, stride=2), :] = x


def kernel(
    nw, nz, f_hbm, k_hbm, l_hbm, out_ref,
    km, ks, pkm, pks, kbm, kbs, kam, kas, fm, fs, lm, ls, dgm, dgs, dm, ds_,
    avm, avs, apm, aps, aqm, aqs, arm, ars, bvm, bvs, bpm, bps, bqm, bqs, brm, brs, tm, ts, tlm, tls,
    pack0, rs0, kd1, kd1x, gg1, gg1x, pv1, rsv1, vv1, vv1x,
    k1l, k1, dg1, f1, va1, t1, kd2, kd2x, gl2, gl2x, k2, dg2, f2, l2, t2, t3, hello, loc_sem, send_sem, recv_sem,
):
    w, z = lax.axis_index("wide"), lax.axis_index("narrow")

    def device(a, b):
        return (lax.rem(w + (a + nw), nw), lax.rem(z + (b + nz), nz))

    def in_grid(a, b):
        ok = jnp.logical_and(w + a >= 0, w + a < nw)
        return ok if b == 0 else jnp.logical_and(ok, jnp.logical_and(z + b >= 0, z + b < nz))

    has_left, has_right = (z > 0).astype(jnp.int32), (z < nz - 1).astype(jnp.int32)

    def inside(step):
        return jnp.logical_and(w + step >= 0, w + step < nw).astype(jnp.int32)

    class Message:
        def __init__(self, n, src, dst, a, b):
            self.to, self.origin = (a, b), (-a, -b)
            self.copy = pltpu.make_async_remote_copy(
                src_ref=src, dst_ref=dst, send_sem=send_sem.at[n], recv_sem=recv_sem.at[n],
                device_id=device(a, b), device_id_type=MESH,
            )
            pl.when(in_grid(*self.to))(self.copy.start)

        def arrived(self):
            pl.when(in_grid(*self.origin))(self.copy.wait_recv)

        def left(self):
            pl.when(in_grid(*self.to))(self.copy.wait_send)

    started = []

    def send(src, dst, a, b):
        started.append(Message(len(started), src, dst, a, b))
        return started[-1]

    def loop(lo, hi, body):
        for i in range(lo, hi):
            body(i)

    lane, row = lanes(), iota((8, 128), 0)
    group, place = lane >> 5, lane & 31

    for ref in (rs0, rsv1, kd1x, gg1x, vv1x, kd2x, gl2x):
        ref[...] = jnp.zeros_like(ref)

    def clear(k_planes, planes, v_plane):
        def body():
            km[k_planes] = jnp.zeros((4, 32, 128), F32)
            fm[planes] = jnp.zeros((2, 32, 128), F32)
            lm[planes] = jnp.zeros((2, 32, 128), F32)
            bvm[v_plane] = jnp.zeros((32, 128), F32)
            bvs[v_plane] = jnp.zeros((8, 128), F32)

        return body

    pl.when(w == 0)(clear(slice(0, 4), slice(0, 2), 0))
    pl.when(w == nw - 1)(clear(slice(12, 16), slice(10, 12), 11))

    barrier = pltpu.get_barrier_semaphore()

    def greet(a, b):
        def body():
            pl.semaphore_signal(barrier, inc=1, device_id=device(a, b), device_id_type=MESH)

        return body

    for a, b in FAR:
        if b >= 0:
            pl.when(in_grid(a, b))(greet(a, b))
    loads = []
    for n, (src, dst) in enumerate(((k_hbm, km.at[4:12]), (f_hbm, fm.at[2:10]), (l_hbm, lm.at[2:10]))):
        loads.append(pltpu.make_async_copy(src, dst, loc_sem.at[n]))
        loads[-1].start()

    def own_strip(m):
        out = rot(m[0:8, :], 8, 1)
        for t in range(1, 4):
            out = jnp.where(group == t, rot(m[8 * t : 8 * t + 8, :], 32 * t + 8, 1), out)
        return jnp.where(place < 16, out, rot(out, 16, 1))

    eighth = place >> 3
    even = (eighth & 1) == 0
    spot = (0, 16, 8, 24)

    def pack_strips(strips):
        left, right = jnp.zeros((8, 128), F32), jnp.zeros((8, 128), F32)
        for x, s in enumerate(strips):
            r = rot(s, spot[x] - 24, 1)
            left = jnp.where(eighth == spot[x] // 8, r, left)
            right = jnp.where(eighth == (spot[x] // 8 + 1) % 4, r, right)
        return left, rot(right, 32, 1)

    def merge(rs, n):
        out = {}
        for step, half in ((0, 1), (1, 0), (1, 1), (2, 0)):
            left, right = rs[step, 0, half, n], rs[step, 1, half, n]
            out[step, half] = (jnp.where(even, left, right), jnp.where(even, right, left))
        return out

    own_lanes = jnp.logical_or(place < 8, place >= 24)

    def whole_strip(own, merged, x):
        at = x % 8
        halo = merged[(x + 8) // 8, at // 4][at % 4 // 2]
        return jnp.where(own_lanes, own, rot(halo, 8 - spot[at % 4], 1))

    def count(pos, reach, size):
        return jnp.minimum(pos, reach) + 1 + jnp.minimum(size - 1 - pos, reach)

    pl.semaphore_wait(barrier, count(w, 4, nw) * (1 + has_left) - 1)

    def say_hello():
        pl.semaphore_signal(hello, inc=1, device_id=device(0, -1), device_id_type=MESH)

    pl.when(z > 0)(say_hello)

    def send_planes(src_lo, dst_hi, src_hi, dst_lo):
        return [send(src_hi, dst_lo, 1, 0), send(src_lo, dst_hi, -1, 0)]

    def send_sides(pack, rs):
        return [send(pack.at[0 if b < 0 else 1], rs.at[1 - a, 0 if b < 0 else 1], a, b) for a, b in SIDES]

    def send_far(src, dst):
        return [send(src, dst.at[4 - a, 1 - b], a, b) for a, b in FAR]

    e0k = send_planes(k_hbm.at[0:4], km.at[12:16], k_hbm.at[4:8], km.at[0:4])
    e0f = send_planes(f_hbm.at[0:2], fm.at[10:12], f_hbm.at[6:8], fm.at[0:2])
    e0l = send_planes(l_hbm.at[0:2], lm.at[10:12], l_hbm.at[6:8], lm.at[0:2])

    for n, (ref, strip, off) in enumerate(((km, ks, 4), (fm, fs, 2), (lm, ls, 2))):
        loads[n].wait()
        own = [own_strip(ref[x + off]) for x in range(8)]
        for x in range(8):
            strip[x + off] = own[x]
        for half in range(2):
            pack0[0, half, n], pack0[1, half, n] = pack_strips(own[4 * half : 4 * half + 4])

    def send_strips(b):
        side = 0 if b < 0 else 1
        out = []
        for a in (0, -1, 1):
            if a == 0:
                out.append(send(pack0.at[side], rs0.at[1, side], a, b))
            else:
                half = 0 if a < 0 else 1
                out.append(send(pack0.at[side, half], rs0.at[1 - a, side, half], a, b))
        return out

    e0s = send_strips(-1)
    def hear_hello():
        pl.semaphore_wait(hello, 1)

    pl.when(z < nz - 1)(hear_hello)
    e0s += send_strips(1)

    def three(ref, i):
        return ref[i - 1], ref[i], ref[i + 1]

    field_a = ((avm, apm, aqm, arm), (avs, aps, aqs, ars))
    field_b = ((bvm, bpm, bqm, brm), (bvs, bps, bqs, brs))
    on_main = ((fm, dgm, dm), (km, kbm, kam), rows_beside)
    on_strip = ((fs, dgs, ds_), (ks, kbs, kas), rows_strip)

    def ready(field, part, i, value):
        v, p, q, r = field
        k, k_below, k_above = part[1]
        v[i] = value
        below, above = beside(value)
        p[i], q[i] = below + above, value * k[i + 2]
        r[i] = below * k_below[i + 2] + above * k_above[i + 2]

    def resid(field, part, i):
        v, p, q, r = field
        (f, dg, _), (k, _, _), rows = part
        s1 = neighbours(three(v, i), three(p, i), rows)
        s2 = neighbours(three(q, i), three(r, i), rows)
        return f[i] - dg[i] * v[i] + 0.5 * (k[i + 2] * s1 + s2)

    def sweep(i, side):
        part = (on_main, on_strip)[side]
        source = field_a[side]
        ready(field_b[side], part, i, source[0][i] + part[0][2][i] * resid(source, part, i))

    def there0(i):
        return inside(-1) if i < 2 else inside(1) if i >= 10 else 1

    lane32 = iota((32, 128), 1)

    def first_main(i):
        around = neighbours(three(km, i + 2), three(pkm, i + 2), rows_beside)
        diag = lm[i] + 0.5 * (CALL * km[i + 2] + around)
        inv = OMEGA / diag
        if not 2 <= i < 10:
            inv = jnp.where(lane32 < 128 * there0(i), inv, 0.0)
        dgm[i], dm[i] = diag, inv
        ready(field_a[0], on_main, i, inv * fm[i])

    def first_strip(i):
        there = there0(i)
        around = neighbours(three(ks, i + 2), three(pks, i + 2), rows_strip)
        diag = ls[i] + 0.5 * (CALL * ks[i + 2] + around)
        keep = jnp.logical_or(place < (8 + 8 * has_right) * there, place >= 32 - (8 + 8 * has_left) * there)
        inv = jnp.where(keep, OMEGA / diag, 0.0)
        dgs[i], ds_[i] = diag, inv
        ready(field_a[1], on_strip, i, inv * fs[i])

    def spread(s):
        return jnp.concatenate([jnp.where(group == t, s, 0.0) for t in range(4)], axis=0)

    def k_main(p):
        below, above = beside(km[p])
        kbm[p], kam[p], pkm[p] = below, above, below + above

    def k_pair(i):
        tm[32 * i : 32 * i + 32, :] = km[2 * i] + km[2 * i + 1]

    rm01, rs01 = ring_map(inner_z, 96), ring_map(outer_z, 96)
    r12, r23 = ring_map(cut(96), 64), ring_map(cut(64), 64)

    for p in range(4, 12):
        k_main(p)
    for i in range(2, 6):
        k_pair(i)
    for i in range(4):
        tlm[32 * i : 32 * i + 32, :] = lm[2 * i + 2] + lm[2 * i + 3]
    loop(3, 9, first_main)
    for i in range(4, 8):
        sweep(i, 0)
    early = {i: resid(field_b[0], on_main, i) for i in (5, 6)}

    for c in e0k + e0s:
        c.arrived()
    merged = merge(rs0, 0)
    for p in range(16):
        own = ks[p] if 4 <= p < 12 else own_strip(km[p])
        ks[p] = whole_strip(own, merged, p - 4)

    for p in range(16):
        below, above = beside(ks[p])
        kbs[p], kas[p], pks[p] = below, above, below + above
    for p in (1, 2, 3, 12, 13, 14):
        k_main(p)
    for i in (0, 1, 6, 7):
        k_pair(i)
    for i in range(8):
        ts[32 * i : 32 * i + 32, :] = spread(ks[2 * i] + ks[2 * i + 1])

    coarse = dot(halve_rows(tm, 128), rm01) + dot(halve_rows(ts, 128), rs01)
    k1l[...] = (0.125 * coarse).reshape(8, 16, 128)

    for c in e0f + e0l:
        c.arrived()
    for n, (ref, strip) in ((1, (fm, fs)), (2, (lm, ls))):
        merged = merge(rs0, n)
        for p in range(12):
            own = strip[p] if 2 <= p < 10 else own_strip(ref[p])
            strip[p] = whole_strip(own, merged, p - 2)

    for i in range(4):
        tls[32 * i : 32 * i + 32, :] = spread(ls[2 * i + 2] + ls[2 * i + 3])
    l1 = dot(halve_rows(tlm, 64), rm01) + dot(halve_rows(tls, 64), rs01)
    l1 = (0.125 * l1).reshape(4, 16, 128)
    own1 = k1l[2:6]
    half1 = 0.5 * 0.25
    diag1 = l1 + half1 * (CALL * own1 + ring_sum(k1l[1:7]))
    kd1[:, 0], kd1[:, 1] = own1, diag1
    ekd = send_planes(kd1.at[0:3], kd1x.at[1], kd1.at[1:4], kd1x.at[0])

    for i in (0, 1, 2, 9, 10, 11):
        first_main(i)
    loop(0, 12, first_strip)
    for i in (1, 2, 3, 8, 9, 10):
        sweep(i, 0)
    for i in range(1, 11):
        sweep(i, 1)
    for i in range(4):
        pair = [early[n] if n in early else resid(field_b[0], on_main, n) for n in (2 * i + 2, 2 * i + 3)]
        tm[32 * i : 32 * i + 32, :] = pair[0] + pair[1]
        pair = [resid(field_b[1], on_strip, n) for n in (2 * i + 2, 2 * i + 3)]
        ts[32 * i : 32 * i + 32, :] = spread(pair[0] + pair[1])
    rhs1 = dot(halve_rows(tm, 64), rm01) + dot(halve_rows(ts, 64), rs01)
    gg1[...] = (0.125 * rhs1).reshape(4, 16, 128)

    e1x = send_planes(gg1.at[0:2], gg1x.at[1], gg1.at[2:4], gg1x.at[0])

    kk = k1l[...]
    for i in range(4):
        t1[16 * i : 16 * i + 16, :] = kk[2 * i] + kk[2 * i + 1]
    k2l = (0.125 * dot(halve_rows(t1, 32), r12)).reshape(4, 8, 128)
    for i in range(2):
        t1[16 * i : 16 * i + 16, :] = l1[2 * i] + l1[2 * i + 1]
    l2own = (0.125 * dot(halve_rows(t1, 16), r12)).reshape(2, 8, 128)
    half2 = 0.5 * 0.0625
    diag2 = l2own + half2 * (CALL * k2l[1:3] + ring_sum(k2l))
    both = (k2l[1], k2l[2], diag2[0], diag2[1])
    low = jnp.where(lane < 32, both[0], rot(both[1], 32, 1))
    high = jnp.where(lane < 96, rot(both[2], 64, 1), rot(both[3], 96, 1))
    kd2[...] = jnp.where(lane < 64, low, high)
    l2sum = rot(l2own[0] + l2own[1], 64, 1)
    ekd2 = send_far(kd2, kd2x)

    evx = []
    for ref in (bvm, bvs):
        evx += [send(ref.at[8], ref.at[0], 1, 0), send(ref.at[3], ref.at[11], -1, 0)]

    def pack_sides1(arr):
        left, right = jnp.zeros((8, 128), F32), jnp.zeros((8, 128), F32)
        for x in range(4):
            for t in range(2):
                slot = 2 * x + t
                r = rot(arr[x, 8 * t : 8 * t + 8, :], 4 * slot, 1)
                left = jnp.where((lane >> 2) == slot, r, left)
                right = jnp.where((lane >> 2) == slot + 15, r, right)
        return left, right

    def fill1(ref, own, x_ref, rs):
        merged = [jnp.where(group == 0, rs[step, 0], rs[step, 1]) for step in range(3)]
        for p in range(10):
            x = p - 3
            for t in range(2):
                side = rot(merged[(x + 4) // 4], 64 - 4 * (2 * (x % 4) + t), 1)
                side = jnp.where(jnp.logical_or(lane < 68, lane >= 124), side, 0.0)
                rows = slice(8 * t, 8 * t + 8)
                center = x_ref[0, x + 3, rows, :] if x < 0 else x_ref[1, x - 4, rows, :] if x > 3 else own[x, rows, :]
                ref[p, 8 * t : 8 * t + 8, :] = jnp.where(lane < 64, center, side)

    for c in ekd + e1x:
        c.arrived()
    k1[0:3], k1[3:7], k1[7:10] = kd1x[0, :, 0], own1, kd1x[1, :, 0]
    dg1[0:2], dg1[2:6], dg1[6:8] = kd1x[0, 1:3, 1], diag1, kd1x[1, 0:2, 1]
    f1[0:2], f1[2:6], f1[6:8] = gg1x[0], gg1[...], gg1x[1]
    k1_all = k1[...]
    k1_all = (k1_all,) + beside(k1_all, 2)

    lane1 = iota((2, 16, 128), 2)

    def inverse1(lo, hi, step):
        there = inside(step)
        keep = jnp.logical_or(lane1 < (64 + 4 * has_right) * there, lane1 >= 128 - 4 * has_left * there)
        return jnp.where(keep, OMEGA / dg1[lo:hi], 0.0)

    def sweep1(v, depth, inv):
        kk = cut_planes(k1_all, 3 - depth, 7 + depth)
        lo, hi = 3 - depth, 5 + depth
        rest = f1[lo:hi] - ring_apply(v, kk, dg1[lo:hi], half1)
        return v[1:-1] + inv[lo:hi] * rest

    inv1 = jnp.concatenate([inverse1(0, 2, -1), inverse1(2, 4, 0), inverse1(4, 6, 0), inverse1(6, 8, 1)], axis=0)
    v = sweep1(inv1 * f1[...], 2, inv1)
    r = f1[2:6] - ring_apply(v, cut_planes(k1_all, 2, 8), dg1[2:6], half1)
    for i in range(2):
        t1[16 * i : 16 * i + 16, :] = r[2 * i] + r[2 * i + 1]
    rhs2 = (0.125 * dot(halve_rows(t1, 16), r12)).reshape(2, 8, 128)

    gl2[...] = jnp.where(lane < 32, rhs2[0], jnp.where(lane < 64, rot(rhs2[1], 32, 1), l2sum))
    e2 = send_far(gl2, gl2x)
    vv1[...] = v[1:5]
    pv1[0], pv1[1] = pack_sides1(v[1:5])
    ev1x = send_planes(vv1.at[0:3], vv1x.at[1], vv1.at[1:4], vv1x.at[0])
    ev1s = send_sides(pv1, rsv1)

    def around2(mine, ref, step):
        mid = mine if step == 4 else ref[step, 1]
        return mid, rot(ref[step, 2], 32, 1), rot(ref[step, 0], -32, 1)

    def near2(parts, n):
        mid, right, left = parts
        at = (lane - 32 * n) & 127
        side = jnp.where(at < 40, right, jnp.where(at >= 120, left, 0.0))
        return rot(jnp.where(at < 32, mid, side), -32 * n, 1)

    for c in ekd2:
        c.arrived()
    mine = kd2[...]
    for step in range(9):
        there = inside(step - 4)
        keep = jnp.logical_or(lane < (32 + 8 * has_right) * there, lane >= 128 - 8 * has_left * there)
        parts = around2(mine, kd2x, step)
        for x in range(2):
            k2[2 * step + x] = near2(parts, x)
            diag = near2(parts, 2 + x)
            dg2[2 * step + x] = diag
            t2[2 * step + x] = jnp.where(keep, OMEGA / diag, 0.0)

    def to_level3(pairs):
        n = len(pairs)
        for i, pair in enumerate(pairs):
            t1[8 * i : 8 * i + 8, :] = pair
        y = 0.125 * dot(halve_rows(t1, 4 * n), r23)
        for i in range(n):
            t3[i, 0:4, :] = y[4 * i : 4 * i + 4, :]
        return t3[0:n]

    k2_all = k2[...]
    k2_all = (k2_all,) + beside(k2_all, 2)
    t3[...] = jnp.zeros_like(t3)
    half3 = 0.5 * 0.015625
    k3 = to_level3([k2[2 * i] + k2[2 * i + 1] for i in range(9)])
    most3 = half3 * (CALL * k3[1:-1] + ring_sum(k3))

    for c in e2:
        c.arrived()
    mine = gl2[...]
    for step in range(9):
        parts = around2(mine, gl2x, step)
        for x in range(2):
            f2[2 * step + x] = near2(parts, x)
        l2[step] = near2(parts, 2)

    def sweep2(v, depth):
        lo, hi = 9 - depth, 9 + depth
        rest = f2[lo:hi] - ring_apply(v, cut_planes(k2_all, lo - 1, hi + 1), dg2[lo:hi], half2)
        return v[1:-1] + t2[lo:hi] * rest

    vb = sweep2(t2[...] * f2[...], 8)
    r = f2[2:16] - ring_apply(vb, cut_planes(k2_all, 1, 17), dg2[2:16], half2)
    l3 = to_level3([l2[i + 1] for i in range(7)])
    f3 = to_level3([r[2 * i] + r[2 * i + 1] for i in range(7)])
    diag3 = l3 + most3
    inv3 = []
    for i in range(7):
        there = inside(i - 3)
        keep = jnp.logical_or(lane < (16 + 4 * has_right) * there, lane >= 128 - 4 * has_left * there)
        inv3.append(jnp.where(jnp.logical_and(keep, row < 4), OMEGA / diag3[i], 0.0)[None])
    inv3 = jnp.concatenate(inv3, axis=0)
    v3 = inv3 * f3
    rest = f3[1:-1] - ring_apply(v3, cut_planes((k3,) + beside(k3, 2), 1, 8), diag3[1:-1], half3)
    v3 = v3[1:-1] + inv3[1:-1] * rest

    p32 = ring_map(cut(64), 64, True)
    wide3 = dot(v3.reshape(40, 128), p32)
    for i in range(5):
        double_rows(t1.at[8 * i : 8 * i + 8, :], wide3[8 * i : 8 * i + 4, :])
    e3 = t1[0:40, :].reshape(5, 8, 128)
    e3 = jnp.concatenate([e3[i // 2][None] for i in range(10)], axis=0)
    vb = vb[3:13] + e3
    vb = sweep2(vb, 4)
    vb = sweep2(vb, 3)

    for c in ev1x + ev1s:
        c.arrived()
    fill1(va1, vv1, vv1x, rsv1)
    p21 = ring_map(cut(96), 64, True)
    double_rows(tm.at[0:96, :], dot(vb.reshape(48, 128), p21))
    e2v = tm[0:96, :].reshape(6, 16, 128)
    inner = jnp.logical_or(lane < 68, lane >= 124)
    inner = jnp.concatenate([inner, inner], axis=0)
    v = [jnp.where(inner, va1[p] + e2v[(p - 3) // 2 + 2], 0.0)[None] for p in range(10)]
    v = sweep1(jnp.concatenate(v, axis=0), 3, inv1)
    v = sweep1(v, 2, inv1)

    e1 = v.reshape(96, 128)
    double_rows(tm.at[0:192, :], dot(e1, ring_map(main_z, 96, True)))
    double_rows(ts.at[0:192, :], dot(e1, ring_map(strip_z, 96, True)))
    for c in evx:
        c.arrived()
        c.left()
    def correct(i):
        at = 32 * (i // 2)
        m = bvm[i] + tm[at : at + 32, :]
        s = ts[at : at + 8, :]
        for t in range(1, 4):
            s = jnp.where(group == t, ts[at + 8 * t : at + 8 * t + 8, :], s)
        ready(field_a[0], on_main, i, m)
        ready(field_a[1], on_strip, i, bvs[i] + s)

    loop(0, 12, correct)
    for i in range(1, 11):
        sweep(i, 0)
        sweep(i, 1)

    def last(i):
        m = bvm[i] + dm[i] * resid(field_b[0], on_main, i)
        s = bvs[i] + ds_[i] * resid(field_b[1], on_strip, i)
        s = jnp.where(place < 8, s, rot(s, -16, 1))
        ends = jnp.concatenate([rot(s, 120 - 32 * t, 1) for t in range(4)], axis=0)
        out_ref[i - 2] = jnp.where(jnp.logical_or(lane32 < 4, lane32 >= 124), ends, m)

    loop(2, 10, last)
    for c in started:
        if not any(c is done for done in evx):
            c.left()


def solution(mesh):
    nw, nz = mesh.shape["wide"], mesh.shape["narrow"]

    def on_device(source, permeability, leakage):
        def vm(*shape):
            return pltpu.VMEM(shape, F32)

        def pair(n):
            return [vm(n, 32, 128), vm(n, 8, 128)]

        scratch = pair(16) * 4 + pair(12) * 4 + pair(12) * 8 + [vm(256, 128), vm(256, 128), vm(128, 128), vm(128, 128)]
        scratch += [vm(2, 2, 3, 8, 128), vm(3, 2, 2, 3, 8, 128)]
        scratch += [vm(4, 2, 16, 128), vm(2, 3, 2, 16, 128), vm(4, 16, 128), vm(2, 2, 16, 128)]
        scratch += [vm(2, 8, 128), vm(3, 2, 8, 128)]
        scratch += [vm(4, 16, 128), vm(2, 3, 16, 128)]
        scratch += [vm(8, 16, 128), vm(10, 16, 128), vm(8, 16, 128), vm(8, 16, 128), vm(10, 16, 128), vm(128, 128)]
        scratch += [vm(8, 128), vm(9, 3, 8, 128), vm(8, 128), vm(9, 3, 8, 128)]
        scratch += [vm(18, 8, 128), vm(18, 8, 128), vm(18, 8, 128), vm(9, 8, 128), vm(18, 8, 128), vm(9, 8, 128)]
        n = 12 + 2 + 2 + 26 + 4 + 26 + 8
        scratch += [pltpu.SemaphoreType.REGULAR, pltpu.SemaphoreType.DMA((3,)), pltpu.SemaphoreType.DMA((n,)), pltpu.SemaphoreType.DMA((n,))]

        def body(*refs):
            kernel(nw, nz, *refs)

        return pl.pallas_call(
            body,
            out_shape=pltpu.VMEM(source.shape, F32),
            in_specs=[pl.BlockSpec(memory_space=pltpu.HBM)] * 3,
            out_specs=pl.BlockSpec(memory_space=pltpu.VMEM),
            scratch_shapes=scratch,
            compiler_params=pltpu.CompilerParams(
                collective_id=0, has_side_effects=True, vmem_limit_bytes=60 * 2**20
            ),
            name="vcycle",
        )(source, permeability, leakage)

    spec = P("wide", None, "narrow")
    return jax.shard_map(on_device, mesh=mesh, in_specs=(spec, spec, spec), out_specs=spec, check_vma=False)
```

```python
import jax
import jax.numpy as jnp
from jax import lax
from jax.experimental import pallas as pl
from jax.experimental.pallas import tpu as pltpu
from jax.sharding import PartitionSpec as P

MESH = pl.DeviceIdType.MESH
OMEGA = 0.8
F32 = jnp.float32


def weight(a, b, c):
    n = a + b + c
    return (a * 1.0 + b * 0.7 + c * 0.4) / n * {1: 1.0, 2: 0.25, 3: 0.1}[n]


CX, CY, CZ = weight(1, 0, 0), weight(0, 1, 0), weight(0, 0, 1)
CXY, CXZ, CYZ, CXYZ = weight(1, 1, 0), weight(1, 0, 1), weight(0, 1, 1), weight(1, 1, 1)
CALL = 2 * (CX + CY + CZ) + 4 * (CXY + CXZ + CYZ) + 8 * CXYZ

SIDES = [(a, b) for b in (-1, 1) for a in (-1, 0, 1)]
FAR = [(a, b) for n in (4, 3, 2, 1, 0) for a in sorted({-n, n}) for b in (-1, 1, 0) if (a, b) != (0, 0)]


def iota(shape, dim):
    return lax.broadcasted_iota(jnp.int32, shape, dim)


def lanes():
    return iota((8, 128), 1)


def rot(x, shift, axis):
    shift %= x.shape[axis]
    return x if shift == 0 else pltpu.roll(x, shift, axis)


def rows_beside(t):
    axis = t.ndim - 2
    n = t.shape[axis]
    row = iota(t.shape, axis)
    up = jnp.where(row == 0, 0.0, rot(t, 1, axis))
    down = jnp.where(row == n - 1, 0.0, rot(t, n - 1, axis))
    return up + down


def neighbours(u, p, y):
    x, xp = u[0] + u[2], p[0] + p[2]
    inner = CXY * x + CXYZ * xp + CY * u[1] + CYZ * p[1]
    return CX * x + CXZ * xp + CZ * p[1] + y(inner)


def beside(u, axis=1):
    return rot(u, 1, axis), rot(u, 127, axis)


def rows_strip(c):
    row, lane = iota((8, 128), 0), iota((8, 128), 1)
    up, down = rot(c, 1, 0), rot(c, 7, 0)
    up = jnp.where(row == 0, jnp.where(lane < 32, 0.0, rot(up, 32, 1)), up)
    down = jnp.where(row == 7, jnp.where(lane >= 96, 0.0, rot(down, 96, 1)), down)
    return up + down


def slabs(u):
    return u[:-2], u[1:-1], u[2:]


def ring_sum(u):
    below, above = beside(u, 2)
    return neighbours(slabs(u), slabs(below + above), rows_beside)


def ring_apply(v, k, diag, half):
    k, k_below, k_above = k
    below, above = beside(v, 2)
    s1 = neighbours(slabs(v), slabs(below + above), rows_beside)
    s2 = neighbours(slabs(k * v), slabs(k_below * below + k_above * above), rows_beside)
    return diag * v[1:-1] - half * (k[1:-1] * s1 + s2)


def cut_planes(k, lo, hi):
    return tuple(part[lo:hi] for part in k)


def dot(a, b):
    return lax.dot_general(a, b, (((1,), (0,)), ((), ())), precision=lax.Precision.HIGHEST, preferred_element_type=F32)


def ring_map(fine_of, coarse_cut):
    i, j = iota((128, 128), 0), iota((128, 128), 1)
    return ((fine_of(i) >> 1) == jnp.where(j < coarse_cut, j, j - 128)).astype(F32)


def cut(c):
    return lambda i: jnp.where(i < c, i, i - 128)


def inner_z(i):
    return jnp.where(jnp.logical_and(i >= 4, i < 124), i, 4096)


def strip_z(i):
    r = i & 31
    return jnp.where(r < 16, r + 120, r - 24)


def outer_z(i):
    r = i & 31
    return jnp.where(jnp.logical_or(r < 4, r >= 28), 4096, strip_z(i))


def from_lanes(x, index):
    index = index if isinstance(index, tuple) else (index,)
    tiles = [x[8 * i : 8 * i + 8] for i in range(x.shape[0] // 8)]
    tiles = [jnp.take_along_axis(t, index[i % len(index)], axis=1) for i, t in enumerate(tiles)]
    return jnp.concatenate(tiles, axis=0)


def halve_rows(ref, n):
    return ref[pl.ds(0, n, stride=2), :] + ref[pl.ds(1, n, stride=2), :]


def double_rows(ref, x):
    n = x.shape[0]
    ref[pl.ds(0, n, stride=2), :] = x
    ref[pl.ds(1, n, stride=2), :] = x


def kernel(
    nw, nz, f_hbm, k_hbm, l_hbm, out_ref,
    km, ks, pkm, pks, kbm, kbs, kam, kas, fm, fs, lm, ls, dgm, dgs, dm, ds_,
    avm, avs, apm, aps, aqm, aqs, arm, ars, bvm, bvs, bpm, bps, bqm, bqs, brm, brs, tm, ts, tlm, tls,
    pack0, rs0, kd1, kd1x, gg1, gg1x, pv1, rsv1, vv1, vv1x,
    k1l, k1, dg1, f1, va1, t1, kd2, kd2x, gl2, gl2x, k2, dg2, f2, l2, t2, t3, hello, loc_sem, send_sem, recv_sem,
):
    w, z = lax.axis_index("wide"), lax.axis_index("narrow")

    def device(a, b):
        return (w + a, z + b)

    def in_grid(a, b):
        ok = jnp.logical_and(w + a >= 0, w + a < nw)
        return ok if b == 0 else jnp.logical_and(ok, jnp.logical_and(z + b >= 0, z + b < nz))

    has_left, has_right = (z > 0).astype(jnp.int32), (z < nz - 1).astype(jnp.int32)

    def inside(step):
        return jnp.logical_and(w + step >= 0, w + step < nw).astype(jnp.int32)

    class Message:
        def __init__(self, n, src, dst, a, b):
            self.to, self.origin = (a, b), (-a, -b)
            self.copy = pltpu.make_async_remote_copy(
                src_ref=src, dst_ref=dst, send_sem=send_sem.at[n], recv_sem=recv_sem.at[n],
                device_id=device(a, b), device_id_type=MESH,
            )
            pl.when(in_grid(*self.to))(self.copy.start)

        def arrived(self):
            pl.when(in_grid(*self.origin))(self.copy.wait_recv)

        def left(self):
            pl.when(in_grid(*self.to))(self.copy.wait_send)

    started = []

    def send(src, dst, a, b):
        started.append(Message(len(started), src, dst, a, b))
        return started[-1]

    def loop(lo, hi, body):
        for i in range(lo, hi):
            body(i)

    lane, row = lanes(), iota((8, 128), 0)
    group, place = lane >> 5, lane & 31

    loads = []
    for n, (src, dst) in enumerate(((k_hbm, km.at[4:12]), (f_hbm, fm.at[2:10]), (l_hbm, lm.at[2:10]))):
        loads.append(pltpu.make_async_copy(src, dst, loc_sem.at[n]))
        loads[-1].start()

    for ref in (rs0, rsv1, kd1x, gg1x, vv1x, kd2x, gl2x):
        ref[...] = jnp.zeros_like(ref)

    def clear(k_planes, planes, v_plane):
        def body():
            km[k_planes] = jnp.zeros((4, 32, 128), F32)
            fm[planes] = jnp.zeros((2, 32, 128), F32)
            lm[planes] = jnp.zeros((2, 32, 128), F32)
            bvm[v_plane] = jnp.zeros((32, 128), F32)
            bvs[v_plane] = jnp.zeros((8, 128), F32)

        return body

    pl.when(w == 0)(clear(slice(0, 4), slice(0, 2), 0))
    pl.when(w == nw - 1)(clear(slice(12, 16), slice(10, 12), 11))

    barrier = pltpu.get_barrier_semaphore()

    def greet(a, b):
        def body():
            pl.semaphore_signal(barrier, inc=1, device_id=device(a, b), device_id_type=MESH)

        return body

    for a, b in FAR:
        if b >= 0:
            pl.when(in_grid(a, b))(greet(a, b))
    def own_strip(m):
        out = rot(m[0:8, :], 8, 1)
        for t in range(1, 4):
            out = jnp.where(group == t, rot(m[8 * t : 8 * t + 8, :], 32 * t + 8, 1), out)
        return jnp.where(place < 16, out, rot(out, 16, 1))

    eighth = place >> 3
    even = (eighth & 1) == 0
    spot = (0, 16, 8, 24)

    def pack_strips(strips):
        left, right = jnp.zeros((8, 128), F32), jnp.zeros((8, 128), F32)
        for x, s in enumerate(strips):
            r = rot(s, spot[x] - 24, 1)
            left = jnp.where(eighth == spot[x] // 8, r, left)
            right = jnp.where(eighth == (spot[x] // 8 + 1) % 4, r, right)
        return left, rot(right, 32, 1)

    def merge(rs, n):
        out = {}
        for step, half in ((0, 1), (1, 0), (1, 1), (2, 0)):
            left, right = rs[step, 0, half, n], rs[step, 1, half, n]
            out[step, half] = (jnp.where(even, left, right), jnp.where(even, right, left))
        return out

    own_lanes = jnp.logical_or(place < 8, place >= 24)

    def whole_strip(own, merged, x):
        at = x % 8
        halo = merged[(x + 8) // 8, at // 4][at % 4 // 2]
        return jnp.where(own_lanes, own, rot(halo, 8 - spot[at % 4], 1))

    def count(pos, reach, size):
        return jnp.minimum(pos, reach) + 1 + jnp.minimum(size - 1 - pos, reach)

    pl.semaphore_wait(barrier, count(w, 4, nw) * (1 + has_left) - 1)

    def say_hello():
        pl.semaphore_signal(hello, inc=1, device_id=device(0, -1), device_id_type=MESH)

    pl.when(z > 0)(say_hello)

    def send_planes(src_lo, dst_hi, src_hi, dst_lo):
        return [send(src_hi, dst_lo, 1, 0), send(src_lo, dst_hi, -1, 0)]

    def send_sides(pack, rs):
        return [send(pack.at[0 if b < 0 else 1], rs.at[1 - a, 0 if b < 0 else 1], a, b) for a, b in SIDES]

    def send_far(src, dst):
        return [send(src, dst.at[4 - a, 1 - b], a, b) for a, b in FAR]

    e0k = send_planes(k_hbm.at[0:4], km.at[12:16], k_hbm.at[4:8], km.at[0:4])
    e0f = send_planes(f_hbm.at[0:2], fm.at[10:12], f_hbm.at[6:8], fm.at[0:2])
    e0l = send_planes(l_hbm.at[0:2], lm.at[10:12], l_hbm.at[6:8], lm.at[0:2])

    for n, (ref, strip, off) in enumerate(((km, ks, 4), (fm, fs, 2), (lm, ls, 2))):
        loads[n].wait()
        own = [own_strip(ref[x + off]) for x in range(8)]
        for x in range(8):
            strip[x + off] = own[x]
        for half in range(2):
            pack0[0, half, n], pack0[1, half, n] = pack_strips(own[4 * half : 4 * half + 4])

    def send_strips(b):
        side = 0 if b < 0 else 1
        out = []
        for a in (0, -1, 1):
            if a == 0:
                out.append(send(pack0.at[side], rs0.at[1, side], a, b))
            else:
                half = 0 if a < 0 else 1
                out.append(send(pack0.at[side, half], rs0.at[1 - a, side, half], a, b))
        return out

    e0s = send_strips(-1)
    def hear_hello():
        pl.semaphore_wait(hello, 1)

    pl.when(z < nz - 1)(hear_hello)
    e0s += send_strips(1)

    def three(ref, i):
        return ref[i - 1], ref[i], ref[i + 1]

    field_a = ((avm, apm, aqm, arm), (avs, aps, aqs, ars))
    field_b = ((bvm, bpm, bqm, brm), (bvs, bps, bqs, brs))
    on_main = ((fm, dgm, dm), (km, kbm, kam), rows_beside)
    on_strip = ((fs, dgs, ds_), (ks, kbs, kas), rows_strip)

    def ready(field, part, i, value):
        v, p, q, r = field
        k, k_below, k_above = part[1]
        v[i] = value
        below, above = beside(value)
        p[i], q[i] = below + above, value * k[i + 2]
        r[i] = below * k_below[i + 2] + above * k_above[i + 2]

    def resid(field, part, i):
        v, p, q, r = field
        (f, dg, _), (k, _, _), rows = part
        s1 = neighbours(three(v, i), three(p, i), rows)
        s2 = neighbours(three(q, i), three(r, i), rows)
        return f[i] - dg[i] * v[i] + 0.5 * (k[i + 2] * s1 + s2)

    def sweep(i, side):
        part = (on_main, on_strip)[side]
        source = field_a[side]
        ready(field_b[side], part, i, source[0][i] + part[0][2][i] * resid(source, part, i))

    def there0(i):
        return inside(-1) if i < 2 else inside(1) if i >= 10 else 1

    lane32 = iota((32, 128), 1)

    def first_main(i):
        around = neighbours(three(km, i + 2), three(pkm, i + 2), rows_beside)
        diag = lm[i] + 0.5 * (CALL * km[i + 2] + around)
        inv = OMEGA / diag
        if not 2 <= i < 10:
            inv = jnp.where(lane32 < 128 * there0(i), inv, 0.0)
        dgm[i], dm[i] = diag, inv
        ready(field_a[0], on_main, i, inv * fm[i])

    def first_strip(i):
        there = there0(i)
        around = neighbours(three(ks, i + 2), three(pks, i + 2), rows_strip)
        diag = ls[i] + 0.5 * (CALL * ks[i + 2] + around)
        keep = jnp.logical_or(place < (8 + 8 * has_right) * there, place >= 32 - (8 + 8 * has_left) * there)
        inv = jnp.where(keep, OMEGA / diag, 0.0)
        dgs[i], ds_[i] = diag, inv
        ready(field_a[1], on_strip, i, inv * fs[i])

    def spread(s):
        return jnp.concatenate([jnp.where(group == t, s, 0.0) for t in range(4)], axis=0)

    def k_main(p):
        below, above = beside(km[p])
        kbm[p], kam[p], pkm[p] = below, above, below + above

    def k_pair(i):
        tm[32 * i : 32 * i + 32, :] = km[2 * i] + km[2 * i + 1]

    rm01, rs01 = ring_map(inner_z, 96), ring_map(outer_z, 96)
    r12, r23 = ring_map(cut(96), 64), ring_map(cut(64), 64)

    for p in range(4, 12):
        k_main(p)
    for i in range(2, 6):
        k_pair(i)
    for i in range(4):
        tlm[32 * i : 32 * i + 32, :] = lm[2 * i + 2] + lm[2 * i + 3]
    loop(3, 9, first_main)
    for i in range(4, 8):
        sweep(i, 0)
    early = {i: resid(field_b[0], on_main, i) for i in (5, 6)}

    for c in e0k + e0s:
        c.arrived()
    merged = merge(rs0, 0)
    for p in range(16):
        own = ks[p] if 4 <= p < 12 else own_strip(km[p])
        ks[p] = whole_strip(own, merged, p - 4)

    for p in range(16):
        below, above = beside(ks[p])
        kbs[p], kas[p], pks[p] = below, above, below + above
    for p in (1, 2, 3, 12, 13, 14):
        k_main(p)
    for i in (0, 1, 6, 7):
        k_pair(i)
    for i in range(8):
        ts[32 * i : 32 * i + 32, :] = spread(ks[2 * i] + ks[2 * i + 1])

    coarse = dot(halve_rows(tm, 128), rm01) + dot(halve_rows(ts, 128), rs01)
    k1l[...] = (0.125 * coarse).reshape(8, 16, 128)

    for c in e0f + e0l:
        c.arrived()
    for n, (ref, strip) in ((1, (fm, fs)), (2, (lm, ls))):
        merged = merge(rs0, n)
        for p in range(12):
            own = strip[p] if 2 <= p < 10 else own_strip(ref[p])
            strip[p] = whole_strip(own, merged, p - 2)

    for i in range(4):
        tls[32 * i : 32 * i + 32, :] = spread(ls[2 * i + 2] + ls[2 * i + 3])
    l1 = dot(halve_rows(tlm, 64), rm01) + dot(halve_rows(tls, 64), rs01)
    l1 = (0.125 * l1).reshape(4, 16, 128)
    own1 = k1l[2:6]
    half1 = 0.5 * 0.25
    diag1 = l1 + half1 * (CALL * own1 + ring_sum(k1l[1:7]))
    kd1[:, 0], kd1[:, 1] = own1, diag1
    ekd = send_planes(kd1.at[0:3], kd1x.at[1], kd1.at[1:4], kd1x.at[0])

    for i in (0, 1, 2, 9, 10, 11):
        first_main(i)
    loop(0, 12, first_strip)
    for i in (1, 2, 3, 8, 9, 10):
        sweep(i, 0)
    for i in range(1, 11):
        sweep(i, 1)
    for i in range(4):
        pair = [early[n] if n in early else resid(field_b[0], on_main, n) for n in (2 * i + 2, 2 * i + 3)]
        tm[32 * i : 32 * i + 32, :] = pair[0] + pair[1]
        pair = [resid(field_b[1], on_strip, n) for n in (2 * i + 2, 2 * i + 3)]
        pair = pair[0] + pair[1]
        ts[32 * i : 32 * i + 32, :] = jnp.concatenate([pair] * 4, axis=0)
    cell = jnp.where(lane < 96, 2 * lane, 2 * lane - 256)
    pairs = halve_rows(tm, 64)
    inner = from_lanes(pairs, cell & 127) + from_lanes(pairs, (cell + 1) & 127)
    at = jnp.where(cell >= 64, cell - 120, cell + 24) & 31
    tile = 32 * (row >> 2)
    even_at, odd_at = (tile + at, tile + 64 + at), (tile + at + 1, tile + 65 + at)
    pairs = halve_rows(ts, 64)
    outer = from_lanes(pairs, even_at) + from_lanes(pairs, odd_at)
    lane64 = iota((64, 128), 1)
    use_inner = jnp.logical_and(lane64 >= 2, lane64 < 62)
    use_outer = jnp.logical_or(lane64 < 68, lane64 >= 124)
    rhs1 = jnp.where(use_inner, inner, jnp.where(use_outer, outer, 0.0))
    gg1[...] = (0.125 * rhs1).reshape(4, 16, 128)

    e1x = send_planes(gg1.at[0:2], gg1x.at[1], gg1.at[2:4], gg1x.at[0])

    kk = k1l[...]
    for i in range(4):
        t1[16 * i : 16 * i + 16, :] = kk[2 * i] + kk[2 * i + 1]
    k2l = (0.125 * dot(halve_rows(t1, 32), r12)).reshape(4, 8, 128)
    for i in range(2):
        t1[16 * i : 16 * i + 16, :] = l1[2 * i] + l1[2 * i + 1]
    l2own = (0.125 * dot(halve_rows(t1, 16), r12)).reshape(2, 8, 128)
    half2 = 0.5 * 0.0625
    diag2 = l2own + half2 * (CALL * k2l[1:3] + ring_sum(k2l))
    both = (k2l[1], k2l[2], diag2[0], diag2[1])
    low = jnp.where(lane < 32, both[0], rot(both[1], 32, 1))
    high = jnp.where(lane < 96, rot(both[2], 64, 1), rot(both[3], 96, 1))
    kd2[...] = jnp.where(lane < 64, low, high)
    l2sum = rot(l2own[0] + l2own[1], 64, 1)
    ekd2 = send_far(kd2, kd2x)

    evx = []
    for ref in (bvm, bvs):
        evx += [send(ref.at[8], ref.at[0], 1, 0), send(ref.at[3], ref.at[11], -1, 0)]

    def pack_sides1(arr):
        left, right = jnp.zeros((8, 128), F32), jnp.zeros((8, 128), F32)
        for x in range(4):
            for t in range(2):
                slot = 2 * x + t
                r = rot(arr[x, 8 * t : 8 * t + 8, :], 4 * slot, 1)
                left = jnp.where((lane >> 2) == slot, r, left)
                right = jnp.where((lane >> 2) == slot + 15, r, right)
        return left, right

    def fill1(ref, own, x_ref, rs):
        merged = [jnp.where(group == 0, rs[step, 0], rs[step, 1]) for step in range(3)]
        for p in range(10):
            x = p - 3
            for t in range(2):
                side = rot(merged[(x + 4) // 4], 64 - 4 * (2 * (x % 4) + t), 1)
                side = jnp.where(jnp.logical_or(lane < 68, lane >= 124), side, 0.0)
                rows = slice(8 * t, 8 * t + 8)
                center = x_ref[0, x + 3, rows, :] if x < 0 else x_ref[1, x - 4, rows, :] if x > 3 else own[x, rows, :]
                ref[p, 8 * t : 8 * t + 8, :] = jnp.where(lane < 64, center, side)

    for c in ekd + e1x:
        c.arrived()
    k1[0:3], k1[3:7], k1[7:10] = kd1x[0, :, 0], own1, kd1x[1, :, 0]
    dg1[0:2], dg1[2:6], dg1[6:8] = kd1x[0, 1:3, 1], diag1, kd1x[1, 0:2, 1]
    f1[0:2], f1[2:6], f1[6:8] = gg1x[0], gg1[...], gg1x[1]
    k1_all = k1[...]
    k1_all = (k1_all,) + beside(k1_all, 2)

    lane1 = iota((2, 16, 128), 2)

    def inverse1(lo, hi, step):
        there = inside(step)
        keep = jnp.logical_or(lane1 < (64 + 4 * has_right) * there, lane1 >= 128 - 4 * has_left * there)
        return jnp.where(keep, OMEGA / dg1[lo:hi], 0.0)

    def sweep1(v, depth, inv):
        kk = cut_planes(k1_all, 3 - depth, 7 + depth)
        lo, hi = 3 - depth, 5 + depth
        rest = f1[lo:hi] - ring_apply(v, kk, dg1[lo:hi], half1)
        return v[1:-1] + inv[lo:hi] * rest

    inv1 = jnp.concatenate([inverse1(0, 2, -1), inverse1(2, 4, 0), inverse1(4, 6, 0), inverse1(6, 8, 1)], axis=0)
    v = sweep1(inv1 * f1[...], 2, inv1)
    r = f1[2:6] - ring_apply(v, cut_planes(k1_all, 2, 8), dg1[2:6], half1)
    for i in range(2):
        t1[16 * i : 16 * i + 16, :] = r[2 * i] + r[2 * i + 1]
    pairs = halve_rows(t1, 16)
    rhs2 = from_lanes(pairs, (2 * lane) & 127) + from_lanes(pairs, (2 * lane + 1) & 127)
    rhs2 = (0.125 * rhs2).reshape(2, 8, 128)

    gl2[...] = jnp.where(lane < 32, rhs2[0], jnp.where(lane < 64, rot(rhs2[1], 32, 1), l2sum))
    e2 = send_far(gl2, gl2x)
    vv1[...] = v[1:5]
    pv1[0], pv1[1] = pack_sides1(v[1:5])
    ev1x = send_planes(vv1.at[0:3], vv1x.at[1], vv1.at[1:4], vv1x.at[0])
    ev1s = send_sides(pv1, rsv1)

    def around2(mine, ref, step):
        mid = mine if step == 4 else ref[step, 1]
        return mid, rot(ref[step, 2], 32, 1), rot(ref[step, 0], -32, 1)

    def near2(parts, n):
        mid, right, left = parts
        at = (lane - 32 * n) & 127
        side = jnp.where(at < 40, right, jnp.where(at >= 120, left, 0.0))
        return rot(jnp.where(at < 32, mid, side), -32 * n, 1)

    for c in ekd2:
        c.arrived()
    mine = kd2[...]
    for step in range(9):
        there = inside(step - 4)
        keep = jnp.logical_or(lane < (32 + 8 * has_right) * there, lane >= 128 - 8 * has_left * there)
        parts = around2(mine, kd2x, step)
        for x in range(2):
            k2[2 * step + x] = near2(parts, x)
            diag = near2(parts, 2 + x)
            dg2[2 * step + x] = diag
            t2[2 * step + x] = jnp.where(keep, OMEGA / diag, 0.0)

    def to_level3(pairs):
        n = len(pairs)
        for i, pair in enumerate(pairs):
            t1[8 * i : 8 * i + 8, :] = pair
        y = 0.125 * dot(halve_rows(t1, 4 * n), r23)
        for i in range(n):
            t3[i, 0:4, :] = y[4 * i : 4 * i + 4, :]
        return t3[0:n]

    k2_all = k2[...]
    k2_all = (k2_all,) + beside(k2_all, 2)
    t3[...] = jnp.zeros_like(t3)
    half3 = 0.5 * 0.015625
    k3 = to_level3([k2[2 * i] + k2[2 * i + 1] for i in range(9)])
    most3 = half3 * (CALL * k3[1:-1] + ring_sum(k3))

    for c in e2:
        c.arrived()
    mine = gl2[...]
    for step in range(9):
        parts = around2(mine, gl2x, step)
        for x in range(2):
            f2[2 * step + x] = near2(parts, x)
        l2[step] = near2(parts, 2)

    def sweep2(v, depth):
        lo, hi = 9 - depth, 9 + depth
        rest = f2[lo:hi] - ring_apply(v, cut_planes(k2_all, lo - 1, hi + 1), dg2[lo:hi], half2)
        return v[1:-1] + t2[lo:hi] * rest

    vb = sweep2(t2[...] * f2[...], 8)
    r = f2[2:16] - ring_apply(vb, cut_planes(k2_all, 1, 17), dg2[2:16], half2)
    l3 = to_level3([l2[i + 1] for i in range(7)])
    f3 = []
    for i in range(7):
        pair = r[2 * i] + r[2 * i + 1]
        f3.append(from_lanes(pair, (2 * lane) & 127) + from_lanes(pair, (2 * lane + 1) & 127))
    t1[0:56, :] = jnp.concatenate(f3, axis=0)
    f3 = 0.125 * halve_rows(t1, 28)
    for i in range(7):
        t3[i, 0:4, :] = f3[4 * i : 4 * i + 4, :]
    f3 = t3[0:7]
    diag3 = l3 + most3
    inv3 = []
    for i in range(7):
        there = inside(i - 3)
        keep = jnp.logical_or(lane < (16 + 4 * has_right) * there, lane >= 128 - 4 * has_left * there)
        inv3.append(jnp.where(jnp.logical_and(keep, row < 4), OMEGA / diag3[i], 0.0)[None])
    inv3 = jnp.concatenate(inv3, axis=0)
    v3 = inv3 * f3
    rest = f3[1:-1] - ring_apply(v3, cut_planes((k3,) + beside(k3, 2), 1, 8), diag3[1:-1], half3)
    v3 = v3[1:-1] + inv3[1:-1] * rest

    wide3 = from_lanes(v3.reshape(40, 128), jnp.where(lane < 64, lane >> 1, ((lane - 128) >> 1) + 128))
    for i in range(5):
        double_rows(t1.at[8 * i : 8 * i + 8, :], wide3[8 * i : 8 * i + 4, :])
    e3 = t1[0:40, :].reshape(5, 8, 128)
    e3 = jnp.concatenate([e3[i // 2][None] for i in range(10)], axis=0)
    vb = vb[3:13] + e3
    vb = sweep2(vb, 4)
    vb = sweep2(vb, 3)

    for c in ev1x + ev1s:
        c.arrived()
    fill1(va1, vv1, vv1x, rsv1)
    wide2 = from_lanes(vb.reshape(48, 128), jnp.where(lane < 96, lane >> 1, ((lane - 128) >> 1) + 128))
    double_rows(tm.at[0:96, :], wide2)
    e2v = tm[0:96, :].reshape(6, 16, 128)
    inner = jnp.logical_or(lane < 68, lane >= 124)
    inner = jnp.concatenate([inner, inner], axis=0)
    v = [jnp.where(inner, va1[p] + e2v[(p - 3) // 2 + 2], 0.0)[None] for p in range(10)]
    v = sweep1(jnp.concatenate(v, axis=0), 3, inv1)
    v = sweep1(v, 2, inv1)

    e1 = v.reshape(96, 128)
    double_rows(tm.at[0:192, :], from_lanes(e1, lane >> 1))
    double_rows(ts.at[0:192, :], from_lanes(e1, (strip_z(lane) >> 1) & 127))
    for c in evx:
        c.arrived()
        c.left()
    def correct(i):
        at = 32 * (i // 2)
        m = bvm[i] + tm[at : at + 32, :]
        s = ts[at : at + 8, :]
        for t in range(1, 4):
            s = jnp.where(group == t, ts[at + 8 * t : at + 8 * t + 8, :], s)
        ready(field_a[0], on_main, i, m)
        ready(field_a[1], on_strip, i, bvs[i] + s)

    loop(0, 12, correct)
    for i in range(1, 11):
        sweep(i, 0)
        sweep(i, 1)

    def last(i):
        m = bvm[i] + dm[i] * resid(field_b[0], on_main, i)
        s = bvs[i] + ds_[i] * resid(field_b[1], on_strip, i)
        s = jnp.where(place < 8, s, rot(s, -16, 1))
        ends = jnp.concatenate([rot(s, 120 - 32 * t, 1) for t in range(4)], axis=0)
        out_ref[i - 2] = jnp.where(jnp.logical_or(lane32 < 4, lane32 >= 124), ends, m)

    loop(2, 10, last)
    for c in started:
        if not any(c is done for done in evx):
            c.left()


def solution(mesh):
    nw, nz = mesh.shape["wide"], mesh.shape["narrow"]

    def on_device(source, permeability, leakage):
        def vm(*shape):
            return pltpu.VMEM(shape, F32)

        def pair(n):
            return [vm(n, 32, 128), vm(n, 8, 128)]

        scratch = pair(16) * 4 + pair(12) * 4 + pair(12) * 8 + [vm(256, 128), vm(256, 128), vm(128, 128), vm(128, 128)]
        scratch += [vm(2, 2, 3, 8, 128), vm(3, 2, 2, 3, 8, 128)]
        scratch += [vm(4, 2, 16, 128), vm(2, 3, 2, 16, 128), vm(4, 16, 128), vm(2, 2, 16, 128)]
        scratch += [vm(2, 8, 128), vm(3, 2, 8, 128)]
        scratch += [vm(4, 16, 128), vm(2, 3, 16, 128)]
        scratch += [vm(8, 16, 128), vm(10, 16, 128), vm(8, 16, 128), vm(8, 16, 128), vm(10, 16, 128), vm(128, 128)]
        scratch += [vm(8, 128), vm(9, 3, 8, 128), vm(8, 128), vm(9, 3, 8, 128)]
        scratch += [vm(18, 8, 128), vm(18, 8, 128), vm(18, 8, 128), vm(9, 8, 128), vm(18, 8, 128), vm(9, 8, 128)]
        n = 12 + 2 + 2 + 26 + 4 + 26 + 8
        scratch += [pltpu.SemaphoreType.REGULAR, pltpu.SemaphoreType.DMA((3,)), pltpu.SemaphoreType.DMA((n,)), pltpu.SemaphoreType.DMA((n,))]

        def body(*refs):
            kernel(nw, nz, *refs)

        return pl.pallas_call(
            body,
            out_shape=pltpu.VMEM(source.shape, F32),
            in_specs=[pl.BlockSpec(memory_space=pltpu.HBM)] * 3,
            out_specs=pl.BlockSpec(memory_space=pltpu.VMEM),
            scratch_shapes=scratch,
            compiler_params=pltpu.CompilerParams(
                collective_id=0, has_side_effects=True, vmem_limit_bytes=60 * 2**20
            ),
            name="vcycle",
        )(source, permeability, leakage)

    spec = P("wide", None, "narrow")
    return jax.shard_map(on_device, mesh=mesh, in_specs=(spec, spec, spec), out_specs=spec, check_vma=False)
```

```python
import jax
import jax.numpy as jnp
from jax import lax
from jax.experimental import pallas as pl
from jax.experimental.pallas import tpu as pltpu
from jax.sharding import PartitionSpec as P

MESH = pl.DeviceIdType.MESH
OMEGA = 0.8
F32 = jnp.float32


def weight(a, b, c):
    n = a + b + c
    return (a * 1.0 + b * 0.7 + c * 0.4) / n * {1: 1.0, 2: 0.25, 3: 0.1}[n]


CX, CY, CZ = weight(1, 0, 0), weight(0, 1, 0), weight(0, 0, 1)
CXY, CXZ, CYZ, CXYZ = weight(1, 1, 0), weight(1, 0, 1), weight(0, 1, 1), weight(1, 1, 1)
CALL = 2 * (CX + CY + CZ) + 4 * (CXY + CXZ + CYZ) + 8 * CXYZ

SIDES = [(a, b) for b in (-1, 1) for a in (-1, 0, 1)]
FAR = [(a, b) for n in (4, 3, 2, 1, 0) for a in sorted({-n, n}) for b in (-1, 1, 0) if (a, b) != (0, 0)]


def iota(shape, dim):
    return lax.broadcasted_iota(jnp.int32, shape, dim)


def lanes():
    return iota((8, 128), 1)


def rot(x, shift, axis):
    shift %= x.shape[axis]
    return x if shift == 0 else pltpu.roll(x, shift, axis)


def rows_beside(t):
    axis = t.ndim - 2
    n = t.shape[axis]
    row = iota(t.shape, axis)
    up = jnp.where(row == 0, 0.0, rot(t, 1, axis))
    down = jnp.where(row == n - 1, 0.0, rot(t, n - 1, axis))
    return up + down


def neighbours(u, p, y):
    x, xp = u[0] + u[2], p[0] + p[2]
    inner = CXY * x + CXYZ * xp + CY * u[1] + CYZ * p[1]
    return CX * x + CXZ * xp + CZ * p[1] + y(inner)


def beside(u, axis=1):
    return rot(u, 1, axis), rot(u, 127, axis)


def rows_strip(c):
    row, lane = iota((8, 128), 0), iota((8, 128), 1)
    up, down = rot(c, 1, 0), rot(c, 7, 0)
    up = jnp.where(row == 0, jnp.where(lane < 32, 0.0, rot(up, 32, 1)), up)
    down = jnp.where(row == 7, jnp.where(lane >= 96, 0.0, rot(down, 96, 1)), down)
    return up + down


def slabs(u):
    return u[:-2], u[1:-1], u[2:]


def ring_sum(u):
    below, above = beside(u, 2)
    return neighbours(slabs(u), slabs(below + above), rows_beside)


def ring_apply(v, k, diag, half):
    k, k_below, k_above = k
    below, above = beside(v, 2)
    s1 = neighbours(slabs(v), slabs(below + above), rows_beside)
    s2 = neighbours(slabs(k * v), slabs(k_below * below + k_above * above), rows_beside)
    return diag * v[1:-1] - half * (k[1:-1] * s1 + s2)


def cut_planes(k, lo, hi):
    return tuple(part[lo:hi] for part in k)


def dot(a, b):
    return lax.dot_general(a, b, (((1,), (0,)), ((), ())), precision=lax.Precision.HIGHEST, preferred_element_type=F32)


def ring_map(fine_of, coarse_cut):
    i, j = iota((128, 128), 0), iota((128, 128), 1)
    return ((fine_of(i) >> 1) == jnp.where(j < coarse_cut, j, j - 128)).astype(F32)


def cut(c):
    return lambda i: jnp.where(i < c, i, i - 128)


def inner_z(i):
    return jnp.where(jnp.logical_and(i >= 4, i < 124), i, 4096)


def strip_z(i):
    r = i & 31
    return jnp.where(r < 16, r + 120, r - 24)


def outer_z(i):
    r = i & 31
    return jnp.where(jnp.logical_or(r < 4, r >= 28), 4096, strip_z(i))


def from_lanes(x, index):
    index = index if isinstance(index, tuple) else (index,)
    tiles = [x[8 * i : 8 * i + 8] for i in range(x.shape[0] // 8)]
    tiles = [jnp.take_along_axis(t, index[i % len(index)], axis=1) for i, t in enumerate(tiles)]
    return jnp.concatenate(tiles, axis=0)


def halve_rows(ref, n):
    return ref[pl.ds(0, n, stride=2), :] + ref[pl.ds(1, n, stride=2), :]


def double_rows(ref, x):
    n = x.shape[0]
    ref[pl.ds(0, n, stride=2), :] = x
    ref[pl.ds(1, n, stride=2), :] = x


def kernel(
    nw, nz, f_hbm, k_hbm, l_hbm, out_ref,
    km, ks, pkm, pks, kbm, kbs, kam, kas, fm, fs, lm, ls, dgm, dgs, dm, ds_,
    avm, avs, apm, aps, aqm, aqs, arm, ars, bvm, bvs, bpm, bps, bqm, bqs, brm, brs, tm, ts, tlm, tls,
    pack0, rs0, pv1, rsv1, vv1, vv1x,
    k1l, k1, dg1, f1, va1, t1, kd2, kd2x, gl2, gl2x, k2, dg2, f2, l2, t2, t3, hello, loc_sem, send_sem, recv_sem,
):
    w, z = lax.axis_index("wide"), lax.axis_index("narrow")

    def device(a, b):
        return (w + a, z + b)

    def in_grid(a, b):
        ok = jnp.logical_and(w + a >= 0, w + a < nw)
        return ok if b == 0 else jnp.logical_and(ok, jnp.logical_and(z + b >= 0, z + b < nz))

    has_left, has_right = (z > 0).astype(jnp.int32), (z < nz - 1).astype(jnp.int32)

    def inside(step):
        return jnp.logical_and(w + step >= 0, w + step < nw).astype(jnp.int32)

    class Message:
        def __init__(self, n, src, dst, a, b):
            self.to, self.origin = (a, b), (-a, -b)
            self.copy = pltpu.make_async_remote_copy(
                src_ref=src, dst_ref=dst, send_sem=send_sem.at[n], recv_sem=recv_sem.at[n],
                device_id=device(a, b), device_id_type=MESH,
            )
            pl.when(in_grid(*self.to))(self.copy.start)

        def arrived(self):
            pl.when(in_grid(*self.origin))(self.copy.wait_recv)

        def left(self):
            pl.when(in_grid(*self.to))(self.copy.wait_send)

    started = []

    def send(src, dst, a, b):
        started.append(Message(len(started), src, dst, a, b))
        return started[-1]

    def loop(lo, hi, body):
        for i in range(lo, hi):
            body(i)

    lane, row = lanes(), iota((8, 128), 0)
    group, place = lane >> 5, lane & 31

    loads = []
    for n, (src, dst) in enumerate(((k_hbm, km.at[8:16]), (f_hbm, fm.at[6:14]), (l_hbm, lm.at[6:14]))):
        loads.append(pltpu.make_async_copy(src, dst, loc_sem.at[n]))
        loads[-1].start()

    for ref in (rs0, rsv1, vv1x, kd2x, gl2x):
        ref[...] = jnp.zeros_like(ref)

    def clear(k_planes, planes):
        def body():
            km[k_planes] = jnp.zeros((8, 32, 128), F32)
            fm[planes] = jnp.zeros((6, 32, 128), F32)
            lm[planes] = jnp.zeros((6, 32, 128), F32)

        return body

    pl.when(w == 0)(clear(slice(0, 8), slice(0, 6)))
    pl.when(w == nw - 1)(clear(slice(16, 24), slice(14, 20)))

    barrier = pltpu.get_barrier_semaphore()

    def greet(a, b):
        def body():
            pl.semaphore_signal(barrier, inc=1, device_id=device(a, b), device_id_type=MESH)

        return body

    for a, b in FAR:
        if b >= 0:
            pl.when(in_grid(a, b))(greet(a, b))
    def own_strip(m):
        out = rot(m[0:8, :], 8, 1)
        for t in range(1, 4):
            out = jnp.where(group == t, rot(m[8 * t : 8 * t + 8, :], 32 * t + 8, 1), out)
        return jnp.where(place < 16, out, rot(out, 16, 1))

    eighth = place >> 3
    even = (eighth & 1) == 0
    spot = (0, 16, 8, 24)

    def pack_strips(planes):
        left, right = jnp.zeros((8, 128), F32), jnp.zeros((8, 128), F32)
        for x, m in enumerate(planes):
            for t in range(4):
                r = rot(m[8 * t : 8 * t + 8, :], 32 * t + spot[x], 1)
                at = 4 * t + spot[x] // 8
                left = jnp.where((lane >> 3) == at, r, left)
                right = jnp.where((lane >> 3) == (at - 1) % 16, r, right)
        return left, rot(right, 16, 1)

    def merge(rs, n):
        out = {}
        for step, half in [(step, half) for step in range(3) for half in range(2)]:
            left, right = rs[step, 0, half, n], rs[step, 1, half, n]
            out[step, half] = (jnp.where(even, left, right), jnp.where(even, right, left))
        return out

    own_lanes = jnp.logical_or(place < 8, place >= 24)

    def whole_strip(own, merged, x):
        at = x % 8
        halo = merged[(x + 8) // 8, at // 4][at % 4 // 2]
        return jnp.where(own_lanes, own, rot(halo, 8 - spot[at % 4], 1))

    def count(pos, reach, size):
        return jnp.minimum(pos, reach) + 1 + jnp.minimum(size - 1 - pos, reach)

    pl.semaphore_wait(barrier, count(w, 4, nw) * (1 + has_left) - 1)

    def say_hello():
        pl.semaphore_signal(hello, inc=1, device_id=device(0, -1), device_id_type=MESH)

    pl.when(z > 0)(say_hello)

    def send_planes(src_lo, dst_hi, src_hi, dst_lo):
        return [send(src_hi, dst_lo, 1, 0), send(src_lo, dst_hi, -1, 0)]

    def send_sides(pack, rs):
        return [send(pack.at[0 if b < 0 else 1], rs.at[1 - a, 0 if b < 0 else 1], a, b) for a, b in SIDES]

    def send_far(src, dst):
        return [send(src, dst.at[4 - a, 1 - b], a, b) for a, b in FAR]

    e0k = send_planes(k_hbm, km.at[16:24], k_hbm, km.at[0:8])

    for load in loads:
        load.wait()
    for n, (ref, off) in enumerate(((km, 8), (fm, 6), (lm, 6))):
        for half in range(2):
            planes = [ref[x + off] for x in range(4 * half, 4 * half + 4)]
            pack0[0, half, n], pack0[1, half, n] = pack_strips(planes)

    def send_strips(b):
        side = 0 if b < 0 else 1
        return [send(pack0.at[side], rs0.at[1 - a, side], a, b) for a in (0, -1, 1)]

    e0s = send_strips(-1)
    e0f = send_planes(f_hbm.at[0:6], fm.at[14:20], f_hbm.at[2:8], fm.at[0:6])
    e0l = send_planes(l_hbm.at[0:6], lm.at[14:20], l_hbm.at[2:8], lm.at[0:6])
    def hear_hello():
        pl.semaphore_wait(hello, 1)

    pl.when(z < nz - 1)(hear_hello)
    e0s += send_strips(1)

    def three(ref, i):
        return ref[i - 1], ref[i], ref[i + 1]

    field_a = ((avm, apm, aqm, arm), (avs, aps, aqs, ars))
    field_b = ((bvm, bpm, bqm, brm), (bvs, bps, bqs, brs))
    on_main = ((fm, dgm, dm), (km, kbm, kam), rows_beside)
    on_strip = ((fs, dgs, ds_), (ks, kbs, kas), rows_strip)

    def ready(field, part, i, value):
        v, p, q, r = field
        k, k_below, k_above = part[1]
        v[i] = value
        below, above = beside(value)
        p[i], q[i] = below + above, value * k[i + 2]
        r[i] = below * k_below[i + 2] + above * k_above[i + 2]

    def resid(field, part, i):
        v, p, q, r = field
        (f, dg, _), (k, _, _), rows = part
        s1 = neighbours(three(v, i), three(p, i), rows)
        s2 = neighbours(three(q, i), three(r, i), rows)
        return f[i] - dg[i] * v[i] + 0.5 * (k[i + 2] * s1 + s2)

    def sweep(i, side):
        part = (on_main, on_strip)[side]
        source = field_a[side]
        ready(field_b[side], part, i, source[0][i] + part[0][2][i] * resid(source, part, i))

    def there0(i):
        return inside(-1) if i < 6 else inside(1) if i >= 14 else 1

    lane32 = iota((32, 128), 1)

    def first_main(i):
        around = neighbours(three(km, i + 2), three(pkm, i + 2), rows_beside)
        diag = lm[i] + 0.5 * (CALL * km[i + 2] + around)
        inv = OMEGA / diag
        if not 6 <= i < 14:
            inv = jnp.where(lane32 < 128 * there0(i), inv, 0.0)
        dgm[i], dm[i] = diag, inv
        ready(field_a[0], on_main, i, inv * fm[i])

    def first_strip(i):
        there = there0(i)
        around = neighbours(three(ks, i + 2), three(pks, i + 2), rows_strip)
        diag = ls[i] + 0.5 * (CALL * ks[i + 2] + around)
        keep = jnp.logical_or(place < (8 + 8 * has_right) * there, place >= 32 - (8 + 8 * has_left) * there)
        inv = jnp.where(keep, OMEGA / diag, 0.0)
        dgs[i], ds_[i] = diag, inv
        ready(field_a[1], on_strip, i, inv * fs[i])

    def spread(s):
        return jnp.concatenate([jnp.where(group == t, s, 0.0) for t in range(4)], axis=0)

    def k_main(p):
        below, above = beside(km[p])
        kbm[p], kam[p], pkm[p] = below, above, below + above

    def k_pair(i):
        tm[32 * i : 32 * i + 32, :] = km[2 * i] + km[2 * i + 1]

    rm01, rs01 = ring_map(inner_z, 96), ring_map(outer_z, 96)
    r12, r23 = ring_map(cut(96), 64), ring_map(cut(64), 64)

    for ref, held, off in ((km, ks, 8), (fm, fs, 6), (lm, ls, 6)):
        for x in range(8):
            held[x + off] = own_strip(ref[x + off])
    for p in range(8, 16):
        k_main(p)
    for i in range(4, 8):
        k_pair(i)
    for i in range(2, 6):
        tlm[32 * i : 32 * i + 32, :] = lm[2 * i + 2] + lm[2 * i + 3]
    loop(7, 13, first_main)
    for i in range(8, 12):
        sweep(i, 0)
    early = {i: resid(field_b[0], on_main, i) for i in (9, 10)}

    for c in e0k + e0s:
        c.arrived()
    merged = merge(rs0, 0)
    for p in range(24):
        own = ks[p] if 8 <= p < 16 else own_strip(km[p])
        ks[p] = whole_strip(own, merged, p - 8)

    for p in range(24):
        below, above = beside(ks[p])
        kbs[p], kas[p], pks[p] = below, above, below + above
    for p in (*range(1, 8), *range(16, 23)):
        k_main(p)
    for i in (0, 1, 2, 3, 8, 9, 10, 11):
        k_pair(i)
    for i in range(12):
        ts[32 * i : 32 * i + 32, :] = spread(ks[2 * i] + ks[2 * i + 1])

    coarse = dot(halve_rows(tm, 192), rm01) + dot(halve_rows(ts, 192), rs01)
    k1l[...] = (0.125 * coarse).reshape(12, 16, 128)

    kk = k1l[2:10]
    for i in range(4):
        t1[16 * i : 16 * i + 16, :] = kk[2 * i] + kk[2 * i + 1]
    k2l = (0.125 * dot(halve_rows(t1, 32), r12)).reshape(4, 8, 128)
    for c in e0f + e0l:
        c.arrived()
    for n, (ref, strip) in ((1, (fm, fs)), (2, (lm, ls))):
        merged = merge(rs0, n)
        for p in range(20):
            own = strip[p] if 6 <= p < 14 else own_strip(ref[p])
            strip[p] = whole_strip(own, merged, p - 6)

    for i in (0, 1, 6, 7):
        tlm[32 * i : 32 * i + 32, :] = lm[2 * i + 2] + lm[2 * i + 3]
    for i in range(8):
        tls[32 * i : 32 * i + 32, :] = spread(ls[2 * i + 2] + ls[2 * i + 3])
    l1 = dot(halve_rows(tlm, 128), rm01) + dot(halve_rows(tls, 128), rs01)
    l1 = (0.125 * l1).reshape(8, 16, 128)
    half1 = 0.5 * 0.25
    dg1[...] = l1 + half1 * (CALL * k1l[2:10] + ring_sum(k1l[1:11]))
    for i in range(2):
        t1[16 * i : 16 * i + 16, :] = l1[2 * i + 2] + l1[2 * i + 3]
    l2own = (0.125 * dot(halve_rows(t1, 16), r12)).reshape(2, 8, 128)
    half2 = 0.5 * 0.0625
    diag2 = l2own + half2 * (CALL * k2l[1:3] + ring_sum(k2l))
    both = (k2l[1], k2l[2], diag2[0], diag2[1])
    low = jnp.where(lane < 32, both[0], rot(both[1], 32, 1))
    high = jnp.where(lane < 96, rot(both[2], 64, 1), rot(both[3], 96, 1))
    kd2[...] = jnp.where(lane < 64, low, high)
    l2sum = rot(l2own[0] + l2own[1], 64, 1)
    for i in (*range(0, 7), *range(13, 20)):
        first_main(i)
    loop(0, 20, first_strip)
    ekd2 = send_far(kd2, kd2x)
    for i in (*range(1, 8), *range(12, 19)):
        sweep(i, 0)
    for i in range(1, 19):
        sweep(i, 1)
    for i in range(8):
        pair = [early[n] if n in early else resid(field_b[0], on_main, n) for n in (2 * i + 2, 2 * i + 3)]
        tm[32 * i : 32 * i + 32, :] = pair[0] + pair[1]
        pair = [resid(field_b[1], on_strip, n) for n in (2 * i + 2, 2 * i + 3)]
        pair = pair[0] + pair[1]
        ts[32 * i : 32 * i + 32, :] = jnp.concatenate([pair] * 4, axis=0)
    cell = jnp.where(lane < 96, 2 * lane, 2 * lane - 256)
    pairs = halve_rows(tm, 128)
    inner = from_lanes(pairs, cell & 127) + from_lanes(pairs, (cell + 1) & 127)
    at = jnp.where(cell >= 64, cell - 120, cell + 24) & 31
    tile = 32 * (row >> 2)
    even_at, odd_at = (tile + at, tile + 64 + at), (tile + at + 1, tile + 65 + at)
    pairs = halve_rows(ts, 128)
    outer = from_lanes(pairs, even_at) + from_lanes(pairs, odd_at)
    lane_all = iota((128, 128), 1)
    use_inner = jnp.logical_and(lane_all >= 2, lane_all < 62)
    use_outer = jnp.logical_or(lane_all < 68, lane_all >= 124)
    rhs1 = jnp.where(use_inner, inner, jnp.where(use_outer, outer, 0.0))
    f1[...] = (0.125 * rhs1).reshape(8, 16, 128)

    def pack_sides1(arr):
        left, right = jnp.zeros((8, 128), F32), jnp.zeros((8, 128), F32)
        for x in range(4):
            for t in range(2):
                slot = 2 * x + t
                r = rot(arr[x, 8 * t : 8 * t + 8, :], 4 * slot, 1)
                left = jnp.where((lane >> 2) == slot, r, left)
                right = jnp.where((lane >> 2) == slot + 15, r, right)
        return left, right

    def fill1(ref, own, x_ref, rs):
        merged = [jnp.where(group == 0, rs[step, 0], rs[step, 1]) for step in range(3)]
        for p in range(10):
            x = p - 3
            for t in range(2):
                side = rot(merged[(x + 4) // 4], 64 - 4 * (2 * (x % 4) + t), 1)
                side = jnp.where(jnp.logical_or(lane < 68, lane >= 124), side, 0.0)
                rows = slice(8 * t, 8 * t + 8)
                center = x_ref[0, x + 3, rows, :] if x < 0 else x_ref[1, x - 4, rows, :] if x > 3 else own[x, rows, :]
                ref[p, 8 * t : 8 * t + 8, :] = jnp.where(lane < 64, center, side)

    k1[...] = k1l[1:11]
    k1_all = k1[...]
    k1_all = (k1_all,) + beside(k1_all, 2)
    lane1 = iota((2, 16, 128), 2)

    def inverse1(lo, hi, step):
        there = inside(step)
        keep = jnp.logical_or(lane1 < (64 + 4 * has_right) * there, lane1 >= 128 - 4 * has_left * there)
        return jnp.where(keep, OMEGA / dg1[lo:hi], 0.0)

    def sweep1(v, depth, inv):
        kk = cut_planes(k1_all, 3 - depth, 7 + depth)
        lo, hi = 3 - depth, 5 + depth
        rest = f1[lo:hi] - ring_apply(v, kk, dg1[lo:hi], half1)
        return v[1:-1] + inv[lo:hi] * rest

    inv1 = jnp.concatenate([inverse1(0, 2, -1), inverse1(2, 4, 0), inverse1(4, 6, 0), inverse1(6, 8, 1)], axis=0)
    v = sweep1(inv1 * f1[...], 2, inv1)
    r = f1[2:6] - ring_apply(v, cut_planes(k1_all, 2, 8), dg1[2:6], half1)
    for i in range(2):
        t1[16 * i : 16 * i + 16, :] = r[2 * i] + r[2 * i + 1]
    pairs = halve_rows(t1, 16)
    rhs2 = from_lanes(pairs, (2 * lane) & 127) + from_lanes(pairs, (2 * lane + 1) & 127)
    rhs2 = (0.125 * rhs2).reshape(2, 8, 128)

    gl2[...] = jnp.where(lane < 32, rhs2[0], jnp.where(lane < 64, rot(rhs2[1], 32, 1), l2sum))
    e2 = send_far(gl2, gl2x)
    vv1[...] = v[1:5]
    pv1[0], pv1[1] = pack_sides1(v[1:5])
    ev1x = send_planes(vv1.at[0:3], vv1x.at[1], vv1.at[1:4], vv1x.at[0])
    ev1s = send_sides(pv1, rsv1)

    later = e2 + ev1x + ev1s
    for c in started:
        if not any(c is other for other in later):
            c.left()
    def around2(mine, ref, step):
        mid = mine if step == 4 else ref[step, 1]
        return mid, rot(ref[step, 2], 32, 1), rot(ref[step, 0], -32, 1)

    def near2(parts, n):
        mid, right, left = parts
        at = (lane - 32 * n) & 127
        side = jnp.where(at < 40, right, jnp.where(at >= 120, left, 0.0))
        return rot(jnp.where(at < 32, mid, side), -32 * n, 1)

    for c in ekd2:
        c.arrived()
    mine = kd2[...]
    for step in range(9):
        there = inside(step - 4)
        keep = jnp.logical_or(lane < (32 + 8 * has_right) * there, lane >= 128 - 8 * has_left * there)
        parts = around2(mine, kd2x, step)
        for x in range(2):
            k2[2 * step + x] = near2(parts, x)
            diag = near2(parts, 2 + x)
            dg2[2 * step + x] = diag
            t2[2 * step + x] = jnp.where(keep, OMEGA / diag, 0.0)

    def to_level3(pairs):
        n = len(pairs)
        for i, pair in enumerate(pairs):
            t1[8 * i : 8 * i + 8, :] = pair
        y = 0.125 * dot(halve_rows(t1, 4 * n), r23)
        for i in range(n):
            t3[i, 0:4, :] = y[4 * i : 4 * i + 4, :]
        return t3[0:n]

    k2_all = k2[...]
    k2_all = (k2_all,) + beside(k2_all, 2)
    t3[...] = jnp.zeros_like(t3)
    half3 = 0.5 * 0.015625
    k3 = to_level3([k2[2 * i] + k2[2 * i + 1] for i in range(9)])
    most3 = half3 * (CALL * k3[1:-1] + ring_sum(k3))

    for c in e2:
        c.arrived()
    mine = gl2[...]
    for step in range(9):
        parts = around2(mine, gl2x, step)
        for x in range(2):
            f2[2 * step + x] = near2(parts, x)
        l2[step] = near2(parts, 2)

    def sweep2(v, depth):
        lo, hi = 9 - depth, 9 + depth
        rest = f2[lo:hi] - ring_apply(v, cut_planes(k2_all, lo - 1, hi + 1), dg2[lo:hi], half2)
        return v[1:-1] + t2[lo:hi] * rest

    vb = sweep2(t2[...] * f2[...], 8)
    r = f2[2:16] - ring_apply(vb, cut_planes(k2_all, 1, 17), dg2[2:16], half2)
    l3 = to_level3([l2[i + 1] for i in range(7)])
    f3 = []
    for i in range(7):
        pair = r[2 * i] + r[2 * i + 1]
        f3.append(from_lanes(pair, (2 * lane) & 127) + from_lanes(pair, (2 * lane + 1) & 127))
    t1[0:56, :] = jnp.concatenate(f3, axis=0)
    f3 = 0.125 * halve_rows(t1, 28)
    for i in range(7):
        t3[i, 0:4, :] = f3[4 * i : 4 * i + 4, :]
    f3 = t3[0:7]
    diag3 = l3 + most3
    inv3 = []
    for i in range(7):
        there = inside(i - 3)
        keep = jnp.logical_or(lane < (16 + 4 * has_right) * there, lane >= 128 - 4 * has_left * there)
        inv3.append(jnp.where(jnp.logical_and(keep, row < 4), OMEGA / diag3[i], 0.0)[None])
    inv3 = jnp.concatenate(inv3, axis=0)
    v3 = inv3 * f3
    rest = f3[1:-1] - ring_apply(v3, cut_planes((k3,) + beside(k3, 2), 1, 8), diag3[1:-1], half3)
    v3 = v3[1:-1] + inv3[1:-1] * rest

    wide3 = from_lanes(v3.reshape(40, 128), jnp.where(lane < 64, lane >> 1, ((lane - 128) >> 1) + 128))
    for i in range(5):
        double_rows(t1.at[8 * i : 8 * i + 8, :], wide3[8 * i : 8 * i + 4, :])
    e3 = t1[0:40, :].reshape(5, 8, 128)
    e3 = jnp.concatenate([e3[i // 2][None] for i in range(10)], axis=0)
    vb = vb[3:13] + e3
    vb = sweep2(vb, 4)
    vb = sweep2(vb, 3)

    for c in ev1x + ev1s:
        c.arrived()
    fill1(va1, vv1, vv1x, rsv1)
    wide2 = from_lanes(vb.reshape(48, 128), jnp.where(lane < 96, lane >> 1, ((lane - 128) >> 1) + 128))
    double_rows(tm.at[0:96, :], wide2)
    e2v = tm[0:96, :].reshape(6, 16, 128)
    inner = jnp.logical_or(lane < 68, lane >= 124)
    inner = jnp.concatenate([inner, inner], axis=0)
    v = [jnp.where(inner, va1[p] + e2v[(p - 3) // 2 + 2], 0.0)[None] for p in range(10)]
    v = sweep1(jnp.concatenate(v, axis=0), 3, inv1)
    v = sweep1(v, 2, inv1)

    e1 = v.reshape(96, 128)
    double_rows(tm.at[0:192, :], from_lanes(e1, lane >> 1))
    double_rows(ts.at[0:192, :], from_lanes(e1, (strip_z(lane) >> 1) & 127))
    def correct(i):
        at = 32 * ((i - 4) // 2)
        m = bvm[i] + tm[at : at + 32, :]
        s = ts[at : at + 8, :]
        for t in range(1, 4):
            s = jnp.where(group == t, ts[at + 8 * t : at + 8 * t + 8, :], s)
        ready(field_a[0], on_main, i, m)
        ready(field_a[1], on_strip, i, bvs[i] + s)

    loop(4, 16, correct)
    for i in range(5, 15):
        sweep(i, 0)
        sweep(i, 1)

    def last(i):
        m = bvm[i] + dm[i] * resid(field_b[0], on_main, i)
        s = bvs[i] + ds_[i] * resid(field_b[1], on_strip, i)
        s = jnp.where(place < 8, s, rot(s, -16, 1))
        ends = jnp.concatenate([rot(s, 120 - 32 * t, 1) for t in range(4)], axis=0)
        out_ref[i - 6] = jnp.where(jnp.logical_or(lane32 < 4, lane32 >= 124), ends, m)

    loop(6, 14, last)
    for c in later:
        c.left()


def solution(mesh):
    nw, nz = mesh.shape["wide"], mesh.shape["narrow"]

    def on_device(source, permeability, leakage):
        def vm(*shape):
            return pltpu.VMEM(shape, F32)

        def pair(n):
            return [vm(n, 32, 128), vm(n, 8, 128)]

        scratch = pair(24) * 4 + pair(20) * 12 + [vm(384, 128), vm(384, 128), vm(256, 128), vm(256, 128)]
        scratch += [vm(2, 2, 3, 8, 128), vm(3, 2, 2, 3, 8, 128)]
        scratch += [vm(2, 8, 128), vm(3, 2, 8, 128)]
        scratch += [vm(4, 16, 128), vm(2, 3, 16, 128)]
        scratch += [vm(12, 16, 128), vm(10, 16, 128), vm(8, 16, 128), vm(8, 16, 128), vm(10, 16, 128), vm(128, 128)]
        scratch += [vm(8, 128), vm(9, 3, 8, 128), vm(8, 128), vm(9, 3, 8, 128)]
        scratch += [vm(18, 8, 128), vm(18, 8, 128), vm(18, 8, 128), vm(9, 8, 128), vm(18, 8, 128), vm(9, 8, 128)]
        n = 12 + 26 + 26 + 8
        scratch += [pltpu.SemaphoreType.REGULAR, pltpu.SemaphoreType.DMA((3,)), pltpu.SemaphoreType.DMA((n,)), pltpu.SemaphoreType.DMA((n,))]

        def body(*refs):
            kernel(nw, nz, *refs)

        return pl.pallas_call(
            body,
            out_shape=pltpu.VMEM(source.shape, F32),
            in_specs=[pl.BlockSpec(memory_space=pltpu.HBM)] * 3,
            out_specs=pl.BlockSpec(memory_space=pltpu.VMEM),
            scratch_shapes=scratch,
            compiler_params=pltpu.CompilerParams(
                collective_id=0, has_side_effects=True, vmem_limit_bytes=60 * 2**20
            ),
            name="vcycle",
        )(source, permeability, leakage)

    spec = P("wide", None, "narrow")
    return jax.shard_map(on_device, mesh=mesh, in_specs=(spec, spec, spec), out_specs=spec, check_vma=False)
```

```python
import jax
import jax.numpy as jnp
from jax import lax
from jax.experimental import pallas as pl
from jax.experimental.pallas import tpu as pltpu
from jax.sharding import PartitionSpec as P

MESH = pl.DeviceIdType.MESH
OMEGA = 0.8
F32 = jnp.float32


def weight(a, b, c):
    n = a + b + c
    return (a * 1.0 + b * 0.7 + c * 0.4) / n * {1: 1.0, 2: 0.25, 3: 0.1}[n]


CX, CY, CZ = weight(1, 0, 0), weight(0, 1, 0), weight(0, 0, 1)
CXY, CXZ, CYZ, CXYZ = weight(1, 1, 0), weight(1, 0, 1), weight(0, 1, 1), weight(1, 1, 1)
CALL = 2 * (CX + CY + CZ) + 4 * (CXY + CXZ + CYZ) + 8 * CXYZ

SIDES = [(a, b) for b in (-1, 1) for a in (-1, 0, 1)]
FAR = [(a, b) for n in (4, 3, 2, 1, 0) for a in sorted({-n, n}) for b in (-1, 1, 0) if (a, b) != (0, 0)]


def iota(shape, dim):
    return lax.broadcasted_iota(jnp.int32, shape, dim)


def lanes():
    return iota((8, 128), 1)


def rot(x, shift, axis):
    shift %= x.shape[axis]
    return x if shift == 0 else pltpu.roll(x, shift, axis)


def rows_beside(t):
    axis = t.ndim - 2
    n = t.shape[axis]
    row = iota(t.shape, axis)
    up = jnp.where(row == 0, 0.0, rot(t, 1, axis))
    down = jnp.where(row == n - 1, 0.0, rot(t, n - 1, axis))
    return up + down


def neighbours(u, p, y):
    x, xp = u[0] + u[2], p[0] + p[2]
    inner = CXY * x + CXYZ * xp + CY * u[1] + CYZ * p[1]
    return CX * x + CXZ * xp + CZ * p[1] + y(inner)


def beside(u, axis=1):
    return rot(u, 1, axis), rot(u, 127, axis)


def rows_strip(c):
    row, lane = iota((8, 128), 0), iota((8, 128), 1)
    up, down = rot(c, 1, 0), rot(c, 7, 0)
    up = jnp.where(row == 0, jnp.where(lane < 32, 0.0, rot(up, 32, 1)), up)
    down = jnp.where(row == 7, jnp.where(lane >= 96, 0.0, rot(down, 96, 1)), down)
    return up + down


def slabs(u):
    return u[:-2], u[1:-1], u[2:]


def ring_sum(u):
    below, above = beside(u, 2)
    return neighbours(slabs(u), slabs(below + above), rows_beside)


def ring_apply(v, k, diag, half):
    k, k_below, k_above = k
    below, above = beside(v, 2)
    s1 = neighbours(slabs(v), slabs(below + above), rows_beside)
    s2 = neighbours(slabs(k * v), slabs(k_below * below + k_above * above), rows_beside)
    return diag * v[1:-1] - half * (k[1:-1] * s1 + s2)


def cut_planes(k, lo, hi):
    return tuple(part[lo:hi] for part in k)


def dot(a, b):
    return lax.dot_general(a, b, (((1,), (0,)), ((), ())), precision=lax.Precision.HIGHEST, preferred_element_type=F32)


def ring_map(fine_of, coarse_cut):
    i, j = iota((128, 128), 0), iota((128, 128), 1)
    return ((fine_of(i) >> 1) == jnp.where(j < coarse_cut, j, j - 128)).astype(F32)


def cut(c):
    return lambda i: jnp.where(i < c, i, i - 128)


def inner_z(i):
    return jnp.where(jnp.logical_and(i >= 4, i < 124), i, 4096)


def strip_z(i):
    r = i & 31
    return jnp.where(r < 16, r + 120, r - 24)


def outer_z(i):
    r = i & 31
    return jnp.where(jnp.logical_or(r < 4, r >= 28), 4096, strip_z(i))


def from_lanes(x, index):
    index = index if isinstance(index, tuple) else (index,)
    tiles = [x[8 * i : 8 * i + 8] for i in range(x.shape[0] // 8)]
    tiles = [jnp.take_along_axis(t, index[i % len(index)], axis=1) for i, t in enumerate(tiles)]
    return jnp.concatenate(tiles, axis=0)


def halve_rows(ref, n):
    return ref[pl.ds(0, n, stride=2), :] + ref[pl.ds(1, n, stride=2), :]


def double_rows(ref, x):
    n = x.shape[0]
    ref[pl.ds(0, n, stride=2), :] = x
    ref[pl.ds(1, n, stride=2), :] = x


def kernel(
    nw, nz, f_hbm, k_hbm, l_hbm, out_ref,
    km, ks, pkm, pks, kbm, kbs, kam, kas, fm, fs, lm, ls, dgm, dgs, dm, ds_,
    avm, avs, apm, aps, aqm, aqs, arm, ars, bvm, bvs, bpm, bps, bqm, bqs, brm, brs, tm, ts, tlm, tls,
    pack0, rs0, pv1, rsv1, vv1, vv1x,
    k1l, k1, dg1, f1, va1, t1, kd2, kd2x, gl2, gl2x, k2, dg2, f2, l2, t2, t3, hello, loc_sem, send_sem, recv_sem,
):
    w, z = lax.axis_index("wide"), lax.axis_index("narrow")

    def device(a, b):
        return (w + a, z + b)

    def in_grid(a, b):
        ok = jnp.logical_and(w + a >= 0, w + a < nw)
        return ok if b == 0 else jnp.logical_and(ok, jnp.logical_and(z + b >= 0, z + b < nz))

    has_left, has_right = (z > 0).astype(jnp.int32), (z < nz - 1).astype(jnp.int32)

    def inside(step):
        return jnp.logical_and(w + step >= 0, w + step < nw).astype(jnp.int32)

    class Message:
        def __init__(self, n, src, dst, a, b):
            self.to, self.origin = (a, b), (-a, -b)
            self.copy = pltpu.make_async_remote_copy(
                src_ref=src, dst_ref=dst, send_sem=send_sem.at[n], recv_sem=recv_sem.at[n],
                device_id=device(a, b), device_id_type=MESH,
            )
            pl.when(in_grid(*self.to))(self.copy.start)

        def arrived(self):
            pl.when(in_grid(*self.origin))(self.copy.wait_recv)

        def left(self):
            pl.when(in_grid(*self.to))(self.copy.wait_send)

    started = []

    def send(src, dst, a, b):
        started.append(Message(len(started), src, dst, a, b))
        return started[-1]

    def loop(lo, hi, body):
        for i in range(lo, hi):
            body(i)

    lane, row = lanes(), iota((8, 128), 0)
    group, place = lane >> 5, lane & 31

    loads = []
    for n, (src, dst) in enumerate(((k_hbm, km.at[8:16]), (f_hbm, fm.at[6:14]), (l_hbm, lm.at[6:14]))):
        loads.append(pltpu.make_async_copy(src, dst, loc_sem.at[n]))
        loads[-1].start()

    for ref in (rs0, rsv1, vv1x, kd2x, gl2x):
        ref[...] = jnp.zeros_like(ref)

    def clear(k_planes, planes):
        def body():
            km[k_planes] = jnp.zeros((8, 32, 128), F32)
            fm[planes] = jnp.zeros((6, 32, 128), F32)
            lm[planes] = jnp.zeros((6, 32, 128), F32)

        return body

    pl.when(w == 0)(clear(slice(0, 8), slice(0, 6)))
    pl.when(w == nw - 1)(clear(slice(16, 24), slice(14, 20)))

    barrier = pltpu.get_barrier_semaphore()

    def greet(a, b):
        def body():
            pl.semaphore_signal(barrier, inc=1, device_id=device(a, b), device_id_type=MESH)

        return body

    for a, b in FAR:
        if b >= 0 and abs(a) <= 3:
            pl.when(in_grid(a, b))(greet(a, b))
    def own_strip(m):
        out = rot(m[0:8, :], 8, 1)
        for t in range(1, 4):
            out = jnp.where(group == t, rot(m[8 * t : 8 * t + 8, :], 32 * t + 8, 1), out)
        return jnp.where(place < 16, out, rot(out, 16, 1))

    eighth = place >> 3
    even = (eighth & 1) == 0
    spot = (0, 16, 8, 24)

    def pack_strips(planes):
        left, right = jnp.zeros((8, 128), F32), jnp.zeros((8, 128), F32)
        for x, m in enumerate(planes):
            for t in range(4):
                r = rot(m[8 * t : 8 * t + 8, :], 32 * t + spot[x], 1)
                at = 4 * t + spot[x] // 8
                left = jnp.where((lane >> 3) == at, r, left)
                right = jnp.where((lane >> 3) == (at - 1) % 16, r, right)
        return left, rot(right, 16, 1)

    def merge(rs, n):
        out = {}
        for step, half in [(step, half) for step in range(3) for half in range(2)]:
            left, right = rs[step, 0, half, n], rs[step, 1, half, n]
            out[step, half] = (jnp.where(even, left, right), jnp.where(even, right, left))
        return out

    own_lanes = jnp.logical_or(place < 8, place >= 24)

    def whole_strip(own, merged, x):
        at = x % 8
        halo = merged[(x + 8) // 8, at // 4][at % 4 // 2]
        return jnp.where(own_lanes, own, rot(halo, 8 - spot[at % 4], 1))

    def count(pos, reach, size):
        return jnp.minimum(pos, reach) + 1 + jnp.minimum(size - 1 - pos, reach)

    pl.semaphore_wait(barrier, count(w, 3, nw) * (1 + has_left) - 1)

    def say_hello():
        pl.semaphore_signal(hello, inc=1, device_id=device(0, -1), device_id_type=MESH)

    pl.when(z > 0)(say_hello)

    def send_planes(src_lo, dst_hi, src_hi, dst_lo):
        return [send(src_hi, dst_lo, 1, 0), send(src_lo, dst_hi, -1, 0)]

    def send_sides(pack, rs):
        return [send(pack.at[0 if b < 0 else 1], rs.at[1 - a, 0 if b < 0 else 1], a, b) for a, b in SIDES]

    def send_far(src, dst):
        return [send(src, dst.at[4 - a, 1 - b], a, b) for a, b in FAR]

    e0k = send_planes(k_hbm, km.at[16:24], k_hbm, km.at[0:8])

    for load in loads:
        load.wait()
    for n, (ref, off) in enumerate(((km, 8), (fm, 6), (lm, 6))):
        for half in range(2):
            planes = [ref[x + off] for x in range(4 * half, 4 * half + 4)]
            pack0[0, half, n], pack0[1, half, n] = pack_strips(planes)

    def send_strips(b):
        side = 0 if b < 0 else 1
        return [send(pack0.at[side], rs0.at[1 - a, side], a, b) for a in (0, -1, 1)]

    e0s = send_strips(-1)
    e0f = send_planes(f_hbm.at[0:6], fm.at[14:20], f_hbm.at[2:8], fm.at[0:6])
    e0l = send_planes(l_hbm.at[0:6], lm.at[14:20], l_hbm.at[2:8], lm.at[0:6])
    def hear_hello():
        pl.semaphore_wait(hello, 1)

    pl.when(z < nz - 1)(hear_hello)
    e0s += send_strips(1)

    def three(ref, i):
        return ref[i - 1], ref[i], ref[i + 1]

    field_a = ((avm, apm, aqm, arm), (avs, aps, aqs, ars))
    field_b = ((bvm, bpm, bqm, brm), (bvs, bps, bqs, brs))
    on_main = ((fm, dgm, dm), (km, kbm, kam), rows_beside)
    on_strip = ((fs, dgs, ds_), (ks, kbs, kas), rows_strip)

    def ready(field, part, i, value):
        v, p, q, r = field
        k, k_below, k_above = part[1]
        v[i] = value
        below, above = beside(value)
        p[i], q[i] = below + above, value * k[i + 2]
        r[i] = below * k_below[i + 2] + above * k_above[i + 2]

    def resid(field, part, i):
        v, p, q, r = field
        (f, dg, _), (k, _, _), rows = part
        s1 = neighbours(three(v, i), three(p, i), rows)
        s2 = neighbours(three(q, i), three(r, i), rows)
        return f[i] - dg[i] * v[i] + 0.5 * (k[i + 2] * s1 + s2)

    def sweep(i, side):
        part = (on_main, on_strip)[side]
        source = field_a[side]
        ready(field_b[side], part, i, source[0][i] + part[0][2][i] * resid(source, part, i))

    def there0(i):
        return inside(-1) if i < 6 else inside(1) if i >= 14 else 1

    lane32 = iota((32, 128), 1)

    def first_main(i):
        around = neighbours(three(km, i + 2), three(pkm, i + 2), rows_beside)
        diag = lm[i] + 0.5 * (CALL * km[i + 2] + around)
        inv = OMEGA / diag
        if not 6 <= i < 14:
            inv = jnp.where(lane32 < 128 * there0(i), inv, 0.0)
        dgm[i], dm[i] = diag, inv
        ready(field_a[0], on_main, i, inv * fm[i])

    def first_strip(i):
        there = there0(i)
        around = neighbours(three(ks, i + 2), three(pks, i + 2), rows_strip)
        diag = ls[i] + 0.5 * (CALL * ks[i + 2] + around)
        keep = jnp.logical_or(place < (8 + 8 * has_right) * there, place >= 32 - (8 + 8 * has_left) * there)
        inv = jnp.where(keep, OMEGA / diag, 0.0)
        dgs[i], ds_[i] = diag, inv
        ready(field_a[1], on_strip, i, inv * fs[i])

    def spread(s):
        return jnp.concatenate([jnp.where(group == t, s, 0.0) for t in range(4)], axis=0)

    def k_main(p):
        below, above = beside(km[p])
        kbm[p], kam[p], pkm[p] = below, above, below + above

    def k_pair(i):
        tm[32 * i : 32 * i + 32, :] = km[2 * i] + km[2 * i + 1]

    rm01, rs01 = ring_map(inner_z, 96), ring_map(outer_z, 96)
    r12, r23 = ring_map(cut(96), 64), ring_map(cut(64), 64)

    for ref, held, off in ((km, ks, 8), (fm, fs, 6), (lm, ls, 6)):
        for x in range(8):
            held[x + off] = own_strip(ref[x + off])
    for p in range(8, 16):
        k_main(p)
    for i in range(4, 8):
        k_pair(i)
    for i in range(2, 6):
        tlm[32 * i : 32 * i + 32, :] = lm[2 * i + 2] + lm[2 * i + 3]
    loop(7, 13, first_main)
    for i in range(8, 12):
        sweep(i, 0)
    early = {i: resid(field_b[0], on_main, i) for i in (9, 10)}

    for c in e0k + e0s:
        c.arrived()
    merged = merge(rs0, 0)
    for p in range(24):
        own = ks[p] if 8 <= p < 16 else own_strip(km[p])
        ks[p] = whole_strip(own, merged, p - 8)

    for p in range(24):
        below, above = beside(ks[p])
        kbs[p], kas[p], pks[p] = below, above, below + above
    for p in (*range(1, 8), *range(16, 23)):
        k_main(p)
    for i in (0, 1, 2, 3, 8, 9, 10, 11):
        k_pair(i)
    for i in range(12):
        ts[32 * i : 32 * i + 32, :] = spread(ks[2 * i] + ks[2 * i + 1])

    coarse = dot(halve_rows(tm, 192), rm01) + dot(halve_rows(ts, 192), rs01)
    k1l[...] = (0.125 * coarse).reshape(12, 16, 128)

    kk = k1l[2:10]
    for i in range(4):
        t1[16 * i : 16 * i + 16, :] = kk[2 * i] + kk[2 * i + 1]
    k2l = (0.125 * dot(halve_rows(t1, 32), r12)).reshape(4, 8, 128)
    for c in e0f + e0l:
        c.arrived()
    for n, (ref, strip) in ((1, (fm, fs)), (2, (lm, ls))):
        merged = merge(rs0, n)
        for p in range(20):
            own = strip[p] if 6 <= p < 14 else own_strip(ref[p])
            strip[p] = whole_strip(own, merged, p - 6)

    for i in (0, 1, 6, 7):
        tlm[32 * i : 32 * i + 32, :] = lm[2 * i + 2] + lm[2 * i + 3]
    for i in range(8):
        tls[32 * i : 32 * i + 32, :] = spread(ls[2 * i + 2] + ls[2 * i + 3])
    l1 = dot(halve_rows(tlm, 128), rm01) + dot(halve_rows(tls, 128), rs01)
    l1 = (0.125 * l1).reshape(8, 16, 128)
    half1 = 0.5 * 0.25
    dg1[...] = l1 + half1 * (CALL * k1l[2:10] + ring_sum(k1l[1:11]))
    for i in range(2):
        t1[16 * i : 16 * i + 16, :] = l1[2 * i + 2] + l1[2 * i + 3]
    l2own = (0.125 * dot(halve_rows(t1, 16), r12)).reshape(2, 8, 128)
    half2 = 0.5 * 0.0625
    diag2 = l2own + half2 * (CALL * k2l[1:3] + ring_sum(k2l))
    both = (k2l[1], k2l[2], diag2[0], diag2[1])
    low = jnp.where(lane < 32, both[0], rot(both[1], 32, 1))
    high = jnp.where(lane < 96, rot(both[2], 64, 1), rot(both[3], 96, 1))
    kd2[...] = jnp.where(lane < 64, low, high)
    l2sum = rot(l2own[0] + l2own[1], 64, 1)
    for i in (*range(0, 7), *range(13, 20)):
        first_main(i)
    loop(0, 20, first_strip)
    ekd2 = send_far(kd2, kd2x)
    for i in (*range(1, 8), *range(12, 19)):
        sweep(i, 0)
    for i in range(1, 19):
        sweep(i, 1)
    for i in range(8):
        pair = [early[n] if n in early else resid(field_b[0], on_main, n) for n in (2 * i + 2, 2 * i + 3)]
        tm[32 * i : 32 * i + 32, :] = pair[0] + pair[1]
        pair = [resid(field_b[1], on_strip, n) for n in (2 * i + 2, 2 * i + 3)]
        pair = pair[0] + pair[1]
        ts[32 * i : 32 * i + 32, :] = jnp.concatenate([pair] * 4, axis=0)
    cell = jnp.where(lane < 96, 2 * lane, 2 * lane - 256)
    pairs = halve_rows(tm, 128)
    inner = from_lanes(pairs, cell & 127) + from_lanes(pairs, (cell + 1) & 127)
    at = jnp.where(cell >= 64, cell - 120, cell + 24) & 31
    tile = 32 * (row >> 2)
    even_at, odd_at = (tile + at, tile + 64 + at), (tile + at + 1, tile + 65 + at)
    pairs = halve_rows(ts, 128)
    outer = from_lanes(pairs, even_at) + from_lanes(pairs, odd_at)
    lane_all = iota((128, 128), 1)
    use_inner = jnp.logical_and(lane_all >= 2, lane_all < 62)
    use_outer = jnp.logical_or(lane_all < 68, lane_all >= 124)
    rhs1 = jnp.where(use_inner, inner, jnp.where(use_outer, outer, 0.0))
    f1[...] = (0.125 * rhs1).reshape(8, 16, 128)

    def pack_sides1(arr):
        left, right = jnp.zeros((8, 128), F32), jnp.zeros((8, 128), F32)
        for x in range(4):
            for t in range(2):
                slot = 2 * x + t
                r = rot(arr[x, 8 * t : 8 * t + 8, :], 4 * slot, 1)
                left = jnp.where((lane >> 2) == slot, r, left)
                right = jnp.where((lane >> 2) == slot + 15, r, right)
        return left, right

    def fill1(ref, own, x_ref, rs):
        merged = [jnp.where(group == 0, rs[step, 0], rs[step, 1]) for step in range(3)]
        for p in range(10):
            x = p - 3
            for t in range(2):
                side = rot(merged[(x + 4) // 4], 64 - 4 * (2 * (x % 4) + t), 1)
                side = jnp.where(jnp.logical_or(lane < 68, lane >= 124), side, 0.0)
                rows = slice(8 * t, 8 * t + 8)
                center = x_ref[0, x + 3, rows, :] if x < 0 else x_ref[1, x - 4, rows, :] if x > 3 else own[x, rows, :]
                ref[p, 8 * t : 8 * t + 8, :] = jnp.where(lane < 64, center, side)

    k1[...] = k1l[1:11]
    k1_all = k1[...]
    k1_all = (k1_all,) + beside(k1_all, 2)
    lane1 = iota((2, 16, 128), 2)

    def inverse1(lo, hi, step):
        there = inside(step)
        keep = jnp.logical_or(lane1 < (64 + 4 * has_right) * there, lane1 >= 128 - 4 * has_left * there)
        return jnp.where(keep, OMEGA / dg1[lo:hi], 0.0)

    def sweep1(v, depth, inv):
        kk = cut_planes(k1_all, 3 - depth, 7 + depth)
        lo, hi = 3 - depth, 5 + depth
        rest = f1[lo:hi] - ring_apply(v, kk, dg1[lo:hi], half1)
        return v[1:-1] + inv[lo:hi] * rest

    inv1 = jnp.concatenate([inverse1(0, 2, -1), inverse1(2, 4, 0), inverse1(4, 6, 0), inverse1(6, 8, 1)], axis=0)
    v = sweep1(inv1 * f1[...], 2, inv1)
    r = f1[2:6] - ring_apply(v, cut_planes(k1_all, 2, 8), dg1[2:6], half1)
    for i in range(2):
        t1[16 * i : 16 * i + 16, :] = r[2 * i] + r[2 * i + 1]
    pairs = halve_rows(t1, 16)
    rhs2 = from_lanes(pairs, (2 * lane) & 127) + from_lanes(pairs, (2 * lane + 1) & 127)
    rhs2 = (0.125 * rhs2).reshape(2, 8, 128)

    gl2[...] = jnp.where(lane < 32, rhs2[0], jnp.where(lane < 64, rot(rhs2[1], 32, 1), l2sum))
    e2 = send_far(gl2, gl2x)
    vv1[...] = v[1:5]
    pv1[0], pv1[1] = pack_sides1(v[1:5])
    ev1x = send_planes(vv1.at[0:3], vv1x.at[1], vv1.at[1:4], vv1x.at[0])
    ev1s = send_sides(pv1, rsv1)

    later = e2 + ev1x + ev1s
    for c in started:
        if not any(c is other for other in later):
            c.left()
    def around2(mine, ref, step):
        mid = mine if step == 4 else ref[step, 1]
        return mid, rot(ref[step, 2], 32, 1), rot(ref[step, 0], -32, 1)

    def near2(parts, n):
        mid, right, left = parts
        at = (lane - 32 * n) & 127
        side = jnp.where(at < 40, right, jnp.where(at >= 120, left, 0.0))
        return rot(jnp.where(at < 32, mid, side), -32 * n, 1)

    for c in ekd2:
        c.arrived()
    mine = kd2[...]
    for step in range(9):
        there = inside(step - 4)
        keep = jnp.logical_or(lane < (32 + 8 * has_right) * there, lane >= 128 - 8 * has_left * there)
        parts = around2(mine, kd2x, step)
        for x in range(2):
            k2[2 * step + x] = near2(parts, x)
            diag = near2(parts, 2 + x)
            dg2[2 * step + x] = diag
            t2[2 * step + x] = jnp.where(keep, OMEGA / diag, 0.0)

    def to_level3(pairs):
        n = len(pairs)
        for i, pair in enumerate(pairs):
            t1[8 * i : 8 * i + 8, :] = pair
        y = 0.125 * dot(halve_rows(t1, 4 * n), r23)
        for i in range(n):
            t3[i, 0:4, :] = y[4 * i : 4 * i + 4, :]
        return t3[0:n]

    k2_all = k2[...]
    k2_all = (k2_all,) + beside(k2_all, 2)
    t3[...] = jnp.zeros_like(t3)
    half3 = 0.5 * 0.015625
    k3 = to_level3([k2[2 * i] + k2[2 * i + 1] for i in range(9)])
    most3 = half3 * (CALL * k3[1:-1] + ring_sum(k3))

    for c in e2:
        c.arrived()
    mine = gl2[...]
    for step in range(9):
        parts = around2(mine, gl2x, step)
        for x in range(2):
            f2[2 * step + x] = near2(parts, x)
        l2[step] = near2(parts, 2)

    def sweep2(v, depth):
        lo, hi = 9 - depth, 9 + depth
        rest = f2[lo:hi] - ring_apply(v, cut_planes(k2_all, lo - 1, hi + 1), dg2[lo:hi], half2)
        return v[1:-1] + t2[lo:hi] * rest

    vb = sweep2(t2[...] * f2[...], 8)
    r = f2[2:16] - ring_apply(vb, cut_planes(k2_all, 1, 17), dg2[2:16], half2)
    l3 = to_level3([l2[i + 1] for i in range(7)])
    f3 = []
    for i in range(7):
        pair = r[2 * i] + r[2 * i + 1]
        f3.append(from_lanes(pair, (2 * lane) & 127) + from_lanes(pair, (2 * lane + 1) & 127))
    t1[0:56, :] = jnp.concatenate(f3, axis=0)
    f3 = 0.125 * halve_rows(t1, 28)
    for i in range(7):
        t3[i, 0:4, :] = f3[4 * i : 4 * i + 4, :]
    f3 = t3[0:7]
    diag3 = l3 + most3
    inv3 = []
    for i in range(7):
        there = inside(i - 3)
        keep = jnp.logical_or(lane < (16 + 4 * has_right) * there, lane >= 128 - 4 * has_left * there)
        inv3.append(jnp.where(jnp.logical_and(keep, row < 4), OMEGA / diag3[i], 0.0)[None])
    inv3 = jnp.concatenate(inv3, axis=0)
    v3 = inv3 * f3
    rest = f3[1:-1] - ring_apply(v3, cut_planes((k3,) + beside(k3, 2), 1, 8), diag3[1:-1], half3)
    v3 = v3[1:-1] + inv3[1:-1] * rest

    wide3 = from_lanes(v3.reshape(40, 128), jnp.where(lane < 64, lane >> 1, ((lane - 128) >> 1) + 128))
    for i in range(5):
        double_rows(t1.at[8 * i : 8 * i + 8, :], wide3[8 * i : 8 * i + 4, :])
    e3 = t1[0:40, :].reshape(5, 8, 128)
    e3 = jnp.concatenate([e3[i // 2][None] for i in range(10)], axis=0)
    vb = vb[3:13] + e3
    vb = sweep2(vb, 4)
    vb = sweep2(vb, 3)

    for c in ev1x + ev1s:
        c.arrived()
    fill1(va1, vv1, vv1x, rsv1)
    wide2 = from_lanes(vb.reshape(48, 128), jnp.where(lane < 96, lane >> 1, ((lane - 128) >> 1) + 128))
    double_rows(tm.at[0:96, :], wide2)
    e2v = tm[0:96, :].reshape(6, 16, 128)
    inner = jnp.logical_or(lane < 68, lane >= 124)
    inner = jnp.concatenate([inner, inner], axis=0)
    v = [jnp.where(inner, va1[p] + e2v[(p - 3) // 2 + 2], 0.0)[None] for p in range(10)]
    v = sweep1(jnp.concatenate(v, axis=0), 3, inv1)
    v = sweep1(v, 2, inv1)

    e1 = v.reshape(96, 128)
    double_rows(tm.at[0:192, :], from_lanes(e1, lane >> 1))
    double_rows(ts.at[0:192, :], from_lanes(e1, (strip_z(lane) >> 1) & 127))
    def correct(i):
        at = 32 * ((i - 4) // 2)
        m = bvm[i] + tm[at : at + 32, :]
        s = ts[at : at + 8, :]
        for t in range(1, 4):
            s = jnp.where(group == t, ts[at + 8 * t : at + 8 * t + 8, :], s)
        ready(field_a[0], on_main, i, m)
        ready(field_a[1], on_strip, i, bvs[i] + s)

    loop(4, 16, correct)
    for i in range(5, 15):
        sweep(i, 0)
        sweep(i, 1)

    def last(i):
        m = bvm[i] + dm[i] * resid(field_b[0], on_main, i)
        s = bvs[i] + ds_[i] * resid(field_b[1], on_strip, i)
        s = jnp.where(place < 8, s, rot(s, -16, 1))
        ends = jnp.concatenate([rot(s, 120 - 32 * t, 1) for t in range(4)], axis=0)
        out_ref[i - 6] = jnp.where(jnp.logical_or(lane32 < 4, lane32 >= 124), ends, m)

    loop(6, 14, last)
    for c in later:
        c.left()


def solution(mesh):
    nw, nz = mesh.shape["wide"], mesh.shape["narrow"]

    def on_device(source, permeability, leakage):
        def vm(*shape):
            return pltpu.VMEM(shape, F32)

        def pair(n):
            return [vm(n, 32, 128), vm(n, 8, 128)]

        scratch = pair(24) * 4 + pair(20) * 12 + [vm(384, 128), vm(384, 128), vm(256, 128), vm(256, 128)]
        scratch += [vm(2, 2, 3, 8, 128), vm(3, 2, 2, 3, 8, 128)]
        scratch += [vm(2, 8, 128), vm(3, 2, 8, 128)]
        scratch += [vm(4, 16, 128), vm(2, 3, 16, 128)]
        scratch += [vm(12, 16, 128), vm(10, 16, 128), vm(8, 16, 128), vm(8, 16, 128), vm(10, 16, 128), vm(128, 128)]
        scratch += [vm(8, 128), vm(9, 3, 8, 128), vm(8, 128), vm(9, 3, 8, 128)]
        scratch += [vm(18, 8, 128), vm(18, 8, 128), vm(18, 8, 128), vm(9, 8, 128), vm(18, 8, 128), vm(9, 8, 128)]
        n = 12 + 26 + 26 + 8
        scratch += [pltpu.SemaphoreType.REGULAR, pltpu.SemaphoreType.DMA((3,)), pltpu.SemaphoreType.DMA((n,)), pltpu.SemaphoreType.DMA((n,))]

        def body(*refs):
            kernel(nw, nz, *refs)

        return pl.pallas_call(
            body,
            out_shape=pltpu.VMEM(source.shape, F32),
            in_specs=[pl.BlockSpec(memory_space=pltpu.HBM)] * 3,
            out_specs=pl.BlockSpec(memory_space=pltpu.VMEM),
            scratch_shapes=scratch,
            compiler_params=pltpu.CompilerParams(
                collective_id=0, has_side_effects=True, vmem_limit_bytes=60 * 2**20
            ),
            name="vcycle",
        )(source, permeability, leakage)

    spec = P("wide", None, "narrow")
    return jax.shard_map(on_device, mesh=mesh, in_specs=(spec, spec, spec), out_specs=spec, check_vma=False)
```

```python
import jax
import jax.numpy as jnp
from jax import lax
from jax.experimental import pallas as pl
from jax.experimental.pallas import tpu as pltpu
from jax.sharding import PartitionSpec as P

MESH = pl.DeviceIdType.MESH
OMEGA = 0.8
F32 = jnp.float32


def weight(a, b, c):
    n = a + b + c
    return (a * 1.0 + b * 0.7 + c * 0.4) / n * {1: 1.0, 2: 0.25, 3: 0.1}[n]


CX, CY, CZ = weight(1, 0, 0), weight(0, 1, 0), weight(0, 0, 1)
CXY, CXZ, CYZ, CXYZ = weight(1, 1, 0), weight(1, 0, 1), weight(0, 1, 1), weight(1, 1, 1)
CALL = 2 * (CX + CY + CZ) + 4 * (CXY + CXZ + CYZ) + 8 * CXYZ

SIDES = [(a, b) for b in (-1, 1) for a in (-1, 0, 1)]
FAR = [(a, b) for n in (4, 3, 2, 1, 0) for a in sorted({-n, n}) for b in (-1, 1, 0) if (a, b) != (0, 0)]


def iota(shape, dim):
    return lax.broadcasted_iota(jnp.int32, shape, dim)


def lanes():
    return iota((8, 128), 1)


def rot(x, shift, axis):
    shift %= x.shape[axis]
    return x if shift == 0 else pltpu.roll(x, shift, axis)


def rows_beside(t):
    axis = t.ndim - 2
    n = t.shape[axis]
    row = iota(t.shape, axis)
    up = jnp.where(row == 0, 0.0, rot(t, 1, axis))
    down = jnp.where(row == n - 1, 0.0, rot(t, n - 1, axis))
    return up + down


def neighbours(u, p, y):
    x, xp = u[0] + u[2], p[0] + p[2]
    inner = CXY * x + CXYZ * xp + CY * u[1] + CYZ * p[1]
    return CX * x + CXZ * xp + CZ * p[1] + y(inner)


def beside(u, axis=1):
    return rot(u, 1, axis), rot(u, 127, axis)


def rows_strip(c):
    row, lane = iota((8, 128), 0), iota((8, 128), 1)
    up, down = rot(c, 1, 0), rot(c, 7, 0)
    up = jnp.where(row == 0, jnp.where(lane < 32, 0.0, rot(up, 32, 1)), up)
    down = jnp.where(row == 7, jnp.where(lane >= 96, 0.0, rot(down, 96, 1)), down)
    return up + down


def slabs(u):
    return u[:-2], u[1:-1], u[2:]


def ring_sum(u):
    below, above = beside(u, 2)
    return neighbours(slabs(u), slabs(below + above), rows_beside)


def ring_apply(v, k, diag, half):
    k, k_below, k_above = k
    below, above = beside(v, 2)
    s1 = neighbours(slabs(v), slabs(below + above), rows_beside)
    s2 = neighbours(slabs(k * v), slabs(k_below * below + k_above * above), rows_beside)
    return diag * v[1:-1] - half * (k[1:-1] * s1 + s2)


def cut_planes(k, lo, hi):
    return tuple(part[lo:hi] for part in k)


def dot(a, b):
    return lax.dot_general(a, b, (((1,), (0,)), ((), ())), precision=lax.Precision.HIGHEST, preferred_element_type=F32)


def ring_map(fine_of, coarse_cut):
    i, j = iota((128, 128), 0), iota((128, 128), 1)
    return ((fine_of(i) >> 1) == jnp.where(j < coarse_cut, j, j - 128)).astype(F32)


def cut(c):
    return lambda i: jnp.where(i < c, i, i - 128)


def inner_z(i):
    return jnp.where(jnp.logical_and(i >= 4, i < 124), i, 4096)


def strip_z(i):
    r = i & 31
    return jnp.where(r < 16, r + 120, r - 24)


def outer_z(i):
    r = i & 31
    return jnp.where(jnp.logical_or(r < 4, r >= 28), 4096, strip_z(i))


def from_lanes(x, index):
    index = index if isinstance(index, tuple) else (index,)
    tiles = [x[8 * i : 8 * i + 8] for i in range(x.shape[0] // 8)]
    tiles = [jnp.take_along_axis(t, index[i % len(index)], axis=1) for i, t in enumerate(tiles)]
    return jnp.concatenate(tiles, axis=0)


def halve_rows(ref, n):
    return ref[pl.ds(0, n, stride=2), :] + ref[pl.ds(1, n, stride=2), :]


def double_rows(ref, x):
    n = x.shape[0]
    ref[pl.ds(0, n, stride=2), :] = x
    ref[pl.ds(1, n, stride=2), :] = x


def kernel(
    nw, nz, f_hbm, k_hbm, l_hbm, out_ref,
    km, ks, pkm, pks, kbm, kbs, kam, kas, fm, fs, lm, ls, dgm, dgs, dm, ds_,
    avm, avs, apm, aps, aqm, aqs, arm, ars, bvm, bvs, bpm, bps, bqm, bqs, brm, brs, tm, ts, tlm, tls,
    pack0, rs0, pv1, rsv1, vv1, vv1x,
    k1l, k1, dg1, f1, va1, t1, kd2, kd2x, gl2, gl2x, k2, dg2, f2, l2, t2, t3, hello, loc_sem, send_sem, recv_sem,
):
    w, z = lax.axis_index("wide"), lax.axis_index("narrow")

    def device(a, b):
        return (w + a, z + b)

    def in_grid(a, b):
        ok = jnp.logical_and(w + a >= 0, w + a < nw)
        return ok if b == 0 else jnp.logical_and(ok, jnp.logical_and(z + b >= 0, z + b < nz))

    has_left, has_right = (z > 0).astype(jnp.int32), (z < nz - 1).astype(jnp.int32)

    def inside(step):
        return jnp.logical_and(w + step >= 0, w + step < nw).astype(jnp.int32)

    class Message:
        def __init__(self, n, src, dst, a, b):
            self.to, self.origin = (a, b), (-a, -b)
            self.copy, self.same = [
                pltpu.make_async_remote_copy(
                    src_ref=src, dst_ref=dst, send_sem=send_sem.at[n], recv_sem=recv_sem.at[n],
                    device_id=device(*other), device_id_type=MESH,
                )
                for other in (self.to, self.origin)
            ]
            pl.when(in_grid(*self.to))(self.copy.start)

        def arrived(self):
            pl.when(in_grid(*self.origin))(self.same.wait_recv)

        def left(self):
            pl.when(in_grid(*self.to))(self.copy.wait_send)

    started = []

    def send(src, dst, a, b):
        started.append(Message(len(started), src, dst, a, b))
        return started[-1]

    def loop(lo, hi, body):
        for i in range(lo, hi):
            body(i)

    lane, row = lanes(), iota((8, 128), 0)
    group, place = lane >> 5, lane & 31

    loads = []
    for n, (src, dst) in enumerate(((k_hbm, km.at[8:16]), (f_hbm, fm.at[6:14]), (l_hbm, lm.at[6:14]))):
        loads.append(pltpu.make_async_copy(src, dst, loc_sem.at[n]))
        loads[-1].start()

    for ref in (rs0, rsv1, vv1x, kd2x, gl2x):
        ref[...] = jnp.zeros_like(ref)

    def clear(k_planes, planes):
        def body():
            km[k_planes] = jnp.zeros((8, 32, 128), F32)
            fm[planes] = jnp.zeros((6, 32, 128), F32)
            lm[planes] = jnp.zeros((6, 32, 128), F32)

        return body

    pl.when(w == 0)(clear(slice(0, 8), slice(0, 6)))
    pl.when(w == nw - 1)(clear(slice(16, 24), slice(14, 20)))

    barrier = pltpu.get_barrier_semaphore()

    def greet(a, b):
        def body():
            pl.semaphore_signal(barrier, inc=1, device_id=device(a, b), device_id_type=MESH)

        return body

    for a, b in FAR:
        if b >= 0 and abs(a) <= 3:
            pl.when(in_grid(a, b))(greet(a, b))
    def own_strip(m):
        out = rot(m[0:8, :], 8, 1)
        for t in range(1, 4):
            out = jnp.where(group == t, rot(m[8 * t : 8 * t + 8, :], 32 * t + 8, 1), out)
        return jnp.where(place < 16, out, rot(out, 16, 1))

    eighth = place >> 3
    even = (eighth & 1) == 0
    spot = (0, 16, 8, 24)

    def pack_strips(planes):
        left, right = jnp.zeros((8, 128), F32), jnp.zeros((8, 128), F32)
        for x, m in enumerate(planes):
            for t in range(4):
                r = rot(m[8 * t : 8 * t + 8, :], 32 * t + spot[x], 1)
                at = 4 * t + spot[x] // 8
                left = jnp.where((lane >> 3) == at, r, left)
                right = jnp.where((lane >> 3) == (at - 1) % 16, r, right)
        return left, rot(right, 16, 1)

    def merge(rs, n):
        out = {}
        for step, half in [(step, half) for step in range(3) for half in range(2)]:
            left, right = rs[step, 0, half, n], rs[step, 1, half, n]
            out[step, half] = (jnp.where(even, left, right), jnp.where(even, right, left))
        return out

    own_lanes = jnp.logical_or(place < 8, place >= 24)

    def whole_strip(own, merged, x):
        at = x % 8
        halo = merged[(x + 8) // 8, at // 4][at % 4 // 2]
        return jnp.where(own_lanes, own, rot(halo, 8 - spot[at % 4], 1))

    def count(pos, reach, size):
        return jnp.minimum(pos, reach) + 1 + jnp.minimum(size - 1 - pos, reach)

    pl.semaphore_wait(barrier, count(w, 3, nw) * (1 + has_left) - 1)

    def say_hello():
        pl.semaphore_signal(hello, inc=1, device_id=device(0, -1), device_id_type=MESH)

    pl.when(z > 0)(say_hello)

    def send_planes(src_lo, dst_hi, src_hi, dst_lo):
        return [send(src_hi, dst_lo, 1, 0), send(src_lo, dst_hi, -1, 0)]

    def send_sides(pack, rs):
        return [send(pack.at[0 if b < 0 else 1], rs.at[1 - a, 0 if b < 0 else 1], a, b) for a, b in SIDES]

    def send_far(src, dst):
        return [send(src, dst.at[4 - a, 1 - b], a, b) for a, b in FAR]

    e0k = send_planes(k_hbm, km.at[16:24], k_hbm, km.at[0:8])

    for load in loads:
        load.wait()
    for n, (ref, off) in enumerate(((km, 8), (fm, 6), (lm, 6))):
        for half in range(2):
            planes = [ref[x + off] for x in range(4 * half, 4 * half + 4)]
            pack0[0, half, n], pack0[1, half, n] = pack_strips(planes)

    def send_strips(b):
        side = 0 if b < 0 else 1
        return [send(pack0.at[side], rs0.at[1 - a, side], a, b) for a in (0, -1, 1)]

    e0s = send_strips(-1)
    e0f = send_planes(f_hbm.at[0:6], fm.at[14:20], f_hbm.at[2:8], fm.at[0:6])
    e0l = send_planes(l_hbm.at[0:6], lm.at[14:20], l_hbm.at[2:8], lm.at[0:6])
    def hear_hello():
        pl.semaphore_wait(hello, 1)

    pl.when(z < nz - 1)(hear_hello)
    e0s += send_strips(1)

    def three(ref, i):
        return ref[i - 1], ref[i], ref[i + 1]

    field_a = ((avm, apm, aqm, arm), (avs, aps, aqs, ars))
    field_b = ((bvm, bpm, bqm, brm), (bvs, bps, bqs, brs))
    on_main = ((fm, dgm, dm), (km, kbm, kam), rows_beside)
    on_strip = ((fs, dgs, ds_), (ks, kbs, kas), rows_strip)

    def ready(field, part, i, value):
        v, p, q, r = field
        k, k_below, k_above = part[1]
        v[i] = value
        below, above = beside(value)
        p[i], q[i] = below + above, value * k[i + 2]
        r[i] = below * k_below[i + 2] + above * k_above[i + 2]

    def resid(field, part, i):
        v, p, q, r = field
        (f, dg, _), (k, _, _), rows = part
        s1 = neighbours(three(v, i), three(p, i), rows)
        s2 = neighbours(three(q, i), three(r, i), rows)
        return f[i] - dg[i] * v[i] + 0.5 * (k[i + 2] * s1 + s2)

    def sweep(i, side):
        part = (on_main, on_strip)[side]
        source = field_a[side]
        ready(field_b[side], part, i, source[0][i] + part[0][2][i] * resid(source, part, i))

    def there0(i):
        return inside(-1) if i < 6 else inside(1) if i >= 14 else 1

    lane32 = iota((32, 128), 1)

    def first_main(i):
        around = neighbours(three(km, i + 2), three(pkm, i + 2), rows_beside)
        diag = lm[i] + 0.5 * (CALL * km[i + 2] + around)
        inv = OMEGA / diag
        if not 6 <= i < 14:
            inv = jnp.where(lane32 < 128 * there0(i), inv, 0.0)
        dgm[i], dm[i] = diag, inv
        ready(field_a[0], on_main, i, inv * fm[i])

    def first_strip(i):
        there = there0(i)
        around = neighbours(three(ks, i + 2), three(pks, i + 2), rows_strip)
        diag = ls[i] + 0.5 * (CALL * ks[i + 2] + around)
        keep = jnp.logical_or(place < (8 + 8 * has_right) * there, place >= 32 - (8 + 8 * has_left) * there)
        inv = jnp.where(keep, OMEGA / diag, 0.0)
        dgs[i], ds_[i] = diag, inv
        ready(field_a[1], on_strip, i, inv * fs[i])

    def spread(s):
        return jnp.concatenate([jnp.where(group == t, s, 0.0) for t in range(4)], axis=0)

    def k_main(p):
        below, above = beside(km[p])
        kbm[p], kam[p], pkm[p] = below, above, below + above

    def k_pair(i):
        tm[32 * i : 32 * i + 32, :] = km[2 * i] + km[2 * i + 1]

    rm01, rs01 = ring_map(inner_z, 96), ring_map(outer_z, 96)
    r12, r23 = ring_map(cut(96), 64), ring_map(cut(64), 64)

    for ref, held, off in ((km, ks, 8), (fm, fs, 6), (lm, ls, 6)):
        for x in range(8):
            held[x + off] = own_strip(ref[x + off])
    for p in range(8, 16):
        k_main(p)
    for i in range(4, 8):
        k_pair(i)
    for i in range(2, 6):
        tlm[32 * i : 32 * i + 32, :] = lm[2 * i + 2] + lm[2 * i + 3]
    loop(7, 13, first_main)
    for i in range(8, 12):
        sweep(i, 0)
    early = {i: resid(field_b[0], on_main, i) for i in (9, 10)}

    for c in e0k + e0s:
        c.arrived()
    merged = merge(rs0, 0)
    for p in range(24):
        own = ks[p] if 8 <= p < 16 else own_strip(km[p])
        ks[p] = whole_strip(own, merged, p - 8)

    for p in range(24):
        below, above = beside(ks[p])
        kbs[p], kas[p], pks[p] = below, above, below + above
    for p in (*range(1, 8), *range(16, 23)):
        k_main(p)
    for i in (0, 1, 2, 3, 8, 9, 10, 11):
        k_pair(i)
    for i in range(12):
        ts[32 * i : 32 * i + 32, :] = spread(ks[2 * i] + ks[2 * i + 1])

    coarse = dot(halve_rows(tm, 192), rm01) + dot(halve_rows(ts, 192), rs01)
    k1l[...] = (0.125 * coarse).reshape(12, 16, 128)

    kk = k1l[2:10]
    for i in range(4):
        t1[16 * i : 16 * i + 16, :] = kk[2 * i] + kk[2 * i + 1]
    k2l = (0.125 * dot(halve_rows(t1, 32), r12)).reshape(4, 8, 128)
    for c in e0f + e0l:
        c.arrived()
    for n, (ref, strip) in ((1, (fm, fs)), (2, (lm, ls))):
        merged = merge(rs0, n)
        for p in range(20):
            own = strip[p] if 6 <= p < 14 else own_strip(ref[p])
            strip[p] = whole_strip(own, merged, p - 6)

    for i in (0, 1, 6, 7):
        tlm[32 * i : 32 * i + 32, :] = lm[2 * i + 2] + lm[2 * i + 3]
    for i in range(8):
        tls[32 * i : 32 * i + 32, :] = spread(ls[2 * i + 2] + ls[2 * i + 3])
    l1 = dot(halve_rows(tlm, 128), rm01) + dot(halve_rows(tls, 128), rs01)
    l1 = (0.125 * l1).reshape(8, 16, 128)
    half1 = 0.5 * 0.25
    dg1[...] = l1 + half1 * (CALL * k1l[2:10] + ring_sum(k1l[1:11]))
    for i in range(2):
        t1[16 * i : 16 * i + 16, :] = l1[2 * i + 2] + l1[2 * i + 3]
    l2own = (0.125 * dot(halve_rows(t1, 16), r12)).reshape(2, 8, 128)
    half2 = 0.5 * 0.0625
    diag2 = l2own + half2 * (CALL * k2l[1:3] + ring_sum(k2l))
    both = (k2l[1], k2l[2], diag2[0], diag2[1])
    low = jnp.where(lane < 32, both[0], rot(both[1], 32, 1))
    high = jnp.where(lane < 96, rot(both[2], 64, 1), rot(both[3], 96, 1))
    kd2[...] = jnp.where(lane < 64, low, high)
    l2sum = rot(l2own[0] + l2own[1], 64, 1)
    for i in (*range(0, 7), *range(13, 20)):
        first_main(i)
    loop(0, 20, first_strip)
    ekd2 = send_far(kd2, kd2x)
    for i in (*range(1, 8), *range(12, 19)):
        sweep(i, 0)
    for i in range(1, 19):
        sweep(i, 1)
    for i in range(8):
        pair = [early[n] if n in early else resid(field_b[0], on_main, n) for n in (2 * i + 2, 2 * i + 3)]
        tm[32 * i : 32 * i + 32, :] = pair[0] + pair[1]
        pair = [resid(field_b[1], on_strip, n) for n in (2 * i + 2, 2 * i + 3)]
        pair = pair[0] + pair[1]
        ts[32 * i : 32 * i + 32, :] = jnp.concatenate([pair] * 4, axis=0)
    cell = jnp.where(lane < 96, 2 * lane, 2 * lane - 256)
    pairs = halve_rows(tm, 128)
    inner = from_lanes(pairs, cell & 127) + from_lanes(pairs, (cell + 1) & 127)
    at = jnp.where(cell >= 64, cell - 120, cell + 24) & 31
    tile = 32 * (row >> 2)
    even_at, odd_at = (tile + at, tile + 64 + at), (tile + at + 1, tile + 65 + at)
    pairs = halve_rows(ts, 128)
    outer = from_lanes(pairs, even_at) + from_lanes(pairs, odd_at)
    lane_all = iota((128, 128), 1)
    use_inner = jnp.logical_and(lane_all >= 2, lane_all < 62)
    use_outer = jnp.logical_or(lane_all < 68, lane_all >= 124)
    rhs1 = jnp.where(use_inner, inner, jnp.where(use_outer, outer, 0.0))
    f1[...] = (0.125 * rhs1).reshape(8, 16, 128)

    def pack_sides1(arr):
        left, right = jnp.zeros((8, 128), F32), jnp.zeros((8, 128), F32)
        for x in range(4):
            for t in range(2):
                slot = 2 * x + t
                r = rot(arr[x, 8 * t : 8 * t + 8, :], 4 * slot, 1)
                left = jnp.where((lane >> 2) == slot, r, left)
                right = jnp.where((lane >> 2) == slot + 15, r, right)
        return left, right

    def fill1(ref, own, x_ref, rs):
        merged = [jnp.where(group == 0, rs[step, 0], rs[step, 1]) for step in range(3)]
        for p in range(10):
            x = p - 3
            for t in range(2):
                side = rot(merged[(x + 4) // 4], 64 - 4 * (2 * (x % 4) + t), 1)
                side = jnp.where(jnp.logical_or(lane < 68, lane >= 124), side, 0.0)
                rows = slice(8 * t, 8 * t + 8)
                center = x_ref[0, x + 3, rows, :] if x < 0 else x_ref[1, x - 4, rows, :] if x > 3 else own[x, rows, :]
                ref[p, 8 * t : 8 * t + 8, :] = jnp.where(lane < 64, center, side)

    k1[...] = k1l[1:11]
    k1_all = k1[...]
    k1_all = (k1_all,) + beside(k1_all, 2)
    lane1 = iota((2, 16, 128), 2)

    def inverse1(lo, hi, step):
        there = inside(step)
        keep = jnp.logical_or(lane1 < (64 + 4 * has_right) * there, lane1 >= 128 - 4 * has_left * there)
        return jnp.where(keep, OMEGA / dg1[lo:hi], 0.0)

    def sweep1(v, depth, inv):
        kk = cut_planes(k1_all, 3 - depth, 7 + depth)
        lo, hi = 3 - depth, 5 + depth
        rest = f1[lo:hi] - ring_apply(v, kk, dg1[lo:hi], half1)
        return v[1:-1] + inv[lo:hi] * rest

    inv1 = jnp.concatenate([inverse1(0, 2, -1), inverse1(2, 4, 0), inverse1(4, 6, 0), inverse1(6, 8, 1)], axis=0)
    v = sweep1(inv1 * f1[...], 2, inv1)
    r = f1[2:6] - ring_apply(v, cut_planes(k1_all, 2, 8), dg1[2:6], half1)
    for i in range(2):
        t1[16 * i : 16 * i + 16, :] = r[2 * i] + r[2 * i + 1]
    pairs = halve_rows(t1, 16)
    rhs2 = from_lanes(pairs, (2 * lane) & 127) + from_lanes(pairs, (2 * lane + 1) & 127)
    rhs2 = (0.125 * rhs2).reshape(2, 8, 128)

    gl2[...] = jnp.where(lane < 32, rhs2[0], jnp.where(lane < 64, rot(rhs2[1], 32, 1), l2sum))
    e2 = send_far(gl2, gl2x)
    vv1[...] = v[1:5]
    pv1[0], pv1[1] = pack_sides1(v[1:5])
    ev1x = send_planes(vv1.at[0:3], vv1x.at[1], vv1.at[1:4], vv1x.at[0])
    ev1s = send_sides(pv1, rsv1)

    later = e2 + ev1x + ev1s
    for c in started:
        if not any(c is other for other in later):
            c.left()
    def around2(mine, ref, step):
        mid = mine if step == 4 else ref[step, 1]
        return mid, rot(ref[step, 2], 32, 1), rot(ref[step, 0], -32, 1)

    def near2(parts, n):
        mid, right, left = parts
        at = (lane - 32 * n) & 127
        side = jnp.where(at < 40, right, jnp.where(at >= 120, left, 0.0))
        return rot(jnp.where(at < 32, mid, side), -32 * n, 1)

    for c in ekd2:
        c.arrived()
    mine = kd2[...]
    for step in range(9):
        there = inside(step - 4)
        keep = jnp.logical_or(lane < (32 + 8 * has_right) * there, lane >= 128 - 8 * has_left * there)
        parts = around2(mine, kd2x, step)
        for x in range(2):
            k2[2 * step + x] = near2(parts, x)
            diag = near2(parts, 2 + x)
            dg2[2 * step + x] = diag
            t2[2 * step + x] = jnp.where(keep, OMEGA / diag, 0.0)

    def to_level3(pairs):
        n = len(pairs)
        for i, pair in enumerate(pairs):
            t1[8 * i : 8 * i + 8, :] = pair
        y = 0.125 * dot(halve_rows(t1, 4 * n), r23)
        for i in range(n):
            t3[i, 0:4, :] = y[4 * i : 4 * i + 4, :]
        return t3[0:n]

    k2_all = k2[...]
    k2_all = (k2_all,) + beside(k2_all, 2)
    t3[...] = jnp.zeros_like(t3)
    half3 = 0.5 * 0.015625
    k3 = to_level3([k2[2 * i] + k2[2 * i + 1] for i in range(9)])
    most3 = half3 * (CALL * k3[1:-1] + ring_sum(k3))

    for c in e2:
        c.arrived()
    mine = gl2[...]
    for step in range(9):
        parts = around2(mine, gl2x, step)
        for x in range(2):
            f2[2 * step + x] = near2(parts, x)
        l2[step] = near2(parts, 2)

    def sweep2(v, depth):
        lo, hi = 9 - depth, 9 + depth
        rest = f2[lo:hi] - ring_apply(v, cut_planes(k2_all, lo - 1, hi + 1), dg2[lo:hi], half2)
        return v[1:-1] + t2[lo:hi] * rest

    vb = sweep2(t2[...] * f2[...], 8)
    r = f2[2:16] - ring_apply(vb, cut_planes(k2_all, 1, 17), dg2[2:16], half2)
    l3 = to_level3([l2[i + 1] for i in range(7)])
    f3 = []
    for i in range(7):
        pair = r[2 * i] + r[2 * i + 1]
        f3.append(from_lanes(pair, (2 * lane) & 127) + from_lanes(pair, (2 * lane + 1) & 127))
    t1[0:56, :] = jnp.concatenate(f3, axis=0)
    f3 = 0.125 * halve_rows(t1, 28)
    for i in range(7):
        t3[i, 0:4, :] = f3[4 * i : 4 * i + 4, :]
    f3 = t3[0:7]
    diag3 = l3 + most3
    inv3 = []
    for i in range(7):
        there = inside(i - 3)
        keep = jnp.logical_or(lane < (16 + 4 * has_right) * there, lane >= 128 - 4 * has_left * there)
        inv3.append(jnp.where(jnp.logical_and(keep, row < 4), OMEGA / diag3[i], 0.0)[None])
    inv3 = jnp.concatenate(inv3, axis=0)
    v3 = inv3 * f3
    rest = f3[1:-1] - ring_apply(v3, cut_planes((k3,) + beside(k3, 2), 1, 8), diag3[1:-1], half3)
    v3 = v3[1:-1] + inv3[1:-1] * rest

    wide3 = from_lanes(v3.reshape(40, 128), jnp.where(lane < 64, lane >> 1, ((lane - 128) >> 1) + 128))
    for i in range(5):
        double_rows(t1.at[8 * i : 8 * i + 8, :], wide3[8 * i : 8 * i + 4, :])
    e3 = t1[0:40, :].reshape(5, 8, 128)
    e3 = jnp.concatenate([e3[i // 2][None] for i in range(10)], axis=0)
    vb = vb[3:13] + e3
    vb = sweep2(vb, 4)
    vb = sweep2(vb, 3)

    for c in ev1x + ev1s:
        c.arrived()
    fill1(va1, vv1, vv1x, rsv1)
    wide2 = from_lanes(vb.reshape(48, 128), jnp.where(lane < 96, lane >> 1, ((lane - 128) >> 1) + 128))
    double_rows(tm.at[0:96, :], wide2)
    e2v = tm[0:96, :].reshape(6, 16, 128)
    inner = jnp.logical_or(lane < 68, lane >= 124)
    inner = jnp.concatenate([inner, inner], axis=0)
    v = [jnp.where(inner, va1[p] + e2v[(p - 3) // 2 + 2], 0.0)[None] for p in range(10)]
    v = sweep1(jnp.concatenate(v, axis=0), 3, inv1)
    v = sweep1(v, 2, inv1)

    e1 = v.reshape(96, 128)
    double_rows(tm.at[0:192, :], from_lanes(e1, lane >> 1))
    double_rows(ts.at[0:192, :], from_lanes(e1, (strip_z(lane) >> 1) & 127))
    def correct(i):
        at = 32 * ((i - 4) // 2)
        m = bvm[i] + tm[at : at + 32, :]
        s = ts[at : at + 8, :]
        for t in range(1, 4):
            s = jnp.where(group == t, ts[at + 8 * t : at + 8 * t + 8, :], s)
        ready(field_a[0], on_main, i, m)
        ready(field_a[1], on_strip, i, bvs[i] + s)

    loop(4, 16, correct)
    for i in range(5, 15):
        sweep(i, 0)
        sweep(i, 1)

    def last(i):
        m = bvm[i] + dm[i] * resid(field_b[0], on_main, i)
        s = bvs[i] + ds_[i] * resid(field_b[1], on_strip, i)
        s = jnp.where(place < 8, s, rot(s, -16, 1))
        ends = jnp.concatenate([rot(s, 120 - 32 * t, 1) for t in range(4)], axis=0)
        out_ref[i - 6] = jnp.where(jnp.logical_or(lane32 < 4, lane32 >= 124), ends, m)

    loop(6, 14, last)
    for c in later:
        c.left()


def solution(mesh):
    nw, nz = mesh.shape["wide"], mesh.shape["narrow"]

    def on_device(source, permeability, leakage):
        def vm(*shape):
            return pltpu.VMEM(shape, F32)

        def pair(n):
            return [vm(n, 32, 128), vm(n, 8, 128)]

        scratch = pair(24) * 4 + pair(20) * 12 + [vm(384, 128), vm(384, 128), vm(256, 128), vm(256, 128)]
        scratch += [vm(2, 2, 3, 8, 128), vm(3, 2, 2, 3, 8, 128)]
        scratch += [vm(2, 8, 128), vm(3, 2, 8, 128)]
        scratch += [vm(4, 16, 128), vm(2, 3, 16, 128)]
        scratch += [vm(12, 16, 128), vm(10, 16, 128), vm(8, 16, 128), vm(8, 16, 128), vm(10, 16, 128), vm(128, 128)]
        scratch += [vm(8, 128), vm(9, 3, 8, 128), vm(8, 128), vm(9, 3, 8, 128)]
        scratch += [vm(18, 8, 128), vm(18, 8, 128), vm(18, 8, 128), vm(9, 8, 128), vm(18, 8, 128), vm(9, 8, 128)]
        n = 12 + 26 + 26 + 8
        scratch += [pltpu.SemaphoreType.REGULAR, pltpu.SemaphoreType.DMA((3,)), pltpu.SemaphoreType.DMA((n,)), pltpu.SemaphoreType.DMA((n,))]

        def body(*refs):
            kernel(nw, nz, *refs)

        return pl.pallas_call(
            body,
            out_shape=pltpu.VMEM(source.shape, F32),
            in_specs=[pl.BlockSpec(memory_space=pltpu.HBM)] * 3,
            out_specs=pl.BlockSpec(memory_space=pltpu.VMEM),
            scratch_shapes=scratch,
            compiler_params=pltpu.CompilerParams(
                collective_id=0, has_side_effects=True, vmem_limit_bytes=60 * 2**20
            ),
            name="vcycle",
        )(source, permeability, leakage)

    spec = P("wide", None, "narrow")
    return jax.shard_map(on_device, mesh=mesh, in_specs=(spec, spec, spec), out_specs=spec, check_vma=False)
```

```python
import jax
import jax.numpy as jnp
from jax import lax
from jax.experimental import pallas as pl
from jax.experimental.pallas import tpu as pltpu
from jax.sharding import PartitionSpec as P

MESH = pl.DeviceIdType.MESH
OMEGA = 0.8
F32 = jnp.float32


def weight(a, b, c):
    n = a + b + c
    return (a * 1.0 + b * 0.7 + c * 0.4) / n * {1: 1.0, 2: 0.25, 3: 0.1}[n]


CX, CY, CZ = weight(1, 0, 0), weight(0, 1, 0), weight(0, 0, 1)
CXY, CXZ, CYZ, CXYZ = weight(1, 1, 0), weight(1, 0, 1), weight(0, 1, 1), weight(1, 1, 1)
CALL = 2 * (CX + CY + CZ) + 4 * (CXY + CXZ + CYZ) + 8 * CXYZ

SIDES = [(a, b) for b in (-1, 1) for a in (-1, 0, 1)]
FAR = [(a, b) for n in (4, 3, 2, 1, 0) for a in sorted({-n, n}) for b in (-1, 1, 0) if (a, b) != (0, 0)]


def iota(shape, dim):
    return lax.broadcasted_iota(jnp.int32, shape, dim)


def lanes():
    return iota((8, 128), 1)


def rot(x, shift, axis):
    shift %= x.shape[axis]
    return x if shift == 0 else pltpu.roll(x, shift, axis)


def rows_beside(t):
    axis = t.ndim - 2
    n = t.shape[axis]
    row = iota(t.shape, axis)
    up = jnp.where(row == 0, 0.0, rot(t, 1, axis))
    down = jnp.where(row == n - 1, 0.0, rot(t, n - 1, axis))
    return up + down


def neighbours(u, p, y):
    x, xp = u[0] + u[2], p[0] + p[2]
    inner = CXY * x + CXYZ * xp + CY * u[1] + CYZ * p[1]
    return CX * x + CXZ * xp + CZ * p[1] + y(inner)


def beside(u, axis=1):
    return rot(u, 1, axis), rot(u, 127, axis)


def rows_strip(c):
    row, lane = iota((8, 128), 0), iota((8, 128), 1)
    up, down = rot(c, 1, 0), rot(c, 7, 0)
    up = jnp.where(row == 0, jnp.where(lane < 32, 0.0, rot(up, 32, 1)), up)
    down = jnp.where(row == 7, jnp.where(lane >= 96, 0.0, rot(down, 96, 1)), down)
    return up + down


def slabs(u):
    return u[:-2], u[1:-1], u[2:]


def ring_sum(u):
    below, above = beside(u, 2)
    return neighbours(slabs(u), slabs(below + above), rows_beside)


def ring_apply(v, k, diag, half):
    k, k_below, k_above = k
    below, above = beside(v, 2)
    s1 = neighbours(slabs(v), slabs(below + above), rows_beside)
    s2 = neighbours(slabs(k * v), slabs(k_below * below + k_above * above), rows_beside)
    return diag * v[1:-1] - half * (k[1:-1] * s1 + s2)


def cut_planes(k, lo, hi):
    return tuple(part[lo:hi] for part in k)


def dot(a, b):
    return lax.dot_general(a, b, (((1,), (0,)), ((), ())), precision=lax.Precision.HIGHEST, preferred_element_type=F32)


def ring_map(fine_of, coarse_cut):
    i, j = iota((128, 128), 0), iota((128, 128), 1)
    return ((fine_of(i) >> 1) == jnp.where(j < coarse_cut, j, j - 128)).astype(F32)


def cut(c):
    return lambda i: jnp.where(i < c, i, i - 128)


def inner_z(i):
    return jnp.where(jnp.logical_and(i >= 4, i < 124), i, 4096)


def strip_z(i):
    r = i & 31
    return jnp.where(r < 16, r + 120, r - 24)


def outer_z(i):
    r = i & 31
    return jnp.where(jnp.logical_or(r < 4, r >= 28), 4096, strip_z(i))


def from_lanes(x, index):
    index = index if isinstance(index, tuple) else (index,)
    tiles = [x[8 * i : 8 * i + 8] for i in range(x.shape[0] // 8)]
    tiles = [jnp.take_along_axis(t, index[i % len(index)], axis=1) for i, t in enumerate(tiles)]
    return jnp.concatenate(tiles, axis=0)


def halve_rows(ref, n):
    return ref[pl.ds(0, n, stride=2), :] + ref[pl.ds(1, n, stride=2), :]


def double_rows(ref, x):
    n = x.shape[0]
    ref[pl.ds(0, n, stride=2), :] = x
    ref[pl.ds(1, n, stride=2), :] = x


def kernel(
    nw, nz, f_hbm, k_hbm, l_hbm, out_ref,
    km, ks, pkm, pks, kbm, kbs, kam, kas, fm, fs, lm, ls, dgm, dgs, dm, ds_,
    avm, avs, apm, aps, aqm, aqs, arm, ars, bvm, bvs, bpm, bps, bqm, bqs, brm, brs, tm, ts, tlm, tls,
    pack0, rs0, pv1, rsv1, vv1, vv1x,
    k1l, dg1, f1, va1, t1, kd2, kd2x, gl2, gl2x, k2, dg2, f2, l2, t2, t3, hello, loc_sem, send_sem, recv_sem,
):
    w, z = lax.axis_index("wide"), lax.axis_index("narrow")

    def device(a, b):
        return (w + a, z + b)

    def in_grid(a, b):
        ok = jnp.logical_and(w + a >= 0, w + a < nw)
        return ok if b == 0 else jnp.logical_and(ok, jnp.logical_and(z + b >= 0, z + b < nz))

    has_left, has_right = (z > 0).astype(jnp.int32), (z < nz - 1).astype(jnp.int32)

    def inside(step):
        return jnp.logical_and(w + step >= 0, w + step < nw).astype(jnp.int32)

    class Message:
        def __init__(self, n, src, dst, a, b):
            self.to, self.origin = (a, b), (-a, -b)
            self.copy, self.same = [
                pltpu.make_async_remote_copy(
                    src_ref=src, dst_ref=dst, send_sem=send_sem.at[n], recv_sem=recv_sem.at[n],
                    device_id=device(*other), device_id_type=MESH,
                )
                for other in (self.to, self.origin)
            ]
            pl.when(in_grid(*self.to))(self.copy.start)

        def arrived(self):
            pl.when(in_grid(*self.origin))(self.same.wait_recv)

        def left(self):
            pl.when(in_grid(*self.to))(self.copy.wait_send)

    started = []

    def send(src, dst, a, b):
        started.append(Message(len(started), src, dst, a, b))
        return started[-1]

    def loop(lo, hi, body):
        for i in range(lo, hi):
            body(i)

    lane, row = lanes(), iota((8, 128), 0)
    group, place = lane >> 5, lane & 31

    loads = []
    for n, (src, dst) in enumerate(((k_hbm, km.at[8:16]), (f_hbm, fm.at[6:14]), (l_hbm, lm.at[6:14]))):
        loads.append(pltpu.make_async_copy(src, dst, loc_sem.at[n]))
        loads[-1].start()

    for ref in (rs0, rsv1, vv1x, kd2x, gl2x):
        ref[...] = jnp.zeros_like(ref)

    def clear(k_planes, planes):
        def body():
            km[k_planes] = jnp.zeros((8, 32, 128), F32)
            fm[planes] = jnp.zeros((6, 32, 128), F32)
            lm[planes] = jnp.zeros((6, 32, 128), F32)

        return body

    pl.when(w == 0)(clear(slice(0, 8), slice(0, 6)))
    pl.when(w == nw - 1)(clear(slice(16, 24), slice(14, 20)))

    barrier = pltpu.get_barrier_semaphore()

    def greet(a, b):
        def body():
            pl.semaphore_signal(barrier, inc=1, device_id=device(a, b), device_id_type=MESH)

        return body

    for a, b in FAR:
        if b >= 0 and abs(a) <= 3:
            pl.when(in_grid(a, b))(greet(a, b))
    def own_strip(m):
        out = rot(m[0:8, :], 8, 1)
        for t in range(1, 4):
            out = jnp.where(group == t, rot(m[8 * t : 8 * t + 8, :], 32 * t + 8, 1), out)
        return jnp.where(place < 16, out, rot(out, 16, 1))

    eighth = place >> 3
    even = (eighth & 1) == 0
    spot = (0, 16, 8, 24)

    def pack_strips(planes):
        left, right = jnp.zeros((8, 128), F32), jnp.zeros((8, 128), F32)
        for x, m in enumerate(planes):
            for t in range(4):
                r = rot(m[8 * t : 8 * t + 8, :], 32 * t + spot[x], 1)
                at = 4 * t + spot[x] // 8
                left = jnp.where((lane >> 3) == at, r, left)
                right = jnp.where((lane >> 3) == (at - 1) % 16, r, right)
        return left, rot(right, 16, 1)

    def merge(rs, n):
        out = {}
        for step, half in [(step, half) for step in range(3) for half in range(2)]:
            left, right = rs[step, 0, half, n], rs[step, 1, half, n]
            out[step, half] = (jnp.where(even, left, right), jnp.where(even, right, left))
        return out

    own_lanes = jnp.logical_or(place < 8, place >= 24)

    def whole_strip(own, merged, x):
        at = x % 8
        halo = merged[(x + 8) // 8, at // 4][at % 4 // 2]
        return jnp.where(own_lanes, own, rot(halo, 8 - spot[at % 4], 1))

    def count(pos, reach, size):
        return jnp.minimum(pos, reach) + 1 + jnp.minimum(size - 1 - pos, reach)

    pl.semaphore_wait(barrier, count(w, 3, nw) * (1 + has_left) - 1)

    def say_hello():
        pl.semaphore_signal(hello, inc=1, device_id=device(0, -1), device_id_type=MESH)

    pl.when(z > 0)(say_hello)

    def send_planes(src_lo, dst_hi, src_hi, dst_lo):
        return [send(src_hi, dst_lo, 1, 0), send(src_lo, dst_hi, -1, 0)]

    def send_sides(pack, rs):
        return [send(pack.at[0 if b < 0 else 1], rs.at[1 - a, 0 if b < 0 else 1], a, b) for a, b in SIDES]

    def send_far(src, dst):
        return [send(src, dst.at[4 - a, 1 - b], a, b) for a, b in FAR]

    e0k = send_planes(k_hbm.at[0:7], km.at[16:23], k_hbm.at[1:8], km.at[1:8])

    for load in loads:
        load.wait()
    for n, (ref, off) in enumerate(((km, 8), (fm, 6), (lm, 6))):
        for half in range(2):
            planes = [ref[x + off] for x in range(4 * half, 4 * half + 4)]
            pack0[0, half, n], pack0[1, half, n] = pack_strips(planes)

    def send_strips(b):
        side = 0 if b < 0 else 1
        return [send(pack0.at[side], rs0.at[1 - a, side], a, b) for a in (0, -1, 1)]

    e0s = send_strips(-1)
    e0f = send_planes(f_hbm.at[0:6], fm.at[14:20], f_hbm.at[2:8], fm.at[0:6])
    e0l = send_planes(l_hbm.at[0:6], lm.at[14:20], l_hbm.at[2:8], lm.at[0:6])
    def hear_hello():
        pl.semaphore_wait(hello, 1)

    pl.when(z < nz - 1)(hear_hello)
    e0s += send_strips(1)

    def three(ref, i):
        return ref[i - 1], ref[i], ref[i + 1]

    field_a = ((avm, apm, aqm, arm), (avs, aps, aqs, ars))
    field_b = ((bvm, bpm, bqm, brm), (bvs, bps, bqs, brs))
    on_main = ((fm, dgm, dm), (km, kbm, kam), rows_beside)
    on_strip = ((fs, dgs, ds_), (ks, kbs, kas), rows_strip)

    def ready(field, part, i, value):
        v, p, q, r = field
        k, k_below, k_above = part[1]
        v[i] = value
        below, above = beside(value)
        p[i], q[i] = below + above, value * k[i + 2]
        r[i] = below * k_below[i + 2] + above * k_above[i + 2]

    def resid(field, part, i):
        v, p, q, r = field
        (f, dg, _), (k, _, _), rows = part
        s1 = neighbours(three(v, i), three(p, i), rows)
        s2 = neighbours(three(q, i), three(r, i), rows)
        return f[i] - dg[i] * v[i] + 0.5 * (k[i + 2] * s1 + s2)

    def sweep(i, side):
        part = (on_main, on_strip)[side]
        source = field_a[side]
        ready(field_b[side], part, i, source[0][i] + part[0][2][i] * resid(source, part, i))

    def there0(i):
        return inside(-1) if i < 6 else inside(1) if i >= 14 else 1

    lane32 = iota((32, 128), 1)

    def first_main(i):
        around = neighbours(three(km, i + 2), three(pkm, i + 2), rows_beside)
        diag = lm[i] + 0.5 * (CALL * km[i + 2] + around)
        inv = OMEGA / diag
        if not 6 <= i < 14:
            inv = jnp.where(lane32 < 128 * there0(i), inv, 0.0)
        dgm[i], dm[i] = diag, inv
        ready(field_a[0], on_main, i, inv * fm[i])

    def first_strip(i):
        there = there0(i)
        around = neighbours(three(ks, i + 2), three(pks, i + 2), rows_strip)
        diag = ls[i] + 0.5 * (CALL * ks[i + 2] + around)
        keep = jnp.logical_or(place < (8 + 8 * has_right) * there, place >= 32 - (8 + 8 * has_left) * there)
        inv = jnp.where(keep, OMEGA / diag, 0.0)
        dgs[i], ds_[i] = diag, inv
        ready(field_a[1], on_strip, i, inv * fs[i])

    def spread(s):
        return jnp.concatenate([jnp.where(group == t, s, 0.0) for t in range(4)], axis=0)

    def k_main(p):
        below, above = beside(km[p])
        kbm[p], kam[p], pkm[p] = below, above, below + above

    def k_pair(i):
        tm[32 * i : 32 * i + 32, :] = km[2 * i] + km[2 * i + 1]

    rm01, rs01 = ring_map(inner_z, 96), ring_map(outer_z, 96)
    r12, r23 = ring_map(cut(96), 64), ring_map(cut(64), 64)

    for ref, held, off in ((km, ks, 8), (fm, fs, 6), (lm, ls, 6)):
        for x in range(8):
            held[x + off] = own_strip(ref[x + off])
    for p in range(8, 16):
        k_main(p)
    for i in range(4, 8):
        k_pair(i)
    for i in range(2, 6):
        tlm[32 * i : 32 * i + 32, :] = lm[2 * i + 2] + lm[2 * i + 3]
    loop(7, 13, first_main)
    for i in range(8, 12):
        sweep(i, 0)
    early = {i: resid(field_b[0], on_main, i) for i in (9, 10)}

    for c in e0k + e0s:
        c.arrived()
    merged = merge(rs0, 0)
    for p in range(1, 23):
        own = ks[p] if 8 <= p < 16 else own_strip(km[p])
        ks[p] = whole_strip(own, merged, p - 8)

    for p in range(1, 23):
        below, above = beside(ks[p])
        kbs[p], kas[p], pks[p] = below, above, below + above
    for p in (*range(1, 8), *range(16, 23)):
        k_main(p)
    for i in (1, 2, 3, 8, 9, 10):
        k_pair(i)
    for i in range(1, 11):
        ts[32 * i : 32 * i + 32, :] = spread(ks[2 * i] + ks[2 * i + 1])

    coarse = dot(halve_rows(tm.at[32:352, :], 160), rm01) + dot(halve_rows(ts.at[32:352, :], 160), rs01)
    k1l[...] = (0.125 * coarse).reshape(10, 16, 128)

    kk = k1l[1:9]
    for i in range(4):
        t1[16 * i : 16 * i + 16, :] = kk[2 * i] + kk[2 * i + 1]
    k2l = (0.125 * dot(halve_rows(t1, 32), r12)).reshape(4, 8, 128)
    for c in e0f + e0l:
        c.arrived()
    for n, (ref, strip) in ((1, (fm, fs)), (2, (lm, ls))):
        merged = merge(rs0, n)
        for p in range(20):
            own = strip[p] if 6 <= p < 14 else own_strip(ref[p])
            strip[p] = whole_strip(own, merged, p - 6)

    for i in (0, 1, 6, 7):
        tlm[32 * i : 32 * i + 32, :] = lm[2 * i + 2] + lm[2 * i + 3]
    for i in range(8):
        tls[32 * i : 32 * i + 32, :] = spread(ls[2 * i + 2] + ls[2 * i + 3])
    l1 = dot(halve_rows(tlm, 128), rm01) + dot(halve_rows(tls, 128), rs01)
    l1 = (0.125 * l1).reshape(8, 16, 128)
    half1 = 0.5 * 0.25
    dg1[...] = l1 + half1 * (CALL * k1l[1:9] + ring_sum(k1l[...]))
    for i in range(2):
        t1[16 * i : 16 * i + 16, :] = l1[2 * i + 2] + l1[2 * i + 3]
    l2own = (0.125 * dot(halve_rows(t1, 16), r12)).reshape(2, 8, 128)
    half2 = 0.5 * 0.0625
    diag2 = l2own + half2 * (CALL * k2l[1:3] + ring_sum(k2l))
    both = (k2l[1], k2l[2], diag2[0], diag2[1])
    low = jnp.where(lane < 32, both[0], rot(both[1], 32, 1))
    high = jnp.where(lane < 96, rot(both[2], 64, 1), rot(both[3], 96, 1))
    kd2[...] = jnp.where(lane < 64, low, high)
    l2sum = rot(l2own[0] + l2own[1], 64, 1)
    for i in (*range(0, 7), *range(13, 20)):
        first_main(i)
    loop(0, 20, first_strip)
    ekd2 = send_far(kd2, kd2x)
    for i in (*range(1, 8), *range(12, 19)):
        sweep(i, 0)
    for i in range(1, 19):
        sweep(i, 1)
    for i in range(8):
        pair = [early[n] if n in early else resid(field_b[0], on_main, n) for n in (2 * i + 2, 2 * i + 3)]
        tm[32 * i : 32 * i + 32, :] = pair[0] + pair[1]
        pair = [resid(field_b[1], on_strip, n) for n in (2 * i + 2, 2 * i + 3)]
        pair = pair[0] + pair[1]
        ts[32 * i : 32 * i + 32, :] = jnp.concatenate([pair] * 4, axis=0)
    cell = jnp.where(lane < 96, 2 * lane, 2 * lane - 256)
    pairs = halve_rows(tm, 128)
    inner = from_lanes(pairs, cell & 127) + from_lanes(pairs, (cell + 1) & 127)
    at = jnp.where(cell >= 64, cell - 120, cell + 24) & 31
    tile = 32 * (row >> 2)
    even_at, odd_at = (tile + at, tile + 64 + at), (tile + at + 1, tile + 65 + at)
    pairs = halve_rows(ts, 128)
    outer = from_lanes(pairs, even_at) + from_lanes(pairs, odd_at)
    lane_all = iota((128, 128), 1)
    use_inner = jnp.logical_and(lane_all >= 2, lane_all < 62)
    use_outer = jnp.logical_or(lane_all < 68, lane_all >= 124)
    rhs1 = jnp.where(use_inner, inner, jnp.where(use_outer, outer, 0.0))
    f1[...] = (0.125 * rhs1).reshape(8, 16, 128)

    def pack_sides1(arr):
        left, right = jnp.zeros((8, 128), F32), jnp.zeros((8, 128), F32)
        for x in range(4):
            for t in range(2):
                slot = 2 * x + t
                r = rot(arr[x, 8 * t : 8 * t + 8, :], 4 * slot, 1)
                left = jnp.where((lane >> 2) == slot, r, left)
                right = jnp.where((lane >> 2) == slot + 15, r, right)
        return left, right

    def fill1(ref, own, x_ref, rs):
        merged = [jnp.where(group == 0, rs[step, 0], rs[step, 1]) for step in range(3)]
        for p in range(10):
            x = p - 3
            for t in range(2):
                side = rot(merged[(x + 4) // 4], 64 - 4 * (2 * (x % 4) + t), 1)
                side = jnp.where(jnp.logical_or(lane < 68, lane >= 124), side, 0.0)
                rows = slice(8 * t, 8 * t + 8)
                center = x_ref[0, x + 3, rows, :] if x < 0 else x_ref[1, x - 4, rows, :] if x > 3 else own[x, rows, :]
                ref[p, 8 * t : 8 * t + 8, :] = jnp.where(lane < 64, center, side)

    k1_all = k1l[...]
    k1_all = (k1_all,) + beside(k1_all, 2)
    lane1 = iota((2, 16, 128), 2)

    def inverse1(lo, hi, step):
        there = inside(step)
        keep = jnp.logical_or(lane1 < (64 + 4 * has_right) * there, lane1 >= 128 - 4 * has_left * there)
        return jnp.where(keep, OMEGA / dg1[lo:hi], 0.0)

    def sweep1(v, depth, inv):
        kk = cut_planes(k1_all, 3 - depth, 7 + depth)
        lo, hi = 3 - depth, 5 + depth
        rest = f1[lo:hi] - ring_apply(v, kk, dg1[lo:hi], half1)
        return v[1:-1] + inv[lo:hi] * rest

    inv1 = jnp.concatenate([inverse1(0, 2, -1), inverse1(2, 4, 0), inverse1(4, 6, 0), inverse1(6, 8, 1)], axis=0)
    v = sweep1(inv1 * f1[...], 2, inv1)
    r = f1[2:6] - ring_apply(v, cut_planes(k1_all, 2, 8), dg1[2:6], half1)
    for i in range(2):
        t1[16 * i : 16 * i + 16, :] = r[2 * i] + r[2 * i + 1]
    pairs = halve_rows(t1, 16)
    rhs2 = from_lanes(pairs, (2 * lane) & 127) + from_lanes(pairs, (2 * lane + 1) & 127)
    rhs2 = (0.125 * rhs2).reshape(2, 8, 128)

    gl2[...] = jnp.where(lane < 32, rhs2[0], jnp.where(lane < 64, rot(rhs2[1], 32, 1), l2sum))
    e2 = send_far(gl2, gl2x)
    vv1[...] = v[1:5]
    pv1[0], pv1[1] = pack_sides1(v[1:5])
    ev1x = send_planes(vv1.at[0:3], vv1x.at[1], vv1.at[1:4], vv1x.at[0])
    ev1s = send_sides(pv1, rsv1)

    later = e2 + ev1x + ev1s
    for c in started:
        if not any(c is other for other in later):
            c.left()
    def around2(mine, ref, step):
        mid = mine if step == 4 else ref[step, 1]
        return mid, rot(ref[step, 2], 32, 1), rot(ref[step, 0], -32, 1)

    def near2(parts, n):
        mid, right, left = parts
        at = (lane - 32 * n) & 127
        side = jnp.where(at < 40, right, jnp.where(at >= 120, left, 0.0))
        return rot(jnp.where(at < 32, mid, side), -32 * n, 1)

    for c in ekd2:
        c.arrived()
    mine = kd2[...]
    for step in range(9):
        there = inside(step - 4)
        keep = jnp.logical_or(lane < (32 + 8 * has_right) * there, lane >= 128 - 8 * has_left * there)
        parts = around2(mine, kd2x, step)
        for x in range(2):
            k2[2 * step + x] = near2(parts, x)
            diag = near2(parts, 2 + x)
            dg2[2 * step + x] = diag
            t2[2 * step + x] = jnp.where(keep, OMEGA / diag, 0.0)

    def to_level3(pairs):
        n = len(pairs)
        for i, pair in enumerate(pairs):
            t1[8 * i : 8 * i + 8, :] = pair
        y = 0.125 * dot(halve_rows(t1, 4 * n), r23)
        for i in range(n):
            t3[i, 0:4, :] = y[4 * i : 4 * i + 4, :]
        return t3[0:n]

    k2_all = k2[...]
    k2_all = (k2_all,) + beside(k2_all, 2)
    t3[...] = jnp.zeros_like(t3)
    half3 = 0.5 * 0.015625
    k3 = to_level3([k2[2 * i] + k2[2 * i + 1] for i in range(9)])
    most3 = half3 * (CALL * k3[1:-1] + ring_sum(k3))

    for c in e2:
        c.arrived()
    mine = gl2[...]
    for step in range(9):
        parts = around2(mine, gl2x, step)
        for x in range(2):
            f2[2 * step + x] = near2(parts, x)
        l2[step] = near2(parts, 2)

    def sweep2(v, depth):
        lo, hi = 9 - depth, 9 + depth
        rest = f2[lo:hi] - ring_apply(v, cut_planes(k2_all, lo - 1, hi + 1), dg2[lo:hi], half2)
        return v[1:-1] + t2[lo:hi] * rest

    vb = sweep2(t2[...] * f2[...], 8)
    r = f2[2:16] - ring_apply(vb, cut_planes(k2_all, 1, 17), dg2[2:16], half2)
    l3 = to_level3([l2[i + 1] for i in range(7)])
    f3 = []
    for i in range(7):
        pair = r[2 * i] + r[2 * i + 1]
        f3.append(from_lanes(pair, (2 * lane) & 127) + from_lanes(pair, (2 * lane + 1) & 127))
    t1[0:56, :] = jnp.concatenate(f3, axis=0)
    f3 = 0.125 * halve_rows(t1, 28)
    for i in range(7):
        t3[i, 0:4, :] = f3[4 * i : 4 * i + 4, :]
    f3 = t3[0:7]
    diag3 = l3 + most3
    inv3 = []
    for i in range(7):
        there = inside(i - 3)
        keep = jnp.logical_or(lane < (16 + 4 * has_right) * there, lane >= 128 - 4 * has_left * there)
        inv3.append(jnp.where(jnp.logical_and(keep, row < 4), OMEGA / diag3[i], 0.0)[None])
    inv3 = jnp.concatenate(inv3, axis=0)
    v3 = inv3 * f3
    rest = f3[1:-1] - ring_apply(v3, cut_planes((k3,) + beside(k3, 2), 1, 8), diag3[1:-1], half3)
    v3 = v3[1:-1] + inv3[1:-1] * rest

    wide3 = from_lanes(v3.reshape(40, 128), jnp.where(lane < 64, lane >> 1, ((lane - 128) >> 1) + 128))
    for i in range(5):
        double_rows(t1.at[8 * i : 8 * i + 8, :], wide3[8 * i : 8 * i + 4, :])
    e3 = t1[0:40, :].reshape(5, 8, 128)
    e3 = jnp.concatenate([e3[i // 2][None] for i in range(10)], axis=0)
    vb = vb[3:13] + e3
    vb = sweep2(vb, 4)
    vb = sweep2(vb, 3)

    for c in ev1x + ev1s:
        c.arrived()
    fill1(va1, vv1, vv1x, rsv1)
    wide2 = from_lanes(vb.reshape(48, 128), jnp.where(lane < 96, lane >> 1, ((lane - 128) >> 1) + 128))
    double_rows(tm.at[0:96, :], wide2)
    e2v = tm[0:96, :].reshape(6, 16, 128)
    inner = jnp.logical_or(lane < 68, lane >= 124)
    inner = jnp.concatenate([inner, inner], axis=0)
    v = [jnp.where(inner, va1[p] + e2v[(p - 3) // 2 + 2], 0.0)[None] for p in range(10)]
    v = sweep1(jnp.concatenate(v, axis=0), 3, inv1)
    v = sweep1(v, 2, inv1)

    e1 = v.reshape(96, 128)
    double_rows(tm.at[0:192, :], from_lanes(e1, lane >> 1))
    double_rows(ts.at[0:192, :], from_lanes(e1, (strip_z(lane) >> 1) & 127))
    def correct(i):
        at = 32 * ((i - 4) // 2)
        m = bvm[i] + tm[at : at + 32, :]
        s = ts[at : at + 8, :]
        for t in range(1, 4):
            s = jnp.where(group == t, ts[at + 8 * t : at + 8 * t + 8, :], s)
        ready(field_a[0], on_main, i, m)
        ready(field_a[1], on_strip, i, bvs[i] + s)

    loop(4, 16, correct)
    for i in range(5, 15):
        sweep(i, 0)
        sweep(i, 1)

    def last(i):
        m = bvm[i] + dm[i] * resid(field_b[0], on_main, i)
        s = bvs[i] + ds_[i] * resid(field_b[1], on_strip, i)
        s = jnp.where(place < 8, s, rot(s, -16, 1))
        ends = jnp.concatenate([rot(s, 120 - 32 * t, 1) for t in range(4)], axis=0)
        out_ref[i - 6] = jnp.where(jnp.logical_or(lane32 < 4, lane32 >= 124), ends, m)

    loop(6, 14, last)
    for c in later:
        c.left()


def solution(mesh):
    nw, nz = mesh.shape["wide"], mesh.shape["narrow"]

    def on_device(source, permeability, leakage):
        def vm(*shape):
            return pltpu.VMEM(shape, F32)

        def pair(n):
            return [vm(n, 32, 128), vm(n, 8, 128)]

        scratch = pair(24) * 4 + pair(20) * 12 + [vm(384, 128), vm(384, 128), vm(256, 128), vm(256, 128)]
        scratch += [vm(2, 2, 3, 8, 128), vm(3, 2, 2, 3, 8, 128)]
        scratch += [vm(2, 8, 128), vm(3, 2, 8, 128)]
        scratch += [vm(4, 16, 128), vm(2, 3, 16, 128)]
        scratch += [vm(10, 16, 128), vm(8, 16, 128), vm(8, 16, 128), vm(10, 16, 128), vm(128, 128)]
        scratch += [vm(8, 128), vm(9, 3, 8, 128), vm(8, 128), vm(9, 3, 8, 128)]
        scratch += [vm(18, 8, 128), vm(18, 8, 128), vm(18, 8, 128), vm(9, 8, 128), vm(18, 8, 128), vm(9, 8, 128)]
        n = 12 + 26 + 26 + 8
        scratch += [pltpu.SemaphoreType.REGULAR, pltpu.SemaphoreType.DMA((3,)), pltpu.SemaphoreType.DMA((n,)), pltpu.SemaphoreType.DMA((n,))]

        def body(*refs):
            kernel(nw, nz, *refs)

        return pl.pallas_call(
            body,
            out_shape=pltpu.VMEM(source.shape, F32),
            in_specs=[pl.BlockSpec(memory_space=pltpu.HBM)] * 3,
            out_specs=pl.BlockSpec(memory_space=pltpu.VMEM),
            scratch_shapes=scratch,
            compiler_params=pltpu.CompilerParams(
                collective_id=0, has_side_effects=True, vmem_limit_bytes=60 * 2**20
            ),
            name="vcycle",
        )(source, permeability, leakage)

    spec = P("wide", None, "narrow")
    return jax.shard_map(on_device, mesh=mesh, in_specs=(spec, spec, spec), out_specs=spec, check_vma=False)
```
